128 devices in a mesh: row: 8 (over z, core), col: 16 (over y, x).
Axes of the slice: x: 4, y: 4, z: 4, core: 2. Of those that a mesh axis runs over, the one named last changes fastest.
Arguments:
- block_cells: float32 [1408, 5, 16, 256], P(('row', 'col')), may hold values from -0.6 to 1.4, as said below
- slot_blocks: int32 [128, 11], replicated, may hold values from -1 to 767, as said below
Outputs:
- new_cells: float32 [896, 5, 16, 256], P(('row', 'col'))
The draws below stay inside these ranges and needn't reach their ends.
Inputs may be any that keep to these rules, and one draw needn't show every extreme that they name: `slot_blocks`: row r * 16 + c lists the blocks held by device (r, c): block ids first, in slot order, then -1. Block b belongs to column group b // 48, and every block of column group c is held by exactly one device of that column group. Each device holds 1 to 11 blocks, the devices of a column group hold 48 blocks together, and in every column group one device holds 11 blocks and one holds 1. `block_cells`: fields 0 and 4 (density, pressure) lie in 0.7 to 1.4 and fields 1 to 3 (velocity) in -0.6 to 0.6. Slots marked -1 in slot_blocks hold values that no output depends on.
All inputs are finite; a program needn't handle non-finite values.
Results may differ from the reference program's by a relative error of at most 0.0001.
Values sent between devices are 32-bit elements; how exact they have to be, the bound alone decides.
No kernel may reach another device: no remote copies, remote signals or barrier semaphores. Data moves between devices by JAX's collectives and lax.ppermute only.
A program may use at most 64 MiB of HBM per device.

```python
import jax
import jax.numpy as jnp
from jax import lax

B = 16
BLK_MEAN = 6
CAP = 11
OUT = 7
NBY = 48
NBLK = 768
N_ROW = 8
N_COL = 16


def draw_slot_blocks(key, part):
    row_count = N_ROW
    columns = N_COL
    per_group = BLK_MEAN * row_count
    slot_width = 2 * BLK_MEAN - 1

    def one_group(column):
        group_key = jax.random.fold_in(jax.random.fold_in(key, 17), column)
        order_key, delta_key, block_key = jax.random.split(group_key, 3)
        shuffle = jax.random.permutation(order_key, row_count)
        deltas = jax.random.randint(delta_key, (row_count // 2 - 1,), 0, BLK_MEAN).astype(jnp.int32)
        paired = jnp.stack([BLK_MEAN + deltas, BLK_MEAN - deltas], axis=1).reshape(-1)
        values = jnp.concatenate([jnp.array([slot_width, 1], jnp.int32), paired.astype(jnp.int32)])
        counts = jnp.zeros((row_count,), jnp.int32).at[shuffle].set(values)
        starts = jnp.cumsum(counts) - counts
        blocks = column * per_group + jax.random.permutation(block_key, per_group).astype(jnp.int32)
        slot_ids = jnp.arange(slot_width, dtype=jnp.int32)
        gather_at = jnp.clip(starts[:, None] + slot_ids[None, :], 0, per_group - 1)
        return jnp.where(slot_ids[None, :] < counts[:, None], blocks[gather_at], -1)
    layout = jax.vmap(one_group)(jnp.arange(columns, dtype=jnp.int32))
    return layout.transpose(1, 0, 2).reshape(row_count * columns, slot_width).astype(jnp.int32)


def draw_block_cells(key, part):
    total_slots = N_ROW * N_COL * CAP
    shape_one = (total_slots, 1, B, B * B)
    density_key, motion_key, pressure_key = jax.random.split(jax.random.fold_in(key, 29), 3)
    matter_per_volume = jax.random.uniform(density_key, shape_one, jnp.float32, 0.7, 1.4)
    velocity = jnp.clip(0.2 * jax.random.normal(motion_key, (total_slots, 3, B, B * B), jnp.float32), -0.6, 0.6)
    fluid_static_stress = jax.random.uniform(pressure_key, shape_one, jnp.float32, 0.7, 1.4)
    return jnp.concatenate([matter_per_volume, velocity, fluid_static_stress], axis=1).astype(jnp.float32)


def setup_inputs(seed: int = 0) -> dict:
    key_list = jax.random.split(jax.random.key(seed), 3)
    block_cells = draw_block_cells(jax.random.fold_in(key_list[2], 71), 0)
    slot_blocks = draw_slot_blocks(jax.random.fold_in(key_list[2], 71), 0)
    return {"block_cells": block_cells, "slot_blocks": slot_blocks}


heat_ratio = 1.4
time_step = 0.12
thermal_leading_multiplier = 0.2
thermal_power_law_index = 0.7

def rebalance_table(anchors, counts):
    row_count, columns, slot_width = anchors.shape
    slot_ids = jnp.arange(slot_width, dtype=jnp.int32)
    row_ids = jnp.arange(row_count, dtype=jnp.int32)
    for section_bit in range(row_count.bit_length() - 1):
        partner = row_ids ^ 1 << section_bit
        other_anchors = anchors[partner]
        other_counts = counts[partner]
        sending = jnp.maximum(counts - other_counts, 0) // 2
        taking = jnp.maximum(other_counts - counts, 0) // 2
        keeping = (counts - sending)[:, :, None]
        anchor_slot = other_counts[:, :, None] - taking[:, :, None] + slot_ids - keeping
        pulled = jnp.take_along_axis(other_anchors, jnp.clip(anchor_slot, 0, slot_width - 1), axis=2)
        anchors = jnp.where(slot_ids < keeping, anchors, jnp.where(slot_ids < keeping + taking[:, :, None], pulled, -1))
        counts = counts - sending + taking
    return (anchors, counts)

def to_conserved(primitive):
    matter_per_volume = primitive[0]
    velocity = primitive[1:4]
    fluid_static_stress = primitive[4]
    energy = fluid_static_stress / (heat_ratio - 1.0) + 0.5 * matter_per_volume * lax.optimization_barrier(jnp.sum(velocity * velocity, axis=0))
    return jnp.concatenate([matter_per_volume[None], matter_per_volume[None] * velocity, energy[None]], axis=0)

def to_primitive(conserved):
    matter_per_volume = conserved[0]
    velocity = conserved[1:4] / matter_per_volume
    fluid_static_stress = (heat_ratio - 1.0) * (conserved[4] - 0.5 * matter_per_volume * lax.optimization_barrier(jnp.sum(velocity * velocity, axis=0)))
    return jnp.concatenate([matter_per_volume[None], velocity, fluid_static_stress[None]], axis=0)

def cell_terms(conserved, normal):
    matter_per_volume = conserved[0]
    momentum = conserved[1:4]
    velocity = momentum / matter_per_volume
    fluid_static_stress = (heat_ratio - 1.0) * (conserved[4] - 0.5 * matter_per_volume * lax.optimization_barrier(jnp.sum(velocity * velocity, axis=0)))
    perpendicular_flow_rate = velocity[normal]
    moment_flux = momentum * perpendicular_flow_rate
    moment_flux = moment_flux.at[normal].add(fluid_static_stress)
    face_transport_amounts = jnp.concatenate([momentum[normal][None], moment_flux, ((conserved[4] + fluid_static_stress) * perpendicular_flow_rate)[None]], axis=0)
    sound_signal_rate = jnp.sqrt(heat_ratio * fluid_static_stress / matter_per_volume)
    fluid_thermal_state = fluid_static_stress / matter_per_volume
    thermal_diffusivity_factor = thermal_leading_multiplier * jnp.power(fluid_thermal_state, thermal_power_law_index)
    return (face_transport_amounts, jnp.abs(perpendicular_flow_rate) + sound_signal_rate, fluid_thermal_state, thermal_diffusivity_factor, fluid_static_stress)

def face_flux(lower_cons, lower_data, upper_cons, upper_data):
    wave_speed = jnp.maximum(lower_data[1], upper_data[1])
    face_transport_amounts = 0.5 * (lower_data[0] + upper_data[0]) - 0.5 * wave_speed[None] * (upper_cons - lower_cons)
    heat_flow = 0.5 * (lower_data[3] + upper_data[3]) * (upper_data[2] - lower_data[2])
    return face_transport_amounts.at[4].add(-heat_flow)

def wall_flux(fluid_static_stress, normal):
    nothing = jnp.zeros_like(fluid_static_stress)
    members = [nothing, nothing, nothing, nothing, nothing]
    members[normal + 1] = fluid_static_stress
    return jnp.stack(members, axis=0)

def tendency(conserved):
    changes = []
    for normal in range(2):
        axis_at = normal - 3
        cell_data = cell_terms(conserved, normal)
        ahead_data = jax.tree.map(lambda member: jnp.roll(member, -1, axis=axis_at), cell_data)
        face_transport_amounts = face_flux(conserved, cell_data, jnp.roll(conserved, -1, axis=axis_at), ahead_data)
        changes.append(face_transport_amounts - jnp.roll(face_transport_amounts, 1, axis=axis_at))
    cell_data = cell_terms(conserved, 2)
    lower_data = jax.tree.map(lambda member: member[..., :-1], cell_data)
    upper_data = jax.tree.map(lambda member: member[..., 1:], cell_data)
    interior = face_flux(conserved[..., :-1], lower_data, conserved[..., 1:], upper_data)
    fluid_static_stress = cell_data[4]
    faces = jnp.concatenate([wall_flux(fluid_static_stress[..., :1], 2), interior, wall_flux(fluid_static_stress[..., -1:], 2)], axis=-1)
    changes.append(faces[..., 1:] - faces[..., :-1])
    return -(changes[0] + changes[1] + changes[2])

def reference(block_cells, slot_blocks):
    row_count = N_ROW
    columns = N_COL
    slot_width = slot_blocks.shape[1]
    occupied = slot_blocks >= 0
    counts = lax.optimization_barrier(jnp.sum(occupied.astype(jnp.int32), axis=1)).reshape(row_count, columns)
    device_ids = jnp.arange(row_count * columns, dtype=jnp.int32)[:, None]
    anchors = jnp.where(occupied, device_ids * slot_width + jnp.arange(slot_width, dtype=jnp.int32)[None, :], -1)
    anchors = anchors.reshape(row_count, columns, slot_width)
    final_anchors, final_counts = rebalance_table(anchors, counts)
    final_anchors = final_anchors[:, :, :OUT].reshape(-1)
    every_slot = slot_blocks.reshape(-1)
    target = jnp.where(every_slot >= 0, every_slot, NBLK)
    every_block = jnp.zeros((NBLK + 1, 5, B, B * B), jnp.float32).at[target].set(block_cells)[:NBLK]
    grid_x = jnp.arange(columns, dtype=jnp.int32)[:, None]
    grid_y = jnp.arange(NBY, dtype=jnp.int32)[None, :]
    placed = (grid_x + grid_y) % columns * NBY + grid_y
    cell_grid = every_block[placed.reshape(-1)].reshape(columns, NBY, 5, B, B, B)
    cell_grid = cell_grid.transpose(2, 0, 3, 1, 4, 5).reshape(5, columns * B, NBY * B, B)
    initial = to_conserved(cell_grid)
    first_section = initial + time_step * tendency(initial)
    second_section = 0.75 * initial + 0.25 * (first_section + time_step * tendency(first_section))
    third_section = 1.0 / 3.0 * initial + 2.0 / 3.0 * (second_section + time_step * tendency(second_section))
    finished = to_primitive(third_section).reshape(5, columns, B, NBY, B, B)
    by_position = finished.transpose(1, 3, 0, 2, 4, 5).reshape(columns * NBY, 5, B, B * B)
    final_ids = jnp.where(final_anchors >= 0, every_slot[jnp.maximum(final_anchors, 0)], 0)
    column_of = final_ids // NBY
    along_y = final_ids % NBY
    position = (column_of - along_y) % columns * NBY + along_y
    result = by_position[position]
    return jnp.where((final_anchors >= 0)[:, None, None, None], result, jnp.zeros_like(result))
```

```python
import jax
import jax.numpy as jnp
from jax import lax
from jax.experimental import pallas as pl
from jax.experimental.pallas import tpu as pltpu
from jax.sharding import PartitionSpec as P

CAP = 11
OUT = 7
NBY = 48
N_ROW = 8
N_COL = 16
HALF = NBY // 2
F = 5
X = 8
L = 128
PAD = 32

GAMMA = 1.4
STEP = 0.12

VMEM = pl.BlockSpec(memory_space=pltpu.VMEM)
SMEM = pl.BlockSpec(memory_space=pltpu.SMEM)
ANY = pl.BlockSpec(memory_space=pl.ANY)
PARAMS = pltpu.CompilerParams(vmem_limit_bytes=48 * 1024 * 1024)


def shape(*dims):
    return jax.ShapeDtypeStruct(dims, jnp.float32)


def tile_x(z):
    return ((z + 1) // 2) % 2


def tile_y(z):
    return z // 2


def pack_in(pos, cells, *rest):
    outs, sems = rest[:4], rest[4]
    z = pos[0]
    copies = []
    for k in (2, 1, 3, 0):
        zk = z ^ k
        copies.append(
            pltpu.make_async_copy(
                cells.at[
                    :, :, pl.ds(pl.multiple_of(tile_x(zk) * X, X), X), pl.ds(pl.multiple_of(tile_y(zk) * L, L), L)
                ],
                outs[k],
                sems.at[k],
            )
        )
    for c in copies:
        c.start()
    for c in copies:
        c.wait()


def unpack_out(pos, *refs):
    parts, out, sems = refs[:4], refs[4], refs[5]
    z = pos[0]
    copies = []
    for k in range(4):
        zk = z ^ k
        copies.append(
            pltpu.make_async_copy(
                parts[k],
                out.at[
                    :, :, pl.ds(pl.multiple_of(tile_x(zk) * X, X), X), pl.ds(pl.multiple_of(tile_y(zk) * L, L), L)
                ],
                sems.at[k],
            )
        )
    for c in copies:
        c.start()
    for c in copies:
        c.wait()


def table(pos, slots, final, held, count):
    g = pos[2]
    for d in range(N_ROW):
        n = jnp.int32(0)
        for s in range(CAP):
            b = slots[d * N_COL + g, s]
            held[d * 16 + s] = b - g * NBY
            n = n + jnp.where(b >= 0, 1, 0)
        count[d] = n
    for bit in range(3):
        for low in range(N_ROW):
            if low >> bit & 1:
                continue
            high = low | 1 << bit
            a, b = count[low], count[high]
            up = a > b
            src = jnp.where(up, low, high)
            dst = jnp.where(up, high, low)
            n_src = jnp.maximum(a, b)
            n_dst = jnp.minimum(a, b)
            moved = (n_src - n_dst) // 2

            def move(i, _, src=src, dst=dst, n_src=n_src, n_dst=n_dst, moved=moved):
                held[dst * 16 + n_dst + i] = held[src * 16 + n_src - moved + i]
                return 0

            lax.fori_loop(0, moved, move, 0)
            count[src] = n_src - moved
            count[dst] = n_dst + moved
    for d in range(N_ROW):
        n = count[d]
        for s in range(8):
            final[d * 8 + s] = jnp.where(s < n, held[d * 16 + s], -1)


def rolled(v, shift):
    shift %= L
    return v if shift == 0 else pltpu.roll(v, shift, 1)


def terms(cons):
    rho, mx, my, mz, energy = cons
    inv = 1.0 / rho
    u, v, w = mx * inv, my * inv, mz * inv
    p = (GAMMA - 1.0) * (energy - 0.5 * rho * (u * u + v * v + w * w))
    theta = p * inv
    sound = jnp.sqrt(GAMMA * theta)
    kappa = 0.2 * jnp.exp(0.7 * jnp.log(theta))
    return (u, v, w), p, theta, sound, kappa


def side(cons, t, n):
    vel, p, theta, sound, kappa = t
    return (*cons, p, theta, kappa, vel[n], jnp.abs(vel[n]) + sound)


def double_flux(low, high, n):
    speed = jnp.maximum(low[9], high[9])
    out = []
    for f in range(F):
        if f == 0:
            total = low[n + 1] + high[n + 1]
        elif f == 4:
            total = (low[4] + low[5]) * low[8] + (high[4] + high[5]) * high[8]
        else:
            total = low[f] * low[8] + high[f] * high[8]
            if f == n + 1:
                total = total + (low[5] + high[5])
        total = total - speed * (high[f] - low[f])
        if f == 4:
            total = total - (low[7] + high[7]) * (high[6] - low[6])
        out.append(total)
    return out


def primitive(cons):
    rho, mx, my, mz, energy = cons
    inv = 1.0 / rho
    u, v, w = mx * inv, my * inv, mz * inv
    return [rho, u, v, w, (GAMMA - 1.0) * (energy - 0.5 * rho * (u * u + v * v + w * w))]


def conserved(prim):
    rho, u, v, w, p = prim
    return [rho, rho * u, rho * v, rho * w, p * (1.0 / (GAMMA - 1.0)) + 0.5 * rho * (u * u + v * v + w * w)]


def rows_of(jv):
    return pl.ds(pl.multiple_of(jv * 8, 8), 8)


def faces(pos, cur, jv, x_in, x_out, y_low, y_high):
    zx = tile_x(pos[0])
    rows = rows_of(jv)
    lane = lax.broadcasted_iota(jnp.int32, (8, L), 1) // 16
    for f in range(F):
        x_in[f, rows, :] = cur[f, 7 - 7 * zx, rows, :]
        x_out[f, rows, :] = cur[f, 7 * zx, rows, :]
        low = high = None
        for x in range(X):
            v = cur[f, x, rows, :]
            a, b = rolled(v, 16 * x), rolled(v, 16 * x + 16)
            low = a if low is None else jnp.where(lane == x, a, low)
            high = b if high is None else jnp.where(lane == x, b, high)
        y_low[f, rows, :] = low
        y_high[f, rows, :] = high


def y_faces(pos, y_low, y_high, y_in, y_out):
    zy = tile_y(pos[0])
    core = pos[1]
    first = jnp.full((HALF, L), zy, jnp.int32) == 0
    turn = jnp.full((HALF, L), jnp.where(core == zy, 1, 0), jnp.int32) == 1
    for f in range(F):
        low, high = y_low[f], y_high[f]
        y_in[f] = jnp.where(first, high, low)
        back = jnp.concatenate([low[1:], low[:1]], axis=0)
        ahead = jnp.concatenate([high[-1:], high[:-1]], axis=0)
        y_out[f] = jnp.where(first, jnp.where(turn, back, low), jnp.where(turn, ahead, high))


def reorder(pos, slots, *refs):
    parts = refs[:8]
    cur, x_in, x_out, y_low, y_high, y_in, y_out = refs[8:15]
    held = refs[15]
    z, core, g = pos[0], pos[1], pos[2]
    for k in range(4):
        for h in range(2):
            d = (z ^ k) * 2 + (core ^ h)
            for s in range(CAP):
                j = slots[d * N_COL + g, s] - g * NBY
                here = jnp.logical_and(j >= 0, j % 2 == core)
                row = jnp.where(here, j // 2, HALF)
                for f in range(F):
                    held[pl.ds(f * X * PAD + row, X, PAD), :] = parts[k * 2 + h][s, f]

    def convert(jv, _):
        for x in range(X):
            prim = [held[pl.ds(pl.multiple_of((f * X + x) * PAD + jv * 8, 8), 8), :] for f in range(F)]
            for f, v in enumerate(conserved(prim)):
                cur[f, x, rows_of(jv), :] = v
        faces(pos, cur, jv, x_in, x_out, y_low, y_high)
        return 0

    lax.fori_loop(0, HALF // 8, convert, 0)
    y_faces(pos, y_low, y_high, y_in, y_out)


def section(number, pos, *refs):
    if number == 0:
        cur = initial = refs[0]
        refs = refs[1:]
    else:
        initial, cur = refs[:2]
        refs = refs[2:]
    x_in, x_out, y_in, y_out, y_low, y_high = refs[:6]
    new = refs[6]
    zx, zy = tile_x(pos[0]), tile_y(pos[0])
    weight = (0.0, 0.75, 1.0 / 3.0)[number]

    def step(jv, _):
        rows = rows_of(jv)
        lane = lax.broadcasted_iota(jnp.int32, (8, L), 1)
        height = lane % 16
        low_y, high_y = lane < 16, lane >= L - 16
        floor, roof = height == 0, height == 15
        first_x = jnp.full((8, L), zx, jnp.int32) == 0
        first_y = jnp.full((8, L), zy, jnp.int32) == 0

        def halo(inner, outer, first):
            a = [inner[f, rows, :] for f in range(F)]
            b = [outer[f, rows, :] for f in range(F)]
            low = [jnp.where(first, o, i) for i, o in zip(a, b)]
            high = [jnp.where(first, i, o) for i, o in zip(a, b)]
            return low, high

        y_before, y_after = halo(y_in, y_out, first_y)
        mine_low = [y_low[f, rows, :] for f in range(F)]
        mine_high = [y_high[f, rows, :] for f in range(F)]
        flux_low = double_flux(side(y_before, terms(y_before), 1), side(mine_low, terms(mine_low), 1), 1)
        flux_high = double_flux(side(mine_high, terms(mine_high), 1), side(y_after, terms(y_after), 1), 1)

        x_before, x_after = halo(x_in, x_out, first_x)
        behind = side(x_before, terms(x_before), 0)
        cons = [cur[f, 0, rows, :] for f in range(F)]
        t = terms(cons)
        here = side(cons, t, 0)
        flux_x = double_flux(behind, here, 0)
        for x in range(X):
            if x < X - 1:
                cons_next = [cur[f, x + 1, rows, :] for f in range(F)]
            else:
                cons_next = x_after
            t_next = terms(cons_next)
            ahead = side(cons_next, t_next, 0)
            flux_next = double_flux(here, ahead, 0)
            change = [b - a for a, b in zip(flux_x, flux_next)]

            low = side(cons, t, 1)
            flux = double_flux(low, [rolled(q, -16) for q in low], 1)
            for f in range(F):
                upper = jnp.where(high_y, rolled(flux_high[f], L - 16 - 16 * x), flux[f])
                lower = jnp.where(low_y, rolled(flux_low[f], -16 * x), rolled(flux[f], 16))
                change[f] = change[f] + (upper - lower)

            low = side(cons, t, 2)
            flux = double_flux(low, [rolled(q, -1) for q in low], 2)
            for f in range(F):
                wall = 2.0 * t[1] if f == 3 else 0.0
                upper = jnp.where(roof, wall, flux[f])
                lower = jnp.where(floor, wall, rolled(flux[f], 1))
                change[f] = change[f] + (upper - lower)

            out = [c - (0.5 * STEP) * d for c, d in zip(cons, change)]
            if number:
                out = [
                    weight * initial[f, x, rows, :] + (1.0 - weight) * o for f, o in enumerate(out)
                ]
            if number == 2:
                out = primitive(out)
            for f in range(F):
                new[f, x, rows, :] = out[f]
            cons, t, here, flux_x = cons_next, t_next, ahead, flux_next
        if number < 2:
            faces(pos, new, jv, *refs[7:11])
        return 0

    lax.fori_loop(0, HALF // 8, step, 0)
    if number < 2:
        y_faces(pos, *refs[9:13])


def pack_out(pos, final, mine, other, *outs):
    z, core = pos[0], pos[1]
    for k in range(4):
        d = (z ^ k) * 2 + core
        for s in range(OUT):
            j = final[d * 8 + s]
            row = jnp.maximum(j, 0) // 2
            kind = jnp.full((X, L), jnp.where(j < 0, 2, j % 2 ^ core), jnp.int32)
            for f in range(F):
                at = pl.ds(f * X * HALF + row, X, HALF)
                a, b = mine[at, :], other[at, :]
                outs[k][s, f] = jnp.where(kind == 0, a, jnp.where(kind == 1, b, 0.0))


def body(block_cells, slot_blocks):
    row, col = lax.axis_index("row"), lax.axis_index("col")
    pos = jnp.stack([row // 2, row % 2, col]).astype(jnp.int32)

    def to(array, route):
        pairs = []
        for r in range(N_ROW):
            for c in range(N_COL):
                z, core, c2 = route(r // 2, r % 2, c)
                pairs.append((r * N_COL + c, (z * 2 + core) * N_COL + c2 % N_COL))
        return lax.ppermute(array, ("row", "col"), pairs)

    def over_z(array, k):
        return array if k == 0 else to(array, lambda z, core, c: (z ^ k, core, c))

    def over_core(array):
        return to(array, lambda z, core, c: (z, 1 - core, c))

    tiles = [shape(CAP, F, X, L)] * 4
    parts = pl.pallas_call(
        pack_in,
        out_shape=tiles,
        in_specs=[SMEM, ANY],
        out_specs=[VMEM] * 4,
        scratch_shapes=[pltpu.SemaphoreType.DMA((4,))],
        compiler_params=PARAMS,
        name="pack_in",
    )(pos, block_cells)
    final = pl.pallas_call(
        table,
        out_shape=jax.ShapeDtypeStruct((N_ROW * 8,), jnp.int32),
        in_specs=[SMEM, SMEM],
        out_specs=SMEM,
        scratch_shapes=[pltpu.SMEM((N_ROW * 16,), jnp.int32), pltpu.SMEM((N_ROW,), jnp.int32)],
        compiler_params=PARAMS,
        name="table",
    )(pos, slot_blocks)
    gathered = []
    for k in range(4):
        here = over_z(parts[k], k)
        gathered += [here, over_core(here)]

    whole = shape(F, X, HALF, L)
    layer = shape(F, HALF, L)
    initial, x_in, x_out, y_low, y_high, y_in, y_out = pl.pallas_call(
        reorder,
        out_shape=[whole] + [layer] * 6,
        in_specs=[SMEM, SMEM] + [VMEM] * 8,
        out_specs=[VMEM] * 7,
        scratch_shapes=[pltpu.VMEM((F * X * PAD, L), jnp.float32)],
        compiler_params=PARAMS,
        name="reorder",
    )(pos, slot_blocks, *gathered)

    def x_partner(z):
        return z ^ 1

    def y_partner(z):
        return z ^ 3

    def exchanged(x_in, x_out, y_in, y_out):
        return (
            to(x_in, lambda z, core, c: (x_partner(z), core, c)),
            to(x_out, lambda z, core, c: (x_partner(z), core, c + 2 * tile_x(z) - 1)),
            to(y_in, lambda z, core, c: (y_partner(z), core, c)),
            to(y_out, lambda z, core, c: (y_partner(z), 1 - core, c + 2 * tile_y(z) - 1)),
        )

    current = initial
    for number in range(3):
        halos = exchanged(x_in, x_out, y_in, y_out)
        states = (current,) if number == 0 else (initial, current)
        outs = [whole] + ([layer] * 6 if number < 2 else [])
        made = pl.pallas_call(
            lambda *refs, number=number: section(number, *refs),
            out_shape=outs,
            in_specs=[SMEM] + [VMEM] * (len(states) + 6),
            out_specs=[VMEM] * len(outs),
            compiler_params=PARAMS,
            name="section" + str(number),
        )(pos, *states, *halos, y_low, y_high)
        current = made[0]
        if number < 2:
            x_in, x_out, y_low, y_high, y_in, y_out = made[1:]

    flat = current.reshape(F * X * HALF, L)
    leaving = pl.pallas_call(
        pack_out,
        out_shape=[shape(OUT, F, X, L)] * 4,
        in_specs=[SMEM, SMEM, VMEM, VMEM],
        out_specs=[VMEM] * 4,
        compiler_params=PARAMS,
        name="pack_out",
    )(pos, final, flat, over_core(flat))
    arrived = [over_z(leaving[k], k) for k in range(4)]
    return pl.pallas_call(
        unpack_out,
        out_shape=shape(OUT, F, 2 * X, 2 * L),
        in_specs=[SMEM] + [ANY] * 4,
        out_specs=ANY,
        scratch_shapes=[pltpu.SemaphoreType.DMA((4,))],
        compiler_params=PARAMS,
        name="unpack_out",
    )(pos, *arrived)


def solution(mesh):
    in_specs = (P(("row", "col"), None, None, None), P())
    out_specs = P(("row", "col"), None, None, None)
    return jax.shard_map(body, mesh=mesh, in_specs=in_specs, out_specs=out_specs, check_vma=False)
```

```python
import jax
import jax.numpy as jnp
from jax import lax
from jax.experimental import pallas as pl
from jax.experimental.pallas import tpu as pltpu
from jax.sharding import PartitionSpec as P

CAP = 11
OUT = 7
NBY = 48
N_ROW = 8
N_COL = 16
HALF = NBY // 2
F = 5
X = Y = 8
L = 128

GAMMA = 1.4
STEP = 0.12

VMEM = pl.BlockSpec(memory_space=pltpu.VMEM)
SMEM = pl.BlockSpec(memory_space=pltpu.SMEM)
ANY = pl.BlockSpec(memory_space=pl.ANY)
PARAMS = pltpu.CompilerParams(vmem_limit_bytes=48 * 1024 * 1024)


def shape(*dims):
    return jax.ShapeDtypeStruct(dims, jnp.float32)


def tile_x(z):
    return ((z + 1) // 2) % 2


def tile_y(z):
    return z // 2


def pack_in(pos, cells, *rest):
    outs, sems = rest[:4], rest[4]
    z = pos[0]
    copies = []
    for k in (2, 1, 3, 0):
        zk = z ^ k
        copies.append(
            pltpu.make_async_copy(
                cells.at[
                    :, :, pl.ds(pl.multiple_of(tile_x(zk) * X, X), X), pl.ds(pl.multiple_of(tile_y(zk) * L, L), L)
                ],
                outs[k],
                sems.at[k],
            )
        )
    for c in copies:
        c.start()
    for c in copies:
        c.wait()


def unpack_out(pos, *refs):
    parts, out, sems = refs[:4], refs[4], refs[5]
    z = pos[0]
    copies = []
    for k in range(4):
        zk = z ^ k
        copies.append(
            pltpu.make_async_copy(
                parts[k],
                out.at[
                    :, :, pl.ds(pl.multiple_of(tile_x(zk) * X, X), X), pl.ds(pl.multiple_of(tile_y(zk) * L, L), L)
                ],
                sems.at[k],
            )
        )
    for c in copies:
        c.start()
    for c in copies:
        c.wait()


def table(pos, slots, _tile, final, rows, _same, held, count):
    z, core, g = pos[0], pos[1], pos[2]
    for d in range(N_ROW):
        n = jnp.int32(0)
        place = ((z ^ d // 2) * 2 + (core ^ d % 2)) * CAP
        for s in range(CAP):
            b = slots[d * N_COL + g, s]
            j = b - g * NBY
            held[d * 16 + s] = j
            here = jnp.logical_and(b >= 0, (j & 1) == core)
            rows[place + s] = jnp.where(here, j >> 1, HALF)
            n = n + jnp.where(b >= 0, 1, 0)
        count[d] = n
    for bit in range(3):
        for low in range(N_ROW):
            if low >> bit & 1:
                continue
            high = low | 1 << bit
            a, b = count[low], count[high]
            up = a > b
            src = jnp.where(up, low, high)
            dst = jnp.where(up, high, low)
            n_src = jnp.maximum(a, b)
            n_dst = jnp.minimum(a, b)
            moved = (n_src - n_dst) // 2

            def move(i, _, src=src, dst=dst, n_src=n_src, n_dst=n_dst, moved=moved):
                held[dst * 16 + n_dst + i] = held[src * 16 + n_src - moved + i]
                return 0

            lax.fori_loop(0, moved, move, 0)
            count[src] = n_src - moved
            count[dst] = n_dst + moved
    for d in range(N_ROW):
        n = count[d]
        for s in range(8):
            final[d * 8 + s] = jnp.where(s < n, held[d * 16 + s], -1)


def rolled(v, shift):
    shift %= L
    return v if shift == 0 else pltpu.roll(v, shift, 1)


def terms(cons):
    rho, mx, my, mz, energy = cons
    inv = 1.0 / rho
    u, v, w = mx * inv, my * inv, mz * inv
    p = (GAMMA - 1.0) * (energy - 0.5 * rho * (u * u + v * v + w * w))
    theta = p * inv
    sound = jnp.sqrt(GAMMA * theta)
    kappa = 0.2 * jnp.exp(0.7 * jnp.log(theta))
    return (u, v, w), p, theta, sound, kappa


def side(cons, t, n):
    vel, p, theta, sound, kappa = t
    return (*cons, p, theta, kappa, vel[n], jnp.abs(vel[n]) + sound)


def double_flux(low, high, n):
    speed = jnp.maximum(low[9], high[9])
    out = []
    for f in range(F):
        if f == 0:
            total = low[n + 1] + high[n + 1]
        elif f == 4:
            total = (low[4] + low[5]) * low[8] + (high[4] + high[5]) * high[8]
        else:
            total = low[f] * low[8] + high[f] * high[8]
            if f == n + 1:
                total = total + (low[5] + high[5])
        total = total - speed * (high[f] - low[f])
        if f == 4:
            total = total - (low[7] + high[7]) * (high[6] - low[6])
        out.append(total)
    return out


def primitive(cons):
    rho, mx, my, mz, energy = cons
    inv = 1.0 / rho
    u, v, w = mx * inv, my * inv, mz * inv
    return [rho, u, v, w, (GAMMA - 1.0) * (energy - 0.5 * rho * (u * u + v * v + w * w))]


def conserved(prim):
    rho, u, v, w, p = prim
    return [rho, rho * u, rho * v, rho * w, p * (1.0 / (GAMMA - 1.0)) + 0.5 * rho * (u * u + v * v + w * w)]


def at(f, y, group):
    return pl.ds(pl.multiple_of((f * Y + y) * HALF + group * 8, 8), 8)


def layer_at(f, group):
    return pl.ds(pl.multiple_of(f * HALF + group * 8, 8), 8)


def x_layer_at(f, group, x):
    return pl.ds(f * Y * HALF + group * 8 + x, Y, HALF)


def transposed(vectors):
    place = lax.broadcasted_iota(jnp.int32, (8, L), 1) // 16
    vectors = list(vectors)
    for bit in (1, 2, 4):
        clear = (place & bit) == 0
        for i in range(8):
            if i & bit:
                continue
            a, b = vectors[i], vectors[i | bit]
            vectors[i] = jnp.where(clear, a, rolled(b, 16 * bit))
            vectors[i | bit] = jnp.where(clear, rolled(a, -16 * bit), b)
    return vectors


def faces(pos, cur, x_in, x_out, y_in, y_out):
    zx, zy, core = tile_x(pos[0]), tile_y(pos[0]), pos[1]
    place = lax.broadcasted_iota(jnp.int32, (8, L), 1) // 16
    first = jnp.full((8, L), zy, jnp.int32) == 0
    turn = jnp.full((8, L), jnp.where(core == zy, 1, 0), jnp.int32) == 1
    for f in range(F):
        ahead, back = [], []
        for group in range(3):
            x_in[layer_at(f, group), :] = cur[x_layer_at(f, group, 7 - 7 * zx), :]
            x_out[layer_at(f, group), :] = cur[x_layer_at(f, group, 7 * zx), :]
            y_in[layer_at(f, group), :] = cur[at(f, 7 - 7 * zy, group), :]
            v = cur[at(f, 7 * zy, group), :]
            ahead.append(rolled(v, 16))
            back.append(rolled(v, -16))
        for group in range(3):
            high = jnp.where(place == 0, ahead[group - 1], ahead[group])
            low = jnp.where(place == 7, back[(group + 1) % 3], back[group])
            v = cur[at(f, 7 * zy, group), :]
            y_out[layer_at(f, group), :] = jnp.where(turn, jnp.where(first, low, high), v)


def reorder(pos, rows, *refs):
    parts = refs[:8]
    cur, x_in, x_out, y_in, y_out = refs[8:13]
    held = refs[13]
    for i in range(8):
        for s in range(CAP):
            held[rows[i * CAP + s]] = parts[i][s]

    def convert(group, _):
        for f in range(F):
            vectors = [held[group * 8 + i, f] for i in range(8)]
            for y, v in enumerate(transposed(vectors)):
                cur[at(f, y, group), :] = v
        for y in range(Y):
            prim = [cur[at(f, y, group), :] for f in range(F)]
            for f, v in enumerate(conserved(prim)):
                if f:
                    cur[at(f, y, group), :] = v
        return 0

    lax.fori_loop(0, 3, convert, 0)
    faces(pos, cur, x_in, x_out, y_in, y_out)


def section(number, pos, *refs):
    if number == 0:
        cur = initial = refs[0]
        refs = refs[1:]
    else:
        initial, cur = refs[:2]
        refs = refs[2:]
    x_in, x_out, y_in, y_out = refs[:4]
    new = refs[4]
    edge = refs[-1]
    zx, zy = tile_x(pos[0]), tile_y(pos[0])
    weight = (0.0, 0.75, 1.0 / 3.0)[number]

    def step(group, _):
        height = lax.broadcasted_iota(jnp.int32, (8, L), 1) % 16
        sub = lax.broadcasted_iota(jnp.int32, (8, L), 0)
        floor, roof = height == 0, height == 15
        left, right = sub == 0, sub == 7
        first_x = jnp.full((8, L), zx, jnp.int32) == 0
        first_y = jnp.full((8, L), zy, jnp.int32) == 0

        def halo(inner, outer, first):
            a = [inner[layer_at(f, group), :] for f in range(F)]
            b = [outer[layer_at(f, group), :] for f in range(F)]
            low = [jnp.where(first, o, i) for i, o in zip(a, b)]
            high = [jnp.where(first, i, o) for i, o in zip(a, b)]
            return low, high

        def all_of(cons, n):
            return side(cons, terms(cons), n)

        x_before, x_after = halo(x_in, x_out, first_x)
        mine_low = [cur[x_layer_at(f, group, 0), :] for f in range(F)]
        mine_high = [cur[x_layer_at(f, group, 7), :] for f in range(F)]
        for f, v in enumerate(double_flux(all_of(x_before, 0), all_of(mine_low, 0), 0)):
            edge[f * 8 : f * 8 + 8, :] = v
        for f, v in enumerate(double_flux(all_of(mine_high, 0), all_of(x_after, 0), 0)):
            edge[(F + f) * 8 : (F + f) * 8 + 8, :] = v

        y_before, y_after = halo(y_in, y_out, first_y)
        cons = [cur[at(f, 0, group), :] for f in range(F)]
        t = terms(cons)
        here = side(cons, t, 1)
        flux_y = double_flux(all_of(y_before, 1), here, 1)
        for y in range(Y):
            cons_next = [cur[at(f, y + 1, group), :] for f in range(F)] if y < Y - 1 else y_after
            t_next = terms(cons_next)
            ahead = side(cons_next, t_next, 1)
            flux_next = double_flux(here, ahead, 1)
            change = [b - a for a, b in zip(flux_y, flux_next)]

            low = side(cons, t, 0)
            flux = double_flux(low, [pltpu.roll(q, 7, 0) for q in low], 0)
            for f in range(F):
                lowest = jnp.broadcast_to(edge[f * 8 + y : f * 8 + y + 1, :], (8, L))
                highest = jnp.broadcast_to(edge[(F + f) * 8 + y : (F + f) * 8 + y + 1, :], (8, L))
                upper = jnp.where(right, highest, flux[f])
                lower = jnp.where(left, lowest, pltpu.roll(flux[f], 1, 0))
                change[f] = change[f] + (upper - lower)

            low = side(cons, t, 2)
            flux = double_flux(low, [rolled(q, -1) for q in low], 2)
            for f in range(F):
                wall = 2.0 * t[1] if f == 3 else 0.0
                upper = jnp.where(roof, wall, flux[f])
                lower = jnp.where(floor, wall, rolled(flux[f], 1))
                change[f] = change[f] + (upper - lower)

            out = [c - (0.5 * STEP) * d for c, d in zip(cons, change)]
            if number:
                out = [weight * initial[at(f, y, group), :] + (1.0 - weight) * o for f, o in enumerate(out)]
            if number == 2:
                out = primitive(out)
            into = refs[-2] if number == 2 else new
            for f in range(F):
                into[at(f, y, group), :] = out[f]
            cons, t, here, flux_y = cons_next, t_next, ahead, flux_next
        if number == 2:
            for f in range(F):
                vectors = [refs[-2][at(f, y, group), :] for y in range(Y)]
                for i, v in enumerate(transposed(vectors)):
                    new[group * 8 + i, f] = v
        return 0

    lax.fori_loop(0, 3, step, 0)
    if number < 2:
        faces(pos, new, *refs[5:9])


def pack_out(pos, final, mine, other, *outs):
    z, core = pos[0], pos[1]
    for k in range(4):
        d = (z ^ k) * 2 + core
        for s in range(OUT):
            j = final[d * 8 + s]
            row = jnp.maximum(j, 0) >> 1
            kind = jnp.full((X, L), jnp.where(j < 0, 2, (j & 1) ^ core), jnp.int32)
            for f in range(F):
                outs[k][s, f] = jnp.where(kind == 0, mine[row, f], jnp.where(kind == 1, other[row, f], 0.0))


def body(block_cells, slot_blocks):
    row, col = lax.axis_index("row"), lax.axis_index("col")
    pos = jnp.stack([row // 2, row % 2, col]).astype(jnp.int32)

    def to(array, route):
        pairs = []
        for r in range(N_ROW):
            for c in range(N_COL):
                z, core, c2 = route(r // 2, r % 2, c)
                pairs.append((r * N_COL + c, (z * 2 + core) * N_COL + c2 % N_COL))
        return lax.ppermute(array, ("row", "col"), pairs)

    def over_z(array, k):
        return array if k == 0 else to(array, lambda z, core, c: (z ^ k, core, c))

    def over_core(array):
        return to(array, lambda z, core, c: (z, 1 - core, c))

    tiles = [shape(CAP, F, X, L)] * 4
    parts = pl.pallas_call(
        pack_in,
        out_shape=tiles,
        in_specs=[SMEM, ANY],
        out_specs=[VMEM] * 4,
        scratch_shapes=[pltpu.SemaphoreType.DMA((4,))],
        compiler_params=PARAMS,
        name="pack_in",
    )(pos, block_cells)
    final, rows, own = pl.pallas_call(
        table,
        out_shape=[
            jax.ShapeDtypeStruct((N_ROW * 8,), jnp.int32),
            jax.ShapeDtypeStruct((N_ROW * CAP,), jnp.int32),
            tiles[0],
        ],
        in_specs=[SMEM, SMEM, ANY],
        out_specs=[SMEM, SMEM, ANY],
        input_output_aliases={2: 2},
        scratch_shapes=[pltpu.SMEM((N_ROW * 16,), jnp.int32), pltpu.SMEM((N_ROW,), jnp.int32)],
        compiler_params=PARAMS,
        cost_estimate=pl.CostEstimate(flops=0, bytes_accessed=20_000_000, transcendentals=0),
        name="table",
    )(pos, slot_blocks, parts[0])
    gathered = []
    for k in range(4):
        here = over_z(parts[k], k) if k else own
        gathered += [here, over_core(here)]

    whole = shape(F * Y * HALF, L)
    layer = shape(F * HALF, L)
    initial, x_in, x_out, y_in, y_out = pl.pallas_call(
        reorder,
        out_shape=[whole] + [layer] * 4,
        in_specs=[SMEM, SMEM] + [VMEM] * 8,
        out_specs=[VMEM] * 5,
        scratch_shapes=[pltpu.VMEM((HALF + 1, F, X, L), jnp.float32)],
        compiler_params=PARAMS,
        name="reorder",
    )(pos, rows, *gathered)

    def x_partner(z):
        return z ^ 1

    def y_partner(z):
        return z ^ 3

    def exchanged(x_in, x_out, y_in, y_out):
        return (
            to(x_in, lambda z, core, c: (x_partner(z), core, c)),
            to(x_out, lambda z, core, c: (x_partner(z), core, c + 2 * tile_x(z) - 1)),
            to(y_in, lambda z, core, c: (y_partner(z), core, c)),
            to(y_out, lambda z, core, c: (y_partner(z), 1 - core, c + 2 * tile_y(z) - 1)),
        )

    current = initial
    for number in range(3):
        halos = exchanged(x_in, x_out, y_in, y_out)
        states = (current,) if number == 0 else (initial, current)
        outs = [whole] + [layer] * 4 if number < 2 else [shape(HALF, F, X, L)]
        scratch = [pltpu.VMEM((2 * F * 8, L), jnp.float32)]
        if number == 2:
            scratch = [pltpu.VMEM((F * Y * HALF, L), jnp.float32)] + scratch
        made = pl.pallas_call(
            lambda *refs, number=number: section(number, *refs),
            out_shape=outs,
            in_specs=[SMEM] + [VMEM] * (len(states) + 4),
            out_specs=[VMEM] * len(outs),
            scratch_shapes=scratch,
            compiler_params=PARAMS,
            name="section" + str(number),
        )(pos, *states, *halos)
        current = made[0]
        if number < 2:
            x_in, x_out, y_in, y_out = made[1:]

    leaving = pl.pallas_call(
        pack_out,
        out_shape=[shape(OUT, F, X, L)] * 4,
        in_specs=[SMEM, SMEM, VMEM, VMEM],
        out_specs=[VMEM] * 4,
        compiler_params=PARAMS,
        name="pack_out",
    )(pos, final, current, over_core(current))
    arrived = [over_z(leaving[k], k) for k in range(4)]
    return pl.pallas_call(
        unpack_out,
        out_shape=shape(OUT, F, 2 * X, 2 * L),
        in_specs=[SMEM] + [ANY] * 4,
        out_specs=ANY,
        scratch_shapes=[pltpu.SemaphoreType.DMA((4,))],
        compiler_params=PARAMS,
        name="unpack_out",
    )(pos, *arrived)


def solution(mesh):
    in_specs = (P(("row", "col"), None, None, None), P())
    out_specs = P(("row", "col"), None, None, None)
    return jax.shard_map(body, mesh=mesh, in_specs=in_specs, out_specs=out_specs, check_vma=False)
```

```python
import jax
import jax.numpy as jnp
from jax import lax
from jax.experimental import pallas as pl
from jax.experimental.pallas import tpu as pltpu
from jax.sharding import PartitionSpec as P

CAP = 11
OUT = 7
NBY = 48
N_ROW = 8
N_COL = 16
HALF = NBY // 2
F = 5
X = Y = 8
L = 128
DEEP = 3
WIDE = Y + 2 * DEEP

GAMMA = 1.4
STEP = 0.12

VMEM = pl.BlockSpec(memory_space=pltpu.VMEM)
SMEM = pl.BlockSpec(memory_space=pltpu.SMEM)
ANY = pl.BlockSpec(memory_space=pl.ANY)
PARAMS = pltpu.CompilerParams(vmem_limit_bytes=48 * 1024 * 1024)


def shape(*dims):
    return jax.ShapeDtypeStruct(dims, jnp.float32)


def tile_x(z):
    return ((z + 1) // 2) % 2


def tile_y(z):
    return z // 2


def pack_in(pos, cells, *rest):
    outs, sems = rest[:4], rest[4]
    z = pos[0]
    copies = []
    for k in (2, 1, 3, 0):
        zk = z ^ k
        copies.append(
            pltpu.make_async_copy(
                cells.at[
                    :, :, pl.ds(pl.multiple_of(tile_x(zk) * X, X), X), pl.ds(pl.multiple_of(tile_y(zk) * L, L), L)
                ],
                outs[k],
                sems.at[k],
            )
        )
    for c in copies:
        c.start()
    for c in copies:
        c.wait()


def unpack_out(pos, *refs):
    parts, out, sems = refs[:4], refs[4], refs[5]
    z = pos[0]
    copies = []
    for k in range(4):
        zk = z ^ k
        copies.append(
            pltpu.make_async_copy(
                parts[k],
                out.at[
                    :, :, pl.ds(pl.multiple_of(tile_x(zk) * X, X), X), pl.ds(pl.multiple_of(tile_y(zk) * L, L), L)
                ],
                sems.at[k],
            )
        )
    for c in copies:
        c.start()
    for c in copies:
        c.wait()


def table(pos, slots, _tile, final, rows, _same, held, count):
    z, core, g = pos[0], pos[1], pos[2]
    for d in range(N_ROW):
        n = jnp.int32(0)
        place = ((z ^ d // 2) * 2 + (core ^ d % 2)) * CAP
        for s in range(CAP):
            b = slots[d * N_COL + g, s]
            j = b - g * NBY
            held[d * 16 + s] = j
            here = jnp.logical_and(b >= 0, (j & 1) == core)
            rows[place + s] = jnp.where(here, j >> 1, HALF)
            n = n + jnp.where(b >= 0, 1, 0)
        count[d] = n
    for bit in range(3):
        for low in range(N_ROW):
            if low >> bit & 1:
                continue
            high = low | 1 << bit
            a, b = count[low], count[high]
            up = a > b
            src = jnp.where(up, low, high)
            dst = jnp.where(up, high, low)
            n_src = jnp.maximum(a, b)
            n_dst = jnp.minimum(a, b)
            moved = (n_src - n_dst) // 2

            def move(i, _, src=src, dst=dst, n_src=n_src, n_dst=n_dst, moved=moved):
                held[dst * 16 + n_dst + i] = held[src * 16 + n_src - moved + i]
                return 0

            lax.fori_loop(0, moved, move, 0)
            count[src] = n_src - moved
            count[dst] = n_dst + moved
    for d in range(N_ROW):
        n = count[d]
        for s in range(8):
            final[d * 8 + s] = jnp.where(s < n, held[d * 16 + s], -1)


def rolled(v, shift):
    shift %= L
    return v if shift == 0 else pltpu.roll(v, shift, 1)


def terms(cons):
    rho, mx, my, mz, energy = cons
    inv = 1.0 / rho
    u, v, w = mx * inv, my * inv, mz * inv
    p = (GAMMA - 1.0) * (energy - 0.5 * rho * (u * u + v * v + w * w))
    theta = p * inv
    sound = jnp.sqrt(GAMMA * theta)
    kappa = 0.2 * jnp.exp(0.7 * jnp.log(theta))
    return (u, v, w), p, theta, sound, kappa


def side(cons, t, n):
    vel, p, theta, sound, kappa = t
    return (*cons, p, theta, kappa, vel[n], jnp.abs(vel[n]) + sound)


def double_flux(low, high, n):
    speed = jnp.maximum(low[9], high[9])
    out = []
    for f in range(F):
        if f == 0:
            total = low[n + 1] + high[n + 1]
        elif f == 4:
            total = (low[4] + low[5]) * low[8] + (high[4] + high[5]) * high[8]
        else:
            total = low[f] * low[8] + high[f] * high[8]
            if f == n + 1:
                total = total + (low[5] + high[5])
        total = total - speed * (high[f] - low[f])
        if f == 4:
            total = total - (low[7] + high[7]) * (high[6] - low[6])
        out.append(total)
    return out


def primitive(cons):
    rho, mx, my, mz, energy = cons
    inv = 1.0 / rho
    u, v, w = mx * inv, my * inv, mz * inv
    return [rho, u, v, w, (GAMMA - 1.0) * (energy - 0.5 * rho * (u * u + v * v + w * w))]


def conserved(prim):
    rho, u, v, w, p = prim
    return [rho, rho * u, rho * v, rho * w, p * (1.0 / (GAMMA - 1.0)) + 0.5 * rho * (u * u + v * v + w * w)]


def at(f, y, group):
    return pl.ds(pl.multiple_of((f * Y + y) * HALF + group * 8, 8), 8)


def wide_at(f, y, group):
    return pl.ds(pl.multiple_of((f * WIDE + DEEP + y) * HALF + group * 8, 8), 8)


def strip_at(f, t, group):
    return pl.ds(pl.multiple_of((f * DEEP + t) * HALF + group * 8, 8), 8)


def x_layer_at(f, group, x):
    return pl.ds(f * Y * HALF + group * 8 + x, Y, HALF)


def transposed(vectors):
    place = lax.broadcasted_iota(jnp.int32, (8, L), 1) // 16
    vectors = list(vectors)
    for bit in (1, 2, 4):
        clear = (place & bit) == 0
        for i in range(8):
            if i & bit:
                continue
            a, b = vectors[i], vectors[i | bit]
            vectors[i] = jnp.where(clear, a, rolled(b, 16 * bit))
            vectors[i | bit] = jnp.where(clear, rolled(a, -16 * bit), b)
    return vectors


def faces(pos, cur, x_in, x_out, y_in, y_out):
    zx, zy, core = tile_x(pos[0]), tile_y(pos[0]), pos[1]
    place = lax.broadcasted_iota(jnp.int32, (8, L), 1) // 16
    first = jnp.full((8, L), zy, jnp.int32) == 0
    turn = jnp.full((8, L), jnp.where(core == zy, 1, 0), jnp.int32) == 1
    far = Y - DEEP
    for f in range(F):
        for t in range(DEEP):
            ahead, back = [], []
            for group in range(3):
                to = pl.ds(((f * 3 + group) * DEEP + t) * 8, 8)
                x_in[to, :] = cur[x_layer_at(f, group, far * (1 - zx) + t), :]
                x_out[to, :] = cur[x_layer_at(f, group, far * zx + t), :]
                y_in[strip_at(f, t, group), :] = cur[at(f, far * (1 - zy) + t, group), :]
                v = cur[at(f, far * zy + t, group), :]
                ahead.append(rolled(v, 16))
                back.append(rolled(v, -16))
            for group in range(3):
                high = jnp.where(place == 0, ahead[group - 1], ahead[group])
                low = jnp.where(place == 7, back[(group + 1) % 3], back[group])
                v = cur[at(f, far * zy + t, group), :]
                y_out[strip_at(f, t, group), :] = jnp.where(turn, jnp.where(first, low, high), v)


def corners(pos, y_in, y_out, to_in, to_out):
    zx, zy = tile_x(pos[0]), tile_y(pos[0])

    def copy(low, high):
        for f in range(F):
            for group in range(3):
                for r in range(2):
                    for out, x in ((to_in, 6 * (1 - zx) + r), (to_out, 6 * zx + r)):
                        row = ((f * 3 + group) * 2 + r) * 4
                        base = f * DEEP * HALF + group * 8 + x
                        out[row : row + 2, :] = low[pl.ds(base + HALF, 2, HALF), :]
                        out[row + 2 : row + 4, :] = high[pl.ds(base, 2, HALF), :]

    @pl.when(zy == 0)
    def _():
        copy(y_out, y_in)

    @pl.when(zy == 1)
    def _():
        copy(y_in, y_out)


def reorder(pos, rows, *refs):
    parts = refs[:8]
    cur, x_in, x_out, y_in, y_out = refs[8:13]
    held = refs[13]
    for i in range(8):
        for s in range(CAP):
            held[rows[i * CAP + s]] = parts[i][s]

    def convert(group, _):
        for f in range(F):
            vectors = [held[group * 8 + i, f] for i in range(8)]
            for y, v in enumerate(transposed(vectors)):
                cur[at(f, y, group), :] = v
        for y in range(Y):
            prim = [cur[at(f, y, group), :] for f in range(F)]
            for f, v in enumerate(conserved(prim)):
                if f:
                    cur[at(f, y, group), :] = v
        return 0

    lax.fori_loop(0, 3, convert, 0)
    faces(pos, cur, x_in, x_out, y_in, y_out)


def widen(pos, cur, x_in, x_out, y_in, y_out, c_in, c_out, main, side_rows):
    zx, zy = tile_x(pos[0]), tile_y(pos[0])
    for f in range(F):
        for group in range(3):
            for y in range(Y):
                main[wide_at(f, y, group), :] = cur[at(f, y, group), :]
            for t in range(DEEP):
                main[wide_at(f, Y * (1 - zy) - DEEP * zy + t, group), :] = y_in[strip_at(f, t, group), :]
                main[wide_at(f, Y * zy - DEEP * (1 - zy) + t, group), :] = y_out[strip_at(f, t, group), :]
                at_t = pl.ds(((f * 3 + group) * DEEP + t) * 8, 8)
                base = (f * WIDE + DEEP) * HALF + group * 8 + t
                side_rows[pl.ds(base + 5 * zx, 8, HALF), :] = x_in[at_t, :]
                side_rows[pl.ds(base + 5 * (1 - zx), 8, HALF), :] = x_out[at_t, :]
            for r in range(2):
                row = ((f * 3 + group) * 2 + r) * 4
                for c, beyond in ((c_in, 6 * zx), (c_out, 6 * (1 - zx))):
                    for k, y in ((0, -2), (2, Y)):
                        to = (f * WIDE + DEEP + y) * HALF + group * 8 + r + beyond
                        side_rows[pl.ds(to, 2, HALF), :] = c[row + k : row + k + 2, :]


def advance(number, source, initial, target, made):
    reach = 2 - number
    weight = (0.0, 0.75, 1.0 / 3.0)[number]

    def step(group, _):
        height = lax.broadcasted_iota(jnp.int32, (8, L), 1) % 16
        sub = lax.broadcasted_iota(jnp.int32, (8, L), 0)
        floor, roof = height == 0, height == 15
        left, right = sub == 0, sub == 7
        cells, fluxes = {}, {}

        def cell(part, y):
            if (part, y) not in cells:
                cons = [source[part][wide_at(f, y, group), :] for f in range(F)]
                cells[part, y] = cons, terms(cons)
            return cells[part, y]

        def flux_y(part, y):
            if (part, y) not in fluxes:
                fluxes[part, y] = double_flux(side(*cell(part, y), 1), side(*cell(part, y + 1), 1), 1)
            return fluxes[part, y]

        for y in range(-reach, Y + reach):
            own = [side(*cell(part, y), 0) for part in range(2)]
            turned = [[pltpu.roll(q, 7, 0) for q in o] for o in own]
            flux = []
            for part in range(2):
                ahead = [jnp.where(right, q, p) for p, q in zip(turned[part], turned[1 - part])]
                flux.append(double_flux(own[part], ahead, 0))
            turned = [[pltpu.roll(q, 1, 0) for q in o] for o in flux]
            beside = reach > 0 and 1 - reach <= y < Y - 1 + reach
            for part in range(2 if beside else 1):
                cons, t = cell(part, y)
                change = [
                    v - jnp.where(left, q, p) for v, p, q in zip(flux[part], turned[part], turned[1 - part])
                ]
                change = [c + (b - a) for c, a, b in zip(change, flux_y(part, y - 1), flux_y(part, y))]
                low = side(cons, t, 2)
                flux_z = double_flux(low, [rolled(q, -1) for q in low], 2)
                for f in range(F):
                    wall = 2.0 * t[1] if f == 3 else 0.0
                    upper = jnp.where(roof, wall, flux_z[f])
                    lower = jnp.where(floor, wall, rolled(flux_z[f], 1))
                    change[f] = change[f] + (upper - lower)
                out = [c - (0.5 * STEP) * d for c, d in zip(cons, change)]
                if number:
                    out = [
                        weight * initial[part][wide_at(f, y, group), :] + (1.0 - weight) * o
                        for f, o in enumerate(out)
                    ]
                if number == 2:
                    out = primitive(out)
                for f in range(F):
                    target[part][wide_at(f, y, group), :] = out[f]
        if number == 2:
            for f in range(F):
                vectors = [target[0][wide_at(f, y, group), :] for y in range(Y)]
                for i, v in enumerate(transposed(vectors)):
                    made[group * 8 + i, f] = v
        return 0

    lax.fori_loop(0, 3, step, 0)


def sections(pos, cur, x_in, x_out, y_in, y_out, c_in, c_out, made, *held):
    initial, first, second = held[0:2], held[2:4], held[4:6]
    widen(pos, cur, x_in, x_out, y_in, y_out, c_in, c_out, *initial)
    advance(0, initial, initial, first, made)
    advance(1, first, initial, second, made)
    advance(2, second, initial, first, made)


def pack_out(pos, final, mine, other, *outs):
    z, core = pos[0], pos[1]
    for k in range(4):
        d = (z ^ k) * 2 + core
        for s in range(OUT):
            j = final[d * 8 + s]
            row = jnp.maximum(j, 0) >> 1
            kind = jnp.full((X, L), jnp.where(j < 0, 2, (j & 1) ^ core), jnp.int32)
            for f in range(F):
                outs[k][s, f] = jnp.where(kind == 0, mine[row, f], jnp.where(kind == 1, other[row, f], 0.0))


def body(block_cells, slot_blocks):
    row, col = lax.axis_index("row"), lax.axis_index("col")
    pos = jnp.stack([row // 2, row % 2, col]).astype(jnp.int32)

    def to(array, route):
        pairs = []
        for r in range(N_ROW):
            for c in range(N_COL):
                z, core, c2 = route(r // 2, r % 2, c)
                pairs.append((r * N_COL + c, (z * 2 + core) * N_COL + c2 % N_COL))
        return lax.ppermute(array, ("row", "col"), pairs)

    def over_z(array, k):
        return array if k == 0 else to(array, lambda z, core, c: (z ^ k, core, c))

    def over_core(array):
        return to(array, lambda z, core, c: (z, 1 - core, c))

    tiles = [shape(CAP, F, X, L)] * 4
    parts = pl.pallas_call(
        pack_in,
        out_shape=tiles,
        in_specs=[SMEM, pl.BlockSpec(memory_space=pltpu.HBM)],
        out_specs=[VMEM] * 4,
        scratch_shapes=[pltpu.SemaphoreType.DMA((4,))],
        compiler_params=PARAMS,
        name="pack_in",
    )(pos, block_cells)
    final, rows, own = pl.pallas_call(
        table,
        out_shape=[
            jax.ShapeDtypeStruct((N_ROW * 8,), jnp.int32),
            jax.ShapeDtypeStruct((N_ROW * CAP,), jnp.int32),
            tiles[0],
        ],
        in_specs=[SMEM, SMEM, ANY],
        out_specs=[SMEM, SMEM, ANY],
        input_output_aliases={2: 2},
        scratch_shapes=[pltpu.SMEM((N_ROW * 16,), jnp.int32), pltpu.SMEM((N_ROW,), jnp.int32)],
        compiler_params=PARAMS,
        cost_estimate=pl.CostEstimate(flops=0, bytes_accessed=20_000_000, transcendentals=0),
        name="table",
    )(pos, slot_blocks, parts[0])
    gathered = []
    for k in range(4):
        here = over_z(parts[k], k) if k else own
        gathered += [here, over_core(here)]

    whole = shape(F * Y * HALF, L)
    layer = shape(F * DEEP * HALF, L)
    initial, x_in, x_out, y_in, y_out = pl.pallas_call(
        reorder,
        out_shape=[whole] + [layer] * 4,
        in_specs=[SMEM, SMEM] + [VMEM] * 8,
        out_specs=[VMEM] * 5,
        scratch_shapes=[pltpu.VMEM((HALF + 1, F, X, L), jnp.float32)],
        compiler_params=PARAMS,
        name="reorder",
    )(pos, rows, *gathered)

    def x_partner(z):
        return z ^ 1

    def y_partner(z):
        return z ^ 3

    def over_x(inner, outer):
        return (
            to(inner, lambda z, core, c: (x_partner(z), core, c)),
            to(outer, lambda z, core, c: (x_partner(z), core, c + 2 * tile_x(z) - 1)),
        )

    def over_y(inner, outer):
        return (
            to(inner, lambda z, core, c: (y_partner(z), core, c)),
            to(outer, lambda z, core, c: (y_partner(z), 1 - core, c + 2 * tile_y(z) - 1)),
        )

    y_layers = over_y(y_in, y_out)
    x_layers = over_x(x_in, x_out)
    corner_cells = pl.pallas_call(
        corners,
        out_shape=[shape(F * 3 * 8, L)] * 2,
        in_specs=[SMEM, VMEM, VMEM],
        out_specs=[VMEM] * 2,
        compiler_params=PARAMS,
        name="corners",
    )(pos, *y_layers)
    corner_cells = over_x(*corner_cells)
    current = pl.pallas_call(
        sections,
        out_shape=shape(HALF, F, X, L),
        in_specs=[SMEM] + [VMEM] * 7,
        out_specs=VMEM,
        scratch_shapes=[pltpu.VMEM((F * WIDE * HALF, L), jnp.float32)] * 6,
        compiler_params=PARAMS,
        name="sections",
    )(pos, initial, *x_layers, *y_layers, *corner_cells)

    leaving = pl.pallas_call(
        pack_out,
        out_shape=[shape(OUT, F, X, L)] * 4,
        in_specs=[SMEM, SMEM, VMEM, VMEM],
        out_specs=[VMEM] * 4,
        compiler_params=PARAMS,
        name="pack_out",
    )(pos, final, current, over_core(current))
    arrived = [over_z(leaving[k], k) for k in range(4)]
    return pl.pallas_call(
        unpack_out,
        out_shape=shape(OUT, F, 2 * X, 2 * L),
        in_specs=[SMEM] + [ANY] * 4,
        out_specs=ANY,
        scratch_shapes=[pltpu.SemaphoreType.DMA((4,))],
        compiler_params=PARAMS,
        name="unpack_out",
    )(pos, *arrived)


def solution(mesh):
    in_specs = (P(("row", "col"), None, None, None), P())
    out_specs = P(("row", "col"), None, None, None)
    return jax.shard_map(body, mesh=mesh, in_specs=in_specs, out_specs=out_specs, check_vma=False)
```

```python
import math

import jax
import jax.numpy as jnp
from jax import lax
from jax.experimental import pallas as pl
from jax.experimental.pallas import tpu as pltpu
from jax.sharding import PartitionSpec as P

CAP = 11
OUT = 7
NBY = 48
N_ROW = 8
N_COL = 16
HALF = NBY // 2
F = 5
X = Y = 8
L = 128
DEEP = 3
WIDE = Y + 2 * DEEP

GAMMA = 1.4
STEP = 0.12
LOG2_E = 1.0 / math.log(2.0)

VMEM = pl.BlockSpec(memory_space=pltpu.VMEM)
SMEM = pl.BlockSpec(memory_space=pltpu.SMEM)
ANY = pl.BlockSpec(memory_space=pl.ANY)
PARAMS = pltpu.CompilerParams(vmem_limit_bytes=48 * 1024 * 1024)


def shape(*dims):
    return jax.ShapeDtypeStruct(dims, jnp.float32)


def tile_x(z):
    return ((z + 1) // 2) % 2


def tile_y(z):
    return z // 2


def pack_in(pos, cells, *outs):
    z = pos[0]
    for k in range(4):
        x = pl.ds(pl.multiple_of(tile_x(z ^ k) * X, X), X)
        y = pl.ds(pl.multiple_of(tile_y(z ^ k) * L, L), L)
        for s in range(CAP):
            for f in range(F):
                outs[k][s, f] = cells[s, f, x, y]


def unpack_out(pos, *refs):
    parts, out, sems = refs[:4], refs[4], refs[5]
    z = pos[0]
    copies = []
    for k in range(4):
        zk = z ^ k
        copies.append(
            pltpu.make_async_copy(
                parts[k],
                out.at[
                    :, :, pl.ds(pl.multiple_of(tile_x(zk) * X, X), X), pl.ds(pl.multiple_of(tile_y(zk) * L, L), L)
                ],
                sems.at[k],
            )
        )
    for c in copies:
        c.start()
    for c in copies:
        c.wait()


def table(pos, slots, _tile, final, rows, _same, held, count):
    z, core, g = pos[0], pos[1], pos[2]
    for d in range(N_ROW):
        n = jnp.int32(0)
        place = ((z ^ d // 2) * 2 + (core ^ d % 2)) * CAP
        for s in range(CAP):
            b = slots[d * N_COL + g, s]
            j = b - g * NBY
            held[d * 16 + s] = j
            here = jnp.logical_and(b >= 0, (j & 1) == core)
            rows[place + s] = jnp.where(here, j >> 1, HALF)
            n = n + jnp.where(b >= 0, 1, 0)
        count[d] = n
    for bit in range(3):
        for low in range(N_ROW):
            if low >> bit & 1:
                continue
            high = low | 1 << bit
            a, b = count[low], count[high]
            up = a > b
            src = jnp.where(up, low, high)
            dst = jnp.where(up, high, low)
            n_src = jnp.maximum(a, b)
            n_dst = jnp.minimum(a, b)
            moved = (n_src - n_dst) // 2

            def move(i, _, src=src, dst=dst, n_src=n_src, n_dst=n_dst, moved=moved):
                held[dst * 16 + n_dst + i] = held[src * 16 + n_src - moved + i]
                return 0

            lax.fori_loop(0, moved, move, 0)
            count[src] = n_src - moved
            count[dst] = n_dst + moved
    for d in range(N_ROW):
        n = count[d]
        for s in range(8):
            final[d * 8 + s] = jnp.where(s < n, held[d * 16 + s], -1)


def rolled(v, shift):
    shift %= L
    return v if shift == 0 else pltpu.roll(v, shift, 1)


def inverse(rho):
    guess = pl.reciprocal(rho, approx=True)
    return guess * (2.0 - rho * guess)


def terms(cons):
    rho, mx, my, mz, energy = cons
    inv = inverse(rho)
    u, v, w = mx * inv, my * inv, mz * inv
    p = (GAMMA - 1.0) * energy - (0.5 * (GAMMA - 1.0)) * (mx * u + my * v + mz * w)
    theta = p * inv
    power = jnp.log(theta)
    sound = jnp.exp2(power * (0.5 * LOG2_E) + 0.5 * math.log2(GAMMA))
    kappa = jnp.exp2(power * (0.7 * LOG2_E) + math.log2(0.2))
    return (u, v, w), p, theta, sound, kappa


def side(cons, t, n):
    vel, p, theta, sound, kappa = t
    flux = [cons[f] * vel[n] for f in (1, 2, 3)]
    flux[n] = flux[n] + p
    return (*cons, *flux, (cons[4] + p) * vel[n], theta, kappa, jnp.abs(vel[n]) + sound)


def double_flux(low, high, n):
    speed = jnp.maximum(low[11], high[11])
    out = []
    for f in range(F):
        k = F + f - 1 if f else n + 1
        out.append((low[k] + high[k]) - speed * (high[f] - low[f]))
    out[4] = out[4] - (low[10] + high[10]) * (high[9] - low[9])
    return out


def primitive(cons):
    rho, mx, my, mz, energy = cons
    inv = inverse(rho)
    u, v, w = mx * inv, my * inv, mz * inv
    return [rho, u, v, w, (GAMMA - 1.0) * (energy - 0.5 * rho * (u * u + v * v + w * w))]


def conserved(prim):
    rho, u, v, w, p = prim
    return [rho, rho * u, rho * v, rho * w, p * (1.0 / (GAMMA - 1.0)) + 0.5 * rho * (u * u + v * v + w * w)]


def at(f, y, group):
    return pl.ds(pl.multiple_of((f * Y + y) * HALF + group * 8, 8), 8)


def wide_at(f, y, group):
    return pl.ds(pl.multiple_of((f * WIDE + DEEP + y) * HALF + group * 8, 8), 8)


def strip_at(f, t, group):
    return pl.ds(pl.multiple_of((f * DEEP + t) * HALF + group * 8, 8), 8)


def x_layer_at(f, group, x):
    return pl.ds(f * Y * HALF + group * 8 + x, Y, HALF)


def transposed(vectors):
    place = lax.broadcasted_iota(jnp.int32, (8, L), 1) // 16
    vectors = list(vectors)
    for bit in (1, 2, 4):
        clear = (place & bit) == 0
        for i in range(8):
            if i & bit:
                continue
            a, b = vectors[i], vectors[i | bit]
            vectors[i] = jnp.where(clear, a, rolled(b, 16 * bit))
            vectors[i | bit] = jnp.where(clear, rolled(a, -16 * bit), b)
    return vectors


def faces(pos, cur, x_in, x_out, y_in, y_out):
    zx, zy, core = tile_x(pos[0]), tile_y(pos[0]), pos[1]
    place = lax.broadcasted_iota(jnp.int32, (8, L), 1) // 16
    first = jnp.full((8, L), zy, jnp.int32) == 0
    turn = jnp.full((8, L), jnp.where(core == zy, 1, 0), jnp.int32) == 1
    far = Y - DEEP
    for f in range(F):
        for t in range(DEEP):
            ahead, back = [], []
            for group in range(3):
                to = pl.ds(((f * 3 + group) * DEEP + t) * 8, 8)
                x_in[to, :] = cur[x_layer_at(f, group, far * (1 - zx) + t), :]
                x_out[to, :] = cur[x_layer_at(f, group, far * zx + t), :]
                y_in[strip_at(f, t, group), :] = cur[at(f, far * (1 - zy) + t, group), :]
                v = cur[at(f, far * zy + t, group), :]
                ahead.append(rolled(v, 16))
                back.append(rolled(v, -16))
            for group in range(3):
                high = jnp.where(place == 0, ahead[group - 1], ahead[group])
                low = jnp.where(place == 7, back[(group + 1) % 3], back[group])
                v = cur[at(f, far * zy + t, group), :]
                y_out[strip_at(f, t, group), :] = jnp.where(turn, jnp.where(first, low, high), v)


def corners(pos, y_in, y_out, to_in, to_out):
    zx, zy = tile_x(pos[0]), tile_y(pos[0])

    def copy(low, high):
        for f in range(F):
            for group in range(3):
                for r in range(2):
                    for out, x in ((to_in, 6 * (1 - zx) + r), (to_out, 6 * zx + r)):
                        row = ((f * 3 + group) * 2 + r) * 4
                        base = f * DEEP * HALF + group * 8 + x
                        out[row : row + 2, :] = low[pl.ds(base + HALF, 2, HALF), :]
                        out[row + 2 : row + 4, :] = high[pl.ds(base, 2, HALF), :]

    @pl.when(zy == 0)
    def _():
        copy(y_out, y_in)

    @pl.when(zy == 1)
    def _():
        copy(y_in, y_out)


def reorder(pos, rows, *refs):
    parts = refs[:8]
    cur, x_in, x_out, y_in, y_out = refs[8:13]
    held = refs[13]
    for i in range(8):
        for s in range(CAP):
            held[rows[i * CAP + s]] = parts[i][s]

    def convert(group, _):
        for f in range(F):
            vectors = [held[group * 8 + i, f] for i in range(8)]
            for y, v in enumerate(transposed(vectors)):
                cur[at(f, y, group), :] = v
        for y in range(Y):
            prim = [cur[at(f, y, group), :] for f in range(F)]
            for f, v in enumerate(conserved(prim)):
                if f:
                    cur[at(f, y, group), :] = v
        return 0

    lax.fori_loop(0, 3, convert, 0)
    faces(pos, cur, x_in, x_out, y_in, y_out)


def widen(pos, cur, x_in, x_out, y_in, y_out, c_in, c_out, main, side_rows):
    zx, zy = tile_x(pos[0]), tile_y(pos[0])
    for f in range(F):
        for group in range(3):
            for y in range(Y):
                main[wide_at(f, y, group), :] = cur[at(f, y, group), :]
            for t in range(DEEP):
                main[wide_at(f, Y * (1 - zy) - DEEP * zy + t, group), :] = y_in[strip_at(f, t, group), :]
                main[wide_at(f, Y * zy - DEEP * (1 - zy) + t, group), :] = y_out[strip_at(f, t, group), :]
                at_t = pl.ds(((f * 3 + group) * DEEP + t) * 8, 8)
                base = (f * WIDE + DEEP) * HALF + group * 8 + t
                side_rows[pl.ds(base + 5 * zx, 8, HALF), :] = x_in[at_t, :]
                side_rows[pl.ds(base + 5 * (1 - zx), 8, HALF), :] = x_out[at_t, :]
            for r in range(2):
                row = ((f * 3 + group) * 2 + r) * 4
                for c, beyond in ((c_in, 6 * zx), (c_out, 6 * (1 - zx))):
                    for k, y in ((0, -2), (2, Y)):
                        to = (f * WIDE + DEEP + y) * HALF + group * 8 + r + beyond
                        side_rows[pl.ds(to, 2, HALF), :] = c[row + k : row + k + 2, :]


def advance(number, source, initial, target, made):
    reach = 2 - number
    weight = (0.0, 0.75, 1.0 / 3.0)[number]

    def step(group, _):
        height = lax.broadcasted_iota(jnp.int32, (8, L), 1) % 16
        sub = lax.broadcasted_iota(jnp.int32, (8, L), 0)
        floor, roof = height == 0, height == 15
        left, right = sub == 0, sub == 7
        cells, fluxes = {}, {}

        def cell(part, y):
            if (part, y) not in cells:
                cons = [source[part][wide_at(f, y, group), :] for f in range(F)]
                cells[part, y] = cons, terms(cons)
            return cells[part, y]

        def flux_y(part, y):
            if (part, y) not in fluxes:
                fluxes[part, y] = double_flux(side(*cell(part, y), 1), side(*cell(part, y + 1), 1), 1)
            return fluxes[part, y]

        for y in range(-reach, Y + reach):
            own = [side(*cell(part, y), 0) for part in range(2)]
            turned = [[pltpu.roll(q, 7, 0) for q in o] for o in own]
            flux = []
            for part in range(2):
                ahead = [jnp.where(right, q, p) for p, q in zip(turned[part], turned[1 - part])]
                flux.append(double_flux(own[part], ahead, 0))
            turned = [[pltpu.roll(q, 1, 0) for q in o] for o in flux]
            beside = reach > 0 and 1 - reach <= y < Y - 1 + reach
            for part in range(2 if beside else 1):
                cons, t = cell(part, y)
                change = [
                    v - jnp.where(left, q, p) for v, p, q in zip(flux[part], turned[part], turned[1 - part])
                ]
                change = [c + (b - a) for c, a, b in zip(change, flux_y(part, y - 1), flux_y(part, y))]
                low = side(cons, t, 2)
                up = [rolled(q, -1) for q in cons]
                flux_z = double_flux(low, side(up, terms(up), 2), 2)
                for f in range(F):
                    upper = jnp.where(roof, 2.0 * t[1] if f == 3 else 0.0, flux_z[f])
                    lower = rolled(upper, 1)
                    if f == 3:
                        lower = jnp.where(floor, 2.0 * t[1], lower)
                    change[f] = change[f] + (upper - lower)
                out = [c - (0.5 * STEP) * d for c, d in zip(cons, change)]
                if number:
                    out = [
                        weight * initial[part][wide_at(f, y, group), :] + (1.0 - weight) * o
                        for f, o in enumerate(out)
                    ]
                if number == 2:
                    out = primitive(out)
                for f in range(F):
                    target[part][wide_at(f, y, group), :] = out[f]
        if number == 2:
            for f in range(F):
                vectors = [target[0][wide_at(f, y, group), :] for y in range(Y)]
                for i, v in enumerate(transposed(vectors)):
                    made[group * 8 + i, f] = v
        return 0

    lax.fori_loop(0, 3, step, 0)


def sections(pos, cur, x_in, x_out, y_in, y_out, c_in, c_out, made, *held):
    initial, first, second = held[0:2], held[2:4], held[4:6]
    widen(pos, cur, x_in, x_out, y_in, y_out, c_in, c_out, *initial)
    advance(0, initial, initial, first, made)
    advance(1, first, initial, second, made)
    advance(2, second, initial, first, made)


def pack_out(pos, final, mine, other, *outs):
    z, core = pos[0], pos[1]
    for k in range(4):
        d = (z ^ k) * 2 + core
        for s in range(OUT):
            j = final[d * 8 + s]
            row = jnp.maximum(j, 0) >> 1
            kind = jnp.full((X, L), jnp.where(j < 0, 2, (j & 1) ^ core), jnp.int32)
            for f in range(F):
                outs[k][s, f] = jnp.where(kind == 0, mine[row, f], jnp.where(kind == 1, other[row, f], 0.0))


def body(block_cells, slot_blocks):
    row, col = lax.axis_index("row"), lax.axis_index("col")
    pos = jnp.stack([row // 2, row % 2, col]).astype(jnp.int32)

    def to(array, route):
        pairs = []
        for r in range(N_ROW):
            for c in range(N_COL):
                z, core, c2 = route(r // 2, r % 2, c)
                pairs.append((r * N_COL + c, (z * 2 + core) * N_COL + c2 % N_COL))
        return lax.ppermute(array, ("row", "col"), pairs)

    def over_z(array, k):
        return array if k == 0 else to(array, lambda z, core, c: (z ^ k, core, c))

    def over_core(array):
        return to(array, lambda z, core, c: (z, 1 - core, c))

    tiles = [shape(CAP, F, X, L)] * 4
    parts = pl.pallas_call(
        pack_in,
        out_shape=tiles,
        in_specs=[SMEM, VMEM],
        out_specs=[VMEM] * 4,
        compiler_params=PARAMS,
        name="pack_in",
    )(pos, block_cells)
    final, rows, own = pl.pallas_call(
        table,
        out_shape=[
            jax.ShapeDtypeStruct((N_ROW * 8,), jnp.int32),
            jax.ShapeDtypeStruct((N_ROW * CAP,), jnp.int32),
            tiles[0],
        ],
        in_specs=[SMEM, SMEM, ANY],
        out_specs=[SMEM, SMEM, ANY],
        input_output_aliases={2: 2},
        scratch_shapes=[pltpu.SMEM((N_ROW * 16,), jnp.int32), pltpu.SMEM((N_ROW,), jnp.int32)],
        compiler_params=PARAMS,
        cost_estimate=pl.CostEstimate(flops=0, bytes_accessed=20_000_000, transcendentals=0),
        name="table",
    )(pos, slot_blocks, parts[0])
    gathered = []
    for k in range(4):
        here = over_z(parts[k], k) if k else own
        gathered += [here, over_core(here)]

    whole = shape(F * Y * HALF, L)
    layer = shape(F * DEEP * HALF, L)
    initial, x_in, x_out, y_in, y_out = pl.pallas_call(
        reorder,
        out_shape=[whole] + [layer] * 4,
        in_specs=[SMEM, SMEM] + [VMEM] * 8,
        out_specs=[VMEM] * 5,
        scratch_shapes=[pltpu.VMEM((HALF + 1, F, X, L), jnp.float32)],
        compiler_params=PARAMS,
        name="reorder",
    )(pos, rows, *gathered)

    def x_partner(z):
        return z ^ 1

    def y_partner(z):
        return z ^ 3

    def over_x(inner, outer):
        return (
            to(inner, lambda z, core, c: (x_partner(z), core, c)),
            to(outer, lambda z, core, c: (x_partner(z), core, c + 2 * tile_x(z) - 1)),
        )

    def over_y(inner, outer):
        return (
            to(inner, lambda z, core, c: (y_partner(z), core, c)),
            to(outer, lambda z, core, c: (y_partner(z), 1 - core, c + 2 * tile_y(z) - 1)),
        )

    y_layers = over_y(y_in, y_out)
    x_layers = over_x(x_in, x_out)
    corner_cells = pl.pallas_call(
        corners,
        out_shape=[shape(F * 3 * 8, L)] * 2,
        in_specs=[SMEM, VMEM, VMEM],
        out_specs=[VMEM] * 2,
        compiler_params=PARAMS,
        name="corners",
    )(pos, *y_layers)
    corner_cells = over_x(*corner_cells)
    current = pl.pallas_call(
        sections,
        out_shape=shape(HALF, F, X, L),
        in_specs=[SMEM] + [VMEM] * 7,
        out_specs=VMEM,
        scratch_shapes=[pltpu.VMEM((F * WIDE * HALF, L), jnp.float32)] * 6,
        compiler_params=PARAMS,
        name="sections",
    )(pos, initial, *x_layers, *y_layers, *corner_cells)

    leaving = pl.pallas_call(
        pack_out,
        out_shape=[shape(OUT, F, X, L)] * 4,
        in_specs=[SMEM, SMEM, VMEM, VMEM],
        out_specs=[VMEM] * 4,
        compiler_params=PARAMS,
        name="pack_out",
    )(pos, final, current, over_core(current))
    arrived = [over_z(leaving[k], k) for k in range(4)]
    return pl.pallas_call(
        unpack_out,
        out_shape=shape(OUT, F, 2 * X, 2 * L),
        in_specs=[SMEM] + [ANY] * 4,
        out_specs=ANY,
        scratch_shapes=[pltpu.SemaphoreType.DMA((4,))],
        compiler_params=PARAMS,
        name="unpack_out",
    )(pos, *arrived)


def solution(mesh):
    in_specs = (P(("row", "col"), None, None, None), P())
    out_specs = P(("row", "col"), None, None, None)
    return jax.shard_map(body, mesh=mesh, in_specs=in_specs, out_specs=out_specs, check_vma=False)
```

```python
import math

import jax
import jax.numpy as jnp
from jax import lax
from jax.experimental import pallas as pl
from jax.experimental.pallas import tpu as pltpu
from jax.sharding import PartitionSpec as P

CAP = 11
OUT = 7
NBY = 48
N_ROW = 8
N_COL = 16
HALF = NBY // 2
F = 5
X = Y = 8
L = 128
DEEP = 3
WIDE = Y + 2 * DEEP

GAMMA = 1.4
STEP = 0.12
LOG2_E = 1.0 / math.log(2.0)

VMEM = pl.BlockSpec(memory_space=pltpu.VMEM)
SMEM = pl.BlockSpec(memory_space=pltpu.SMEM)
ANY = pl.BlockSpec(memory_space=pl.ANY)
PARAMS = pltpu.CompilerParams(vmem_limit_bytes=48 * 1024 * 1024)


def shape(*dims):
    return jax.ShapeDtypeStruct(dims, jnp.float32)


def tile_x(z):
    return ((z + 1) // 2) % 2


def tile_y(z):
    return z // 2


def pack_in(pos, cells, *outs):
    z = pos[0]
    for k in range(4):
        x = pl.ds(pl.multiple_of(tile_x(z ^ k) * X, X), X)
        y = pl.ds(pl.multiple_of(tile_y(z ^ k) * L, L), L)
        for s in range(CAP):
            for f in range(F):
                outs[k][s, f] = cells[s, f, x, y]


def unpack_out(pos, *refs):
    parts, out, sems = refs[:4], refs[4], refs[5]
    z = pos[0]
    copies = []
    for k in range(4):
        zk = z ^ k
        copies.append(
            pltpu.make_async_copy(
                parts[k],
                out.at[
                    :, :, pl.ds(pl.multiple_of(tile_x(zk) * X, X), X), pl.ds(pl.multiple_of(tile_y(zk) * L, L), L)
                ],
                sems.at[k],
            )
        )
    for c in copies:
        c.start()
    for c in copies:
        c.wait()


def table(pos, slots, _tile, final, rows, _same, held, count):
    z, core, g = pos[0], pos[1], pos[2]
    for d in range(N_ROW):
        n = jnp.int32(0)
        place = ((z ^ d // 2) * 2 + (core ^ d % 2)) * CAP
        for s in range(CAP):
            b = slots[d * N_COL + g, s]
            j = b - g * NBY
            held[d * 16 + s] = j
            here = jnp.logical_and(b >= 0, (j & 1) == core)
            rows[place + s] = jnp.where(here, j >> 1, HALF)
            n = n + jnp.where(b >= 0, 1, 0)
        count[d] = n
    for bit in range(3):
        for low in range(N_ROW):
            if low >> bit & 1:
                continue
            high = low | 1 << bit
            a, b = count[low], count[high]
            up = a > b
            src = jnp.where(up, low, high)
            dst = jnp.where(up, high, low)
            n_src = jnp.maximum(a, b)
            n_dst = jnp.minimum(a, b)
            moved = (n_src - n_dst) // 2

            def move(i, _, src=src, dst=dst, n_src=n_src, n_dst=n_dst, moved=moved):
                held[dst * 16 + n_dst + i] = held[src * 16 + n_src - moved + i]
                return 0

            lax.fori_loop(0, moved, move, 0)
            count[src] = n_src - moved
            count[dst] = n_dst + moved
    for d in range(N_ROW):
        n = count[d]
        for s in range(8):
            final[d * 8 + s] = jnp.where(s < n, held[d * 16 + s], -1)


def rolled(v, shift):
    shift %= L
    return v if shift == 0 else pltpu.roll(v, shift, 1)


def inverse(rho):
    guess = pl.reciprocal(rho, approx=True)
    return guess * (2.0 - rho * guess)


def terms(cons):
    rho, mx, my, mz, energy = cons
    inv = inverse(rho)
    u, v, w = mx * inv, my * inv, mz * inv
    p = (GAMMA - 1.0) * energy - (0.5 * (GAMMA - 1.0)) * (mx * u + my * v + mz * w)
    theta = p * inv
    power = jnp.log(theta)
    sound = jnp.exp2(power * (0.5 * LOG2_E) + 0.5 * math.log2(GAMMA))
    kappa = jnp.exp2(power * (0.7 * LOG2_E) + math.log2(0.2))
    return (u, v, w), p, theta, sound, kappa


def side(cons, t, n):
    vel, p, theta, sound, kappa = t
    flux = [cons[f] * vel[n] for f in (1, 2, 3)]
    flux[n] = flux[n] + p
    return (*cons, *flux, (cons[4] + p) * vel[n], theta, kappa, jnp.abs(vel[n]) + sound)


def double_flux(low, high, n):
    speed = jnp.maximum(low[11], high[11])
    out = []
    for f in range(F):
        k = F + f - 1 if f else n + 1
        out.append((low[k] + high[k]) - speed * (high[f] - low[f]))
    out[4] = out[4] - (low[10] + high[10]) * (high[9] - low[9])
    return out


def primitive(cons):
    rho, mx, my, mz, energy = cons
    inv = inverse(rho)
    u, v, w = mx * inv, my * inv, mz * inv
    return [rho, u, v, w, (GAMMA - 1.0) * (energy - 0.5 * rho * (u * u + v * v + w * w))]


def conserved(prim):
    rho, u, v, w, p = prim
    return [rho, rho * u, rho * v, rho * w, p * (1.0 / (GAMMA - 1.0)) + 0.5 * rho * (u * u + v * v + w * w)]


def at(f, y, group):
    return pl.ds(pl.multiple_of((f * Y + y) * HALF + group * 8, 8), 8)


def wide_at(f, y, group):
    return pl.ds(pl.multiple_of((f * WIDE + DEEP + y) * HALF + group * 8, 8), 8)


def strip_at(f, t, group):
    return pl.ds(pl.multiple_of((f * DEEP + t) * HALF + group * 8, 8), 8)


def x_layer_at(f, group, x):
    return pl.ds(f * Y * HALF + group * 8 + x, Y, HALF)


def transposed(vectors):
    place = lax.broadcasted_iota(jnp.int32, (8, L), 1) // 16
    vectors = list(vectors)
    for bit in (1, 2, 4):
        clear = (place & bit) == 0
        for i in range(8):
            if i & bit:
                continue
            a, b = vectors[i], vectors[i | bit]
            vectors[i] = jnp.where(clear, a, rolled(b, 16 * bit))
            vectors[i | bit] = jnp.where(clear, rolled(a, -16 * bit), b)
    return vectors


def faces(pos, cur, x_in, x_out, y_in, y_out):
    zx, zy, core = tile_x(pos[0]), tile_y(pos[0]), pos[1]
    place = lax.broadcasted_iota(jnp.int32, (8, L), 1) // 16
    first = jnp.full((8, L), zy, jnp.int32) == 0
    turn = jnp.full((8, L), jnp.where(core == zy, 1, 0), jnp.int32) == 1
    far = Y - DEEP
    for f in range(F):
        for t in range(DEEP):
            ahead, back = [], []
            for group in range(3):
                to = pl.ds(((f * 3 + group) * DEEP + t) * 8, 8)
                x_in[to, :] = cur[x_layer_at(f, group, far * (1 - zx) + t), :]
                x_out[to, :] = cur[x_layer_at(f, group, far * zx + t), :]
                y_in[strip_at(f, t, group), :] = cur[at(f, far * (1 - zy) + t, group), :]
                v = cur[at(f, far * zy + t, group), :]
                ahead.append(rolled(v, 16))
                back.append(rolled(v, -16))
            for group in range(3):
                high = jnp.where(place == 0, ahead[group - 1], ahead[group])
                low = jnp.where(place == 7, back[(group + 1) % 3], back[group])
                v = cur[at(f, far * zy + t, group), :]
                y_out[strip_at(f, t, group), :] = jnp.where(turn, jnp.where(first, low, high), v)


def corners(pos, y_in, y_out, to_in, to_out):
    zx, zy = tile_x(pos[0]), tile_y(pos[0])

    def copy(low, high):
        for f in range(F):
            for group in range(3):
                for r in range(2):
                    for out, x in ((to_in, 6 * (1 - zx) + r), (to_out, 6 * zx + r)):
                        row = ((f * 3 + group) * 2 + r) * 4
                        base = f * DEEP * HALF + group * 8 + x
                        out[row : row + 2, :] = low[pl.ds(base + HALF, 2, HALF), :]
                        out[row + 2 : row + 4, :] = high[pl.ds(base, 2, HALF), :]

    @pl.when(zy == 0)
    def _():
        copy(y_out, y_in)

    @pl.when(zy == 1)
    def _():
        copy(y_in, y_out)


def reorder(pos, rows, *refs):
    parts = refs[:8]
    cur, x_in, x_out, y_in, y_out = refs[8:13]
    held = refs[13]
    for i in range(8):
        for s in range(CAP):
            held[rows[i * CAP + s]] = parts[i][s]

    def convert(group, _):
        for f in range(F):
            vectors = [held[group * 8 + i, f] for i in range(8)]
            for y, v in enumerate(transposed(vectors)):
                cur[at(f, y, group), :] = v
        for y in range(Y):
            prim = [cur[at(f, y, group), :] for f in range(F)]
            for f, v in enumerate(conserved(prim)):
                if f:
                    cur[at(f, y, group), :] = v
        return 0

    lax.fori_loop(0, 3, convert, 0)
    faces(pos, cur, x_in, x_out, y_in, y_out)


def widen(pos, cur, x_in, x_out, y_in, y_out, main, side_rows):
    zx, zy = tile_x(pos[0]), tile_y(pos[0])
    for f in range(F):
        for group in range(3):
            for y in range(Y):
                main[wide_at(f, y, group), :] = cur[at(f, y, group), :]
            for t in range(DEEP):
                main[wide_at(f, Y * (1 - zy) - DEEP * zy + t, group), :] = y_in[strip_at(f, t, group), :]
                main[wide_at(f, Y * zy - DEEP * (1 - zy) + t, group), :] = y_out[strip_at(f, t, group), :]
                at_t = pl.ds(((f * 3 + group) * DEEP + t) * 8, 8)
                base = (f * WIDE + DEEP) * HALF + group * 8 + t
                side_rows[pl.ds(base + 5 * zx, 8, HALF), :] = x_in[at_t, :]
                side_rows[pl.ds(base + 5 * (1 - zx), 8, HALF), :] = x_out[at_t, :]


def add_corners(pos, c_in, c_out, side_rows):
    zx = tile_x(pos[0])
    for f in range(F):
        for group in range(3):
            for r in range(2):
                row = ((f * 3 + group) * 2 + r) * 4
                for c, beyond in ((c_in, 6 * zx), (c_out, 6 * (1 - zx))):
                    for k, y in ((0, -2), (2, Y)):
                        to = (f * WIDE + DEEP + y) * HALF + group * 8 + r + beyond
                        side_rows[pl.ds(to, 2, HALF), :] = c[row + k : row + k + 2, :]


def advance(number, source, initial, target, main_ys, side_ys, made=None):
    weight = (0.0, 0.75, 1.0 / 3.0)[number]

    def step(group, _):
        height = lax.broadcasted_iota(jnp.int32, (8, L), 1) % 16
        sub = lax.broadcasted_iota(jnp.int32, (8, L), 0)
        floor, roof = height == 0, height == 15
        left, right = sub == 0, sub == 7
        cells, fluxes = {}, {}

        def cell(part, y):
            if (part, y) not in cells:
                cons = [source(part, y)[wide_at(f, y, group), :] for f in range(F)]
                cells[part, y] = cons, terms(cons)
            return cells[part, y]

        def flux_y(part, y):
            if (part, y) not in fluxes:
                fluxes[part, y] = double_flux(side(*cell(part, y), 1), side(*cell(part, y + 1), 1), 1)
            return fluxes[part, y]

        for y in sorted({*main_ys, *side_ys}):
            own = [side(*cell(part, y), 0) for part in range(2)]
            turned = [[pltpu.roll(q, 7, 0) for q in o] for o in own]
            flux = []
            for part in range(2):
                ahead = [jnp.where(right, q, p) for p, q in zip(turned[part], turned[1 - part])]
                flux.append(double_flux(own[part], ahead, 0))
            turned = [[pltpu.roll(q, 1, 0) for q in o] for o in flux]
            for part, ys in enumerate((main_ys, side_ys)):
                if y not in ys:
                    continue
                cons, t = cell(part, y)
                change = [
                    v - jnp.where(left, q, p) for v, p, q in zip(flux[part], turned[part], turned[1 - part])
                ]
                change = [c + (b - a) for c, a, b in zip(change, flux_y(part, y - 1), flux_y(part, y))]
                low = side(cons, t, 2)
                up = [rolled(q, -1) for q in cons]
                flux_z = double_flux(low, side(up, terms(up), 2), 2)
                for f in range(F):
                    upper = jnp.where(roof, 2.0 * t[1] if f == 3 else 0.0, flux_z[f])
                    lower = rolled(upper, 1)
                    if f == 3:
                        lower = jnp.where(floor, 2.0 * t[1], lower)
                    change[f] = change[f] + (upper - lower)
                out = [c - (0.5 * STEP) * d for c, d in zip(cons, change)]
                if number:
                    out = [
                        weight * initial(part, y)[wide_at(f, y, group), :] + (1.0 - weight) * o
                        for f, o in enumerate(out)
                    ]
                if number == 2:
                    out = primitive(out)
                for f in range(F):
                    target(part, y)[wide_at(f, y, group), :] = out[f]
        if number == 2:
            for f in range(F):
                vectors = [target(0, y)[wide_at(f, y, group), :] for y in range(Y)]
                for i, v in enumerate(transposed(vectors)):
                    made[group * 8 + i, f] = v
        return 0

    lax.fori_loop(0, 3, step, 0)


EARLY_MAIN = range(0, Y)
EARLY_SIDE = range(1, Y - 1)


def begin(pos, cur, x_in, x_out, y_in, y_out, main, side_rows, first_main, first_side):
    widen(pos, cur, x_in, x_out, y_in, y_out, main, side_rows)
    initial, first = (main, side_rows), (first_main, first_side)
    advance(0, lambda part, y: initial[part], None, lambda part, y: first[part], EARLY_MAIN, EARLY_SIDE)


def finish(pos, main, side_rows, early_main, early_side, c_in, c_out, made, corner_rows, *held):
    late, second = held[0:2], held[2:4]
    add_corners(pos, c_in, c_out, corner_rows)

    def initial(part, y):
        return (side_rows if 0 <= y < Y else corner_rows) if part else main

    def first(part, y):
        if part:
            return early_side if y in EARLY_SIDE else late[1]
        return early_main if y in EARLY_MAIN else late[0]

    advance(0, initial, None, first, (-2, -1, Y, Y + 1), (-1, 0, Y - 1, Y))
    advance(1, first, initial, lambda part, y: second[part], range(-1, Y + 1), range(0, Y))
    advance(2, lambda part, y: second[part], initial, lambda part, y: late[part], range(0, Y), (), made)


def pack_out(pos, final, mine, other, *outs):
    z, core = pos[0], pos[1]
    for k in range(4):
        d = (z ^ k) * 2 + core
        for s in range(OUT):
            j = final[d * 8 + s]
            row = jnp.maximum(j, 0) >> 1
            kind = jnp.full((X, L), jnp.where(j < 0, 2, (j & 1) ^ core), jnp.int32)
            for f in range(F):
                outs[k][s, f] = jnp.where(kind == 0, mine[row, f], jnp.where(kind == 1, other[row, f], 0.0))


def body(block_cells, slot_blocks):
    row, col = lax.axis_index("row"), lax.axis_index("col")
    pos = jnp.stack([row // 2, row % 2, col]).astype(jnp.int32)

    def to(array, route):
        pairs = []
        for r in range(N_ROW):
            for c in range(N_COL):
                z, core, c2 = route(r // 2, r % 2, c)
                pairs.append((r * N_COL + c, (z * 2 + core) * N_COL + c2 % N_COL))
        return lax.ppermute(array, ("row", "col"), pairs)

    def over_z(array, k):
        return array if k == 0 else to(array, lambda z, core, c: (z ^ k, core, c))

    def over_core(array):
        return to(array, lambda z, core, c: (z, 1 - core, c))

    tiles = [shape(CAP, F, X, L)] * 4
    parts = pl.pallas_call(
        pack_in,
        out_shape=tiles,
        in_specs=[SMEM, VMEM],
        out_specs=[VMEM] * 4,
        compiler_params=PARAMS,
        name="pack_in",
    )(pos, block_cells)
    final, rows, own = pl.pallas_call(
        table,
        out_shape=[
            jax.ShapeDtypeStruct((N_ROW * 8,), jnp.int32),
            jax.ShapeDtypeStruct((N_ROW * CAP,), jnp.int32),
            tiles[0],
        ],
        in_specs=[SMEM, SMEM, ANY],
        out_specs=[SMEM, SMEM, ANY],
        input_output_aliases={2: 2},
        scratch_shapes=[pltpu.SMEM((N_ROW * 16,), jnp.int32), pltpu.SMEM((N_ROW,), jnp.int32)],
        compiler_params=PARAMS,
        cost_estimate=pl.CostEstimate(flops=0, bytes_accessed=20_000_000, transcendentals=0),
        name="table",
    )(pos, slot_blocks, parts[0])
    gathered = []
    for k in range(4):
        here = over_z(parts[k], k) if k else own
        gathered += [here, over_core(here)]

    whole = shape(F * Y * HALF, L)
    layer = shape(F * DEEP * HALF, L)
    initial, x_in, x_out, y_in, y_out = pl.pallas_call(
        reorder,
        out_shape=[whole] + [layer] * 4,
        in_specs=[SMEM, SMEM] + [VMEM] * 8,
        out_specs=[VMEM] * 5,
        scratch_shapes=[pltpu.VMEM((HALF + 1, F, X, L), jnp.float32)],
        compiler_params=PARAMS,
        name="reorder",
    )(pos, rows, *gathered)

    def x_partner(z):
        return z ^ 1

    def y_partner(z):
        return z ^ 3

    def over_x(inner, outer):
        return (
            to(inner, lambda z, core, c: (x_partner(z), core, c)),
            to(outer, lambda z, core, c: (x_partner(z), core, c + 2 * tile_x(z) - 1)),
        )

    def over_y(inner, outer):
        return (
            to(inner, lambda z, core, c: (y_partner(z), core, c)),
            to(outer, lambda z, core, c: (y_partner(z), 1 - core, c + 2 * tile_y(z) - 1)),
        )

    y_layers = over_y(y_in, y_out)
    x_layers = over_x(x_in, x_out)
    corner_cells = pl.pallas_call(
        corners,
        out_shape=[shape(F * 3 * 8, L)] * 2,
        in_specs=[SMEM, VMEM, VMEM],
        out_specs=[VMEM] * 2,
        compiler_params=PARAMS,
        name="corners",
    )(pos, *y_layers)
    corner_cells = over_x(*corner_cells)
    wide = [F * WIDE * HALF, L]
    early = pl.pallas_call(
        begin,
        out_shape=[shape(*wide)] * 4,
        in_specs=[SMEM] + [VMEM] * 5,
        out_specs=[VMEM] * 4,
        compiler_params=PARAMS,
        cost_estimate=pl.CostEstimate(flops=0, bytes_accessed=10_000_000, transcendentals=0),
        name="begin",
    )(pos, initial, *x_layers, *y_layers)
    current = pl.pallas_call(
        finish,
        out_shape=shape(HALF, F, X, L),
        in_specs=[SMEM] + [VMEM] * 6,
        out_specs=VMEM,
        scratch_shapes=[pltpu.VMEM(wide, jnp.float32)] * 5,
        compiler_params=PARAMS,
        name="finish",
    )(pos, *early, *corner_cells)

    leaving = pl.pallas_call(
        pack_out,
        out_shape=[shape(OUT, F, X, L)] * 4,
        in_specs=[SMEM, SMEM, VMEM, VMEM],
        out_specs=[VMEM] * 4,
        compiler_params=PARAMS,
        name="pack_out",
    )(pos, final, current, over_core(current))
    arrived = [over_z(leaving[k], k) for k in range(4)]
    return pl.pallas_call(
        unpack_out,
        out_shape=shape(OUT, F, 2 * X, 2 * L),
        in_specs=[SMEM] + [ANY] * 4,
        out_specs=ANY,
        scratch_shapes=[pltpu.SemaphoreType.DMA((4,))],
        compiler_params=PARAMS,
        name="unpack_out",
    )(pos, *arrived)


def solution(mesh):
    in_specs = (P(("row", "col"), None, None, None), P())
    out_specs = P(("row", "col"), None, None, None)
    return jax.shard_map(body, mesh=mesh, in_specs=in_specs, out_specs=out_specs, check_vma=False)
```

```python
import math

import jax
import jax.numpy as jnp
from jax import lax
from jax.experimental import pallas as pl
from jax.experimental.pallas import tpu as pltpu
from jax.sharding import PartitionSpec as P

CAP = 11
OUT = 7
NBY = 48
N_ROW = 8
N_COL = 16
HALF = NBY // 2
F = 5
X = Y = 8
L = 128
DEEP = 3
WIDE = Y + 2 * DEEP

GAMMA = 1.4
STEP = 0.12
LOG2_E = 1.0 / math.log(2.0)

VMEM = pl.BlockSpec(memory_space=pltpu.VMEM)
SMEM = pl.BlockSpec(memory_space=pltpu.SMEM)
ANY = pl.BlockSpec(memory_space=pl.ANY)
PARAMS = pltpu.CompilerParams(vmem_limit_bytes=48 * 1024 * 1024)


def shape(*dims):
    return jax.ShapeDtypeStruct(dims, jnp.float32)


def tile_x(z):
    return ((z + 1) // 2) % 2


def tile_y(z):
    return z // 2


def pack_in(pos, cells, *outs):
    z = pos[0]
    for k in range(4):
        x = pl.ds(pl.multiple_of(tile_x(z ^ k) * X, X), X)
        y = pl.ds(pl.multiple_of(tile_y(z ^ k) * L, L), L)
        for s in range(CAP):
            for f in range(F):
                outs[k][s, f] = cells[s, f, x, y]


def unpack_out(which, pos, *refs):
    out, sems = refs[-2:]
    z = pos[0]
    copies = []
    for i, k in enumerate(which):
        x = pl.ds(pl.multiple_of(tile_x(z ^ k) * X, X), X)
        y = pl.ds(pl.multiple_of(tile_y(z ^ k) * L, L), L)
        copies.append(pltpu.make_async_copy(refs[i], out.at[:, :, x, y], sems.at[i]))
    for c in copies:
        c.start()
    for c in copies:
        c.wait()


def table(pos, slots, _tile, final, kept, given, mask, _same, held, count):
    z, core, g = pos[0], pos[1], pos[2]
    for d in range(N_ROW):
        n = jnp.int32(0)
        place = jnp.where(core == d % 2, (z ^ d // 2) * CAP, 4 * CAP)
        for s in range(CAP):
            b = slots[d * N_COL + g, s]
            j = b - g * NBY
            held[d * 16 + s] = j
            match = (j & 1) == core
            row = jnp.where(b >= 0, j >> 1, HALF)
            mine = jnp.where(match, row, HALF)
            kept[place + s] = mine
            given[place + s] = jnp.where(match, HALF, row)
            mask[mine] = jnp.where(core == d % 2, 1, 0)
            n = n + jnp.where(b >= 0, 1, 0)
        count[d] = n
    for bit in range(3):
        for low in range(N_ROW):
            if low >> bit & 1:
                continue
            high = low | 1 << bit
            a, b = count[low], count[high]
            up = a > b
            src = jnp.where(up, low, high)
            dst = jnp.where(up, high, low)
            n_src = jnp.maximum(a, b)
            n_dst = jnp.minimum(a, b)
            moved = (n_src - n_dst) // 2

            def move(i, _, src=src, dst=dst, n_src=n_src, n_dst=n_dst, moved=moved):
                held[dst * 16 + n_dst + i] = held[src * 16 + n_src - moved + i]
                return 0

            lax.fori_loop(0, moved, move, 0)
            count[src] = n_src - moved
            count[dst] = n_dst + moved
    for d in range(N_ROW):
        n = count[d]
        for s in range(8):
            final[d * 8 + s] = jnp.where(s < n, held[d * 16 + s], -1)


def rolled(v, shift):
    shift %= L
    return v if shift == 0 else pltpu.roll(v, shift, 1)


def inverse(rho):
    guess = pl.reciprocal(rho, approx=True)
    return guess * (2.0 - rho * guess)


def terms(cons):
    rho, mx, my, mz, energy = cons
    inv = inverse(rho)
    u, v, w = mx * inv, my * inv, mz * inv
    p = (GAMMA - 1.0) * energy - (0.5 * (GAMMA - 1.0)) * (mx * u + my * v + mz * w)
    theta = p * inv
    power = jnp.log(theta)
    sound = jnp.exp2(power * (0.5 * LOG2_E) + 0.5 * math.log2(GAMMA))
    kappa = jnp.exp2(power * (0.7 * LOG2_E) + math.log2(0.2))
    return (u, v, w), p, theta, sound, kappa


def side(cons, t, n):
    vel, p, theta, sound, kappa = t
    flux = [cons[f] * vel[n] for f in (1, 2, 3)]
    flux[n] = flux[n] + p
    return (*cons, *flux, (cons[4] + p) * vel[n], theta, kappa, jnp.abs(vel[n]) + sound)


def double_flux(low, high, n):
    speed = jnp.maximum(low[11], high[11])
    out = []
    for f in range(F):
        k = F + f - 1 if f else n + 1
        out.append((low[k] + high[k]) - speed * (high[f] - low[f]))
    out[4] = out[4] - (low[10] + high[10]) * (high[9] - low[9])
    return out


def primitive(cons):
    rho, mx, my, mz, energy = cons
    inv = inverse(rho)
    u, v, w = mx * inv, my * inv, mz * inv
    return [rho, u, v, w, (GAMMA - 1.0) * (energy - 0.5 * rho * (u * u + v * v + w * w))]


def conserved(prim):
    rho, u, v, w, p = prim
    return [rho, rho * u, rho * v, rho * w, p * (1.0 / (GAMMA - 1.0)) + 0.5 * rho * (u * u + v * v + w * w)]


def at(f, y, group):
    return pl.ds(pl.multiple_of((f * Y + y) * HALF + group * 8, 8), 8)


def wide_at(f, y, group):
    return pl.ds(pl.multiple_of((f * WIDE + DEEP + y) * HALF + group * 8, 8), 8)


def strip_at(f, t, group):
    return pl.ds(pl.multiple_of((f * DEEP + t) * HALF + group * 8, 8), 8)


def x_layer_at(f, group, x):
    return pl.ds(f * Y * HALF + group * 8 + x, Y, HALF)


def transposed(vectors):
    place = lax.broadcasted_iota(jnp.int32, (8, L), 1) // 16
    vectors = list(vectors)
    for bit in (1, 2, 4):
        clear = (place & bit) == 0
        for i in range(8):
            if i & bit:
                continue
            a, b = vectors[i], vectors[i | bit]
            vectors[i] = jnp.where(clear, a, rolled(b, 16 * bit))
            vectors[i | bit] = jnp.where(clear, rolled(a, -16 * bit), b)
    return vectors


def faces(pos, cur, x_in, x_out, y_in, y_out):
    zx, zy, core = tile_x(pos[0]), tile_y(pos[0]), pos[1]
    place = lax.broadcasted_iota(jnp.int32, (8, L), 1) // 16
    first = jnp.full((8, L), zy, jnp.int32) == 0
    turn = jnp.full((8, L), jnp.where(core == zy, 1, 0), jnp.int32) == 1
    far = Y - DEEP
    for f in range(F):
        for t in range(DEEP):
            ahead, back = [], []
            for group in range(3):
                to = pl.ds(((f * 3 + group) * DEEP + t) * 8, 8)
                x_in[to, :] = cur[x_layer_at(f, group, far * (1 - zx) + t), :]
                x_out[to, :] = cur[x_layer_at(f, group, far * zx + t), :]
                y_in[strip_at(f, t, group), :] = cur[at(f, far * (1 - zy) + t, group), :]
                v = cur[at(f, far * zy + t, group), :]
                ahead.append(rolled(v, 16))
                back.append(rolled(v, -16))
            for group in range(3):
                high = jnp.where(place == 0, ahead[group - 1], ahead[group])
                low = jnp.where(place == 7, back[(group + 1) % 3], back[group])
                v = cur[at(f, far * zy + t, group), :]
                y_out[strip_at(f, t, group), :] = jnp.where(turn, jnp.where(first, low, high), v)


def corners(pos, y_in, y_out, to_in, to_out):
    zx, zy = tile_x(pos[0]), tile_y(pos[0])

    def copy(low, high):
        for f in range(F):
            for group in range(3):
                for r in range(2):
                    for out, x in ((to_in, 6 * (1 - zx) + r), (to_out, 6 * zx + r)):
                        row = ((f * 3 + group) * 2 + r) * 4
                        base = f * DEEP * HALF + group * 8 + x
                        out[row : row + 2, :] = low[pl.ds(base + HALF, 2, HALF), :]
                        out[row + 2 : row + 4, :] = high[pl.ds(base, 2, HALF), :]

    @pl.when(zy == 0)
    def _():
        copy(y_out, y_in)

    @pl.when(zy == 1)
    def _():
        copy(y_in, y_out)


def sort_out(kept, given, *refs):
    parts, mine, other = refs[:4], refs[4], refs[5]
    for i in range(4):
        for s in range(CAP):
            tile = parts[i][s]
            mine[kept[i * CAP + s]] = tile
            other[given[i * CAP + s]] = tile


def reorder(pos, mask, mine, other, cur, x_in, x_out, y_in, y_out):
    def convert(group, _):
        here = [jnp.full((X, L), mask[group * 8 + i], jnp.int32) == 1 for i in range(8)]
        for f in range(F):
            vectors = [jnp.where(here[i], mine[group * 8 + i, f], other[group * 8 + i, f]) for i in range(8)]
            for y, v in enumerate(transposed(vectors)):
                cur[at(f, y, group), :] = v
        for y in range(Y):
            prim = [cur[at(f, y, group), :] for f in range(F)]
            for f, v in enumerate(conserved(prim)):
                if f:
                    cur[at(f, y, group), :] = v
        return 0

    lax.fori_loop(0, 3, convert, 0)
    faces(pos, cur, x_in, x_out, y_in, y_out)


def widen(pos, cur, x_in, x_out, y_in, y_out, main, side_rows):
    zx, zy = tile_x(pos[0]), tile_y(pos[0])
    for f in range(F):
        for group in range(3):
            for y in range(Y):
                main[wide_at(f, y, group), :] = cur[at(f, y, group), :]
            for t in range(DEEP):
                main[wide_at(f, Y * (1 - zy) - DEEP * zy + t, group), :] = y_in[strip_at(f, t, group), :]
                main[wide_at(f, Y * zy - DEEP * (1 - zy) + t, group), :] = y_out[strip_at(f, t, group), :]
                at_t = pl.ds(((f * 3 + group) * DEEP + t) * 8, 8)
                base = (f * WIDE + DEEP) * HALF + group * 8 + t
                side_rows[pl.ds(base + 5 * zx, 8, HALF), :] = x_in[at_t, :]
                side_rows[pl.ds(base + 5 * (1 - zx), 8, HALF), :] = x_out[at_t, :]


def add_corners(pos, c_in, c_out, side_rows):
    zx = tile_x(pos[0])
    for f in range(F):
        for group in range(3):
            for r in range(2):
                row = ((f * 3 + group) * 2 + r) * 4
                for c, beyond in ((c_in, 6 * zx), (c_out, 6 * (1 - zx))):
                    for k, y in ((0, -2), (2, Y)):
                        to = (f * WIDE + DEEP + y) * HALF + group * 8 + r + beyond
                        side_rows[pl.ds(to, 2, HALF), :] = c[row + k : row + k + 2, :]


def advance(number, source, initial, target, main_ys, side_ys, made=None):
    weight = (0.0, 0.75, 1.0 / 3.0)[number]

    def step(group, _):
        height = lax.broadcasted_iota(jnp.int32, (8, L), 1) % 16
        sub = lax.broadcasted_iota(jnp.int32, (8, L), 0)
        floor, roof = height == 0, height == 15
        left, right = sub == 0, sub == 7
        cells, fluxes = {}, {}

        def cell(part, y):
            if (part, y) not in cells:
                cons = [source(part, y)[wide_at(f, y, group), :] for f in range(F)]
                cells[part, y] = cons, terms(cons)
            return cells[part, y]

        def flux_y(part, y):
            if (part, y) not in fluxes:
                fluxes[part, y] = double_flux(side(*cell(part, y), 1), side(*cell(part, y + 1), 1), 1)
            return fluxes[part, y]

        for y in sorted({*main_ys, *side_ys}):
            own = [side(*cell(part, y), 0) for part in range(2)]
            turned = [[pltpu.roll(q, 7, 0) for q in o] for o in own]
            flux = []
            for part in range(2):
                ahead = [jnp.where(right, q, p) for p, q in zip(turned[part], turned[1 - part])]
                flux.append(double_flux(own[part], ahead, 0))
            turned = [[pltpu.roll(q, 1, 0) for q in o] for o in flux]
            for part, ys in enumerate((main_ys, side_ys)):
                if y not in ys:
                    continue
                cons, t = cell(part, y)
                change = [
                    v - jnp.where(left, q, p) for v, p, q in zip(flux[part], turned[part], turned[1 - part])
                ]
                change = [c + (b - a) for c, a, b in zip(change, flux_y(part, y - 1), flux_y(part, y))]
                low = side(cons, t, 2)
                up = [rolled(q, -1) for q in cons]
                flux_z = double_flux(low, side(up, terms(up), 2), 2)
                for f in range(F):
                    upper = jnp.where(roof, 2.0 * t[1] if f == 3 else 0.0, flux_z[f])
                    lower = rolled(upper, 1)
                    if f == 3:
                        lower = jnp.where(floor, 2.0 * t[1], lower)
                    change[f] = change[f] + (upper - lower)
                out = [c - (0.5 * STEP) * d for c, d in zip(cons, change)]
                if number:
                    out = [
                        weight * initial(part, y)[wide_at(f, y, group), :] + (1.0 - weight) * o
                        for f, o in enumerate(out)
                    ]
                if number == 2:
                    out = primitive(out)
                for f in range(F):
                    target(part, y)[wide_at(f, y, group), :] = out[f]
        if number == 2:
            for f in range(F):
                vectors = [target(0, y)[wide_at(f, y, group), :] for y in range(Y)]
                for i, v in enumerate(transposed(vectors)):
                    made[group * 8 + i, f] = v
        return 0

    lax.fori_loop(0, 3, step, 0)


EARLY_MAIN = range(0, Y)
EARLY_SIDE = range(1, Y - 1)


def begin(pos, cur, x_in, x_out, y_in, y_out, main, side_rows, first_main, first_side):
    widen(pos, cur, x_in, x_out, y_in, y_out, main, side_rows)
    initial, first = (main, side_rows), (first_main, first_side)
    advance(0, lambda part, y: initial[part], None, lambda part, y: first[part], EARLY_MAIN, EARLY_SIDE)


def finish(pos, main, side_rows, early_main, early_side, c_in, c_out, made, corner_rows, *held):
    late, second = held[0:2], held[2:4]
    add_corners(pos, c_in, c_out, corner_rows)

    def initial(part, y):
        return (side_rows if 0 <= y < Y else corner_rows) if part else main

    def first(part, y):
        if part:
            return early_side if y in EARLY_SIDE else late[1]
        return early_main if y in EARLY_MAIN else late[0]

    advance(0, initial, None, first, (-2, -1, Y, Y + 1), (-1, 0, Y - 1, Y))
    advance(1, first, initial, lambda part, y: second[part], range(-1, Y + 1), range(0, Y))
    advance(2, lambda part, y: second[part], initial, lambda part, y: late[part], range(0, Y), (), made)


def pack_out(pos, final, mine, other, *outs):
    z, core = pos[0], pos[1]
    for k in range(4):
        d = (z ^ k) * 2 + core
        for s in range(OUT):
            j = final[d * 8 + s]
            row = jnp.maximum(j, 0) >> 1
            kind = jnp.full((X, L), jnp.where(j < 0, 2, (j & 1) ^ core), jnp.int32)
            for f in range(F):
                outs[k][s, f] = jnp.where(kind == 0, mine[row, f], jnp.where(kind == 1, other[row, f], 0.0))


def body(block_cells, slot_blocks):
    row, col = lax.axis_index("row"), lax.axis_index("col")
    pos = jnp.stack([row // 2, row % 2, col]).astype(jnp.int32)

    def to(array, route):
        pairs = []
        for r in range(N_ROW):
            for c in range(N_COL):
                z, core, c2 = route(r // 2, r % 2, c)
                pairs.append((r * N_COL + c, (z * 2 + core) * N_COL + c2 % N_COL))
        return lax.ppermute(array, ("row", "col"), pairs)

    def over_z(array, k):
        return array if k == 0 else to(array, lambda z, core, c: (z ^ k, core, c))

    def over_core(array):
        return to(array, lambda z, core, c: (z, 1 - core, c))

    tiles = [shape(CAP, F, X, L)] * 4
    parts = pl.pallas_call(
        pack_in,
        out_shape=tiles,
        in_specs=[SMEM, VMEM],
        out_specs=[VMEM] * 4,
        compiler_params=PARAMS,
        name="pack_in",
    )(pos, block_cells)
    index = jax.ShapeDtypeStruct((5 * CAP,), jnp.int32)
    final, kept, given, mask, own = pl.pallas_call(
        table,
        out_shape=[
            jax.ShapeDtypeStruct((N_ROW * 8,), jnp.int32),
            index,
            index,
            jax.ShapeDtypeStruct((HALF + 1,), jnp.int32),
            tiles[0],
        ],
        in_specs=[SMEM, SMEM, ANY],
        out_specs=[SMEM] * 4 + [ANY],
        input_output_aliases={2: 4},
        scratch_shapes=[pltpu.SMEM((N_ROW * 16,), jnp.int32), pltpu.SMEM((N_ROW,), jnp.int32)],
        compiler_params=PARAMS,
        cost_estimate=pl.CostEstimate(flops=0, bytes_accessed=20_000_000, transcendentals=0),
        name="table",
    )(pos, slot_blocks, parts[0])
    gathered = [over_z(parts[k], k) if k else own for k in range(4)]
    mine, other = pl.pallas_call(
        sort_out,
        out_shape=[shape(HALF + 1, F, X, L)] * 2,
        in_specs=[SMEM, SMEM] + [VMEM] * 4,
        out_specs=[VMEM] * 2,
        compiler_params=PARAMS,
        name="sort_out",
    )(kept, given, *gathered)

    whole = shape(F * Y * HALF, L)
    layer = shape(F * DEEP * HALF, L)
    initial, x_in, x_out, y_in, y_out = pl.pallas_call(
        reorder,
        out_shape=[whole] + [layer] * 4,
        in_specs=[SMEM, SMEM, VMEM, VMEM],
        out_specs=[VMEM] * 5,
        compiler_params=PARAMS,
        name="reorder",
    )(pos, mask, mine, over_core(other))

    def x_partner(z):
        return z ^ 1

    def y_partner(z):
        return z ^ 3

    def over_x(inner, outer):
        return (
            to(inner, lambda z, core, c: (x_partner(z), core, c)),
            to(outer, lambda z, core, c: (x_partner(z), core, c + 2 * tile_x(z) - 1)),
        )

    def over_y(inner, outer):
        return (
            to(inner, lambda z, core, c: (y_partner(z), core, c)),
            to(outer, lambda z, core, c: (y_partner(z), 1 - core, c + 2 * tile_y(z) - 1)),
        )

    y_layers = over_y(y_in, y_out)
    x_layers = over_x(x_in, x_out)
    corner_cells = pl.pallas_call(
        corners,
        out_shape=[shape(F * 3 * 8, L)] * 2,
        in_specs=[SMEM, VMEM, VMEM],
        out_specs=[VMEM] * 2,
        compiler_params=PARAMS,
        name="corners",
    )(pos, *y_layers)
    corner_cells = over_x(*corner_cells)
    wide = [F * WIDE * HALF, L]
    early = pl.pallas_call(
        begin,
        out_shape=[shape(*wide)] * 4,
        in_specs=[SMEM] + [VMEM] * 5,
        out_specs=[VMEM] * 4,
        compiler_params=PARAMS,
        cost_estimate=pl.CostEstimate(flops=0, bytes_accessed=10_000_000, transcendentals=0),
        name="begin",
    )(pos, initial, *x_layers, *y_layers)
    current = pl.pallas_call(
        finish,
        out_shape=shape(HALF, F, X, L),
        in_specs=[SMEM] + [VMEM] * 6,
        out_specs=VMEM,
        scratch_shapes=[pltpu.VMEM(wide, jnp.float32)] * 5,
        compiler_params=PARAMS,
        name="finish",
    )(pos, *early, *corner_cells)

    leaving = pl.pallas_call(
        pack_out,
        out_shape=[shape(OUT, F, X, L)] * 4,
        in_specs=[SMEM, SMEM, VMEM, VMEM],
        out_specs=[VMEM] * 4,
        compiler_params=PARAMS,
        name="pack_out",
    )(pos, final, current, over_core(current))
    arrived = [over_z(leaving[k], k) for k in range(4)]
    result = []
    for which in ((0, 1, 3), (2,)):
        n = len(which)
        result = [
            pl.pallas_call(
                lambda *refs, which=which: unpack_out(which, *refs),
                out_shape=shape(OUT, F, 2 * X, 2 * L),
                in_specs=[SMEM] + [ANY] * (n + len(result)),
                out_specs=ANY,
                input_output_aliases={n + 1: 0} if result else {},
                scratch_shapes=[pltpu.SemaphoreType.DMA((n,))],
                compiler_params=PARAMS,
                name="unpack_out",
            )(pos, *[arrived[k] for k in which], *result)
        ]
    return result[0]


def solution(mesh):
    in_specs = (P(("row", "col"), None, None, None), P())
    out_specs = P(("row", "col"), None, None, None)
    return jax.shard_map(body, mesh=mesh, in_specs=in_specs, out_specs=out_specs, check_vma=False)
```

```python
import math

import jax
import jax.numpy as jnp
from jax import lax
from jax.experimental import pallas as pl
from jax.experimental.pallas import tpu as pltpu
from jax.sharding import PartitionSpec as P

CAP = 11
OUT = 7
NBY = 48
N_ROW = 8
N_COL = 16
HALF = NBY // 2
F = 5
X = Y = 8
L = 128
DEEP = 3
WIDE = Y + 2 * DEEP

GAMMA = 1.4
STEP = 0.12
LOG2_E = 1.0 / math.log(2.0)

VMEM = pl.BlockSpec(memory_space=pltpu.VMEM)
SMEM = pl.BlockSpec(memory_space=pltpu.SMEM)
ANY = pl.BlockSpec(memory_space=pl.ANY)
PARAMS = pltpu.CompilerParams(vmem_limit_bytes=48 * 1024 * 1024)


def shape(*dims):
    return jax.ShapeDtypeStruct(dims, jnp.float32)


def tile_x(z):
    return ((z + 1) // 2) % 2


def tile_y(z):
    return z // 2


def pack_in(pos, cells, *outs):
    z = pos[0]
    for k in range(4):
        x = pl.ds(pl.multiple_of(tile_x(z ^ k) * X, X), X)
        y = pl.ds(pl.multiple_of(tile_y(z ^ k) * L, L), L)
        for s in range(CAP):
            for f in range(F):
                outs[k][s, f] = cells[s, f, x, y]


def unpack_out(which, pos, *refs):
    out, sems = refs[-2:]
    z = pos[0]
    copies = []
    for i, k in enumerate(which):
        x = pl.ds(pl.multiple_of(tile_x(z ^ k) * X, X), X)
        y = pl.ds(pl.multiple_of(tile_y(z ^ k) * L, L), L)
        copies.append(pltpu.make_async_copy(refs[i], out.at[:, :, x, y], sems.at[i]))
    for c in copies:
        c.start()
    for c in copies:
        c.wait()


def table(pos, slots, _tile, final, rows, _same, held, count):
    z, core, g = pos[0], pos[1], pos[2]
    for d in range(N_ROW):
        n = jnp.int32(0)
        place = ((z ^ d // 2) * 2 + (core ^ d % 2)) * CAP
        for s in range(CAP):
            b = slots[d * N_COL + g, s]
            j = b - g * NBY
            held[d * 16 + s] = j
            here = jnp.logical_and(b >= 0, (j & 1) == core)
            rows[place + s] = jnp.where(here, j >> 1, HALF)
            n = n + jnp.where(b >= 0, 1, 0)
        count[d] = n
    for bit in range(3):
        for low in range(N_ROW):
            if low >> bit & 1:
                continue
            high = low | 1 << bit
            a, b = count[low], count[high]
            up = a > b
            src = jnp.where(up, low, high)
            dst = jnp.where(up, high, low)
            n_src = jnp.maximum(a, b)
            n_dst = jnp.minimum(a, b)
            moved = (n_src - n_dst) // 2

            def move(i, _, src=src, dst=dst, n_src=n_src, n_dst=n_dst, moved=moved):
                held[dst * 16 + n_dst + i] = held[src * 16 + n_src - moved + i]
                return 0

            lax.fori_loop(0, moved, move, 0)
            count[src] = n_src - moved
            count[dst] = n_dst + moved
    for d in range(N_ROW):
        n = count[d]
        for s in range(8):
            final[d * 8 + s] = jnp.where(s < n, held[d * 16 + s], -1)


def rolled(v, shift):
    shift %= L
    return v if shift == 0 else pltpu.roll(v, shift, 1)


def inverse(rho):
    guess = pl.reciprocal(rho, approx=True)
    return guess * (2.0 - rho * guess)


def terms(cons):
    rho, mx, my, mz, energy = cons
    inv = inverse(rho)
    u, v, w = mx * inv, my * inv, mz * inv
    p = (GAMMA - 1.0) * energy - (0.5 * (GAMMA - 1.0)) * (mx * u + my * v + mz * w)
    theta = p * inv
    power = jnp.log(theta)
    sound = jnp.exp2(power * (0.5 * LOG2_E) + 0.5 * math.log2(GAMMA))
    kappa = jnp.exp2(power * (0.7 * LOG2_E) + math.log2(0.2))
    return (u, v, w), p, theta, sound, kappa


def side(cons, t, n):
    vel, p, theta, sound, kappa = t
    flux = [cons[f] * vel[n] for f in (1, 2, 3)]
    flux[n] = flux[n] + p
    return (*cons, *flux, (cons[4] + p) * vel[n], theta, kappa, jnp.abs(vel[n]) + sound)


def double_flux(low, high, n):
    speed = jnp.maximum(low[11], high[11])
    out = []
    for f in range(F):
        k = F + f - 1 if f else n + 1
        out.append((low[k] + high[k]) - speed * (high[f] - low[f]))
    out[4] = out[4] - (low[10] + high[10]) * (high[9] - low[9])
    return out


def primitive(cons):
    rho, mx, my, mz, energy = cons
    inv = inverse(rho)
    u, v, w = mx * inv, my * inv, mz * inv
    return [rho, u, v, w, (GAMMA - 1.0) * (energy - 0.5 * rho * (u * u + v * v + w * w))]


def conserved(prim):
    rho, u, v, w, p = prim
    return [rho, rho * u, rho * v, rho * w, p * (1.0 / (GAMMA - 1.0)) + 0.5 * rho * (u * u + v * v + w * w)]


def at(f, y, group):
    return pl.ds(pl.multiple_of((f * Y + y) * HALF + group * 8, 8), 8)


def wide_at(f, y, group):
    return pl.ds(pl.multiple_of((f * WIDE + DEEP + y) * HALF + group * 8, 8), 8)


def strip_at(f, t, group):
    return pl.ds(pl.multiple_of((f * DEEP + t) * HALF + group * 8, 8), 8)


def x_layer_at(f, group, x):
    return pl.ds(f * Y * HALF + group * 8 + x, Y, HALF)


def transposed(vectors):
    place = lax.broadcasted_iota(jnp.int32, (8, L), 1) // 16
    vectors = list(vectors)
    for bit in (1, 2, 4):
        clear = (place & bit) == 0
        for i in range(8):
            if i & bit:
                continue
            a, b = vectors[i], vectors[i | bit]
            vectors[i] = jnp.where(clear, a, rolled(b, 16 * bit))
            vectors[i | bit] = jnp.where(clear, rolled(a, -16 * bit), b)
    return vectors


def faces(pos, cur, x_in, x_out, y_in, y_out):
    zx, zy, core = tile_x(pos[0]), tile_y(pos[0]), pos[1]
    place = lax.broadcasted_iota(jnp.int32, (8, L), 1) // 16
    first = jnp.full((8, L), zy, jnp.int32) == 0
    turn = jnp.full((8, L), jnp.where(core == zy, 1, 0), jnp.int32) == 1
    far = Y - DEEP
    for f in range(F):
        for t in range(DEEP):
            ahead, back = [], []
            for group in range(3):
                to = pl.ds(((f * 3 + group) * DEEP + t) * 8, 8)
                x_in[to, :] = cur[x_layer_at(f, group, far * (1 - zx) + t), :]
                x_out[to, :] = cur[x_layer_at(f, group, far * zx + t), :]
                y_in[strip_at(f, t, group), :] = cur[at(f, far * (1 - zy) + t, group), :]
                v = cur[at(f, far * zy + t, group), :]
                ahead.append(rolled(v, 16))
                back.append(rolled(v, -16))
            for group in range(3):
                high = jnp.where(place == 0, ahead[group - 1], ahead[group])
                low = jnp.where(place == 7, back[(group + 1) % 3], back[group])
                v = cur[at(f, far * zy + t, group), :]
                y_out[strip_at(f, t, group), :] = jnp.where(turn, jnp.where(first, low, high), v)


def corners(pos, y_in, y_out, to_in, to_out):
    zx, zy = tile_x(pos[0]), tile_y(pos[0])

    def copy(low, high):
        for f in range(F):
            for group in range(3):
                for r in range(2):
                    for out, x in ((to_in, 6 * (1 - zx) + r), (to_out, 6 * zx + r)):
                        row = ((f * 3 + group) * 2 + r) * 4
                        base = f * DEEP * HALF + group * 8 + x
                        out[row : row + 2, :] = low[pl.ds(base + HALF, 2, HALF), :]
                        out[row + 2 : row + 4, :] = high[pl.ds(base, 2, HALF), :]

    @pl.when(zy == 0)
    def _():
        copy(y_out, y_in)

    @pl.when(zy == 1)
    def _():
        copy(y_in, y_out)


def reorder(pos, rows, *refs):
    parts = refs[:8]
    cur, x_in, x_out, y_in, y_out = refs[8:13]
    held = refs[13]
    for i in range(8):
        for s in range(CAP):
            held[rows[i * CAP + s]] = parts[i][s]

    def convert(group, _):
        for f in range(F):
            vectors = [held[group * 8 + i, f] for i in range(8)]
            for y, v in enumerate(transposed(vectors)):
                cur[at(f, y, group), :] = v
        for y in range(Y):
            prim = [cur[at(f, y, group), :] for f in range(F)]
            for f, v in enumerate(conserved(prim)):
                if f:
                    cur[at(f, y, group), :] = v
        return 0

    lax.fori_loop(0, 3, convert, 0)
    faces(pos, cur, x_in, x_out, y_in, y_out)


def widen(pos, cur, x_in, x_out, y_in, y_out, main, side_rows):
    zx, zy = tile_x(pos[0]), tile_y(pos[0])
    for f in range(F):
        for group in range(3):
            for y in range(Y):
                main[wide_at(f, y, group), :] = cur[at(f, y, group), :]
            for t in range(DEEP):
                main[wide_at(f, Y * (1 - zy) - DEEP * zy + t, group), :] = y_in[strip_at(f, t, group), :]
                main[wide_at(f, Y * zy - DEEP * (1 - zy) + t, group), :] = y_out[strip_at(f, t, group), :]
                at_t = pl.ds(((f * 3 + group) * DEEP + t) * 8, 8)
                base = (f * WIDE + DEEP) * HALF + group * 8 + t
                side_rows[pl.ds(base + 5 * zx, 8, HALF), :] = x_in[at_t, :]
                side_rows[pl.ds(base + 5 * (1 - zx), 8, HALF), :] = x_out[at_t, :]


def add_corners(pos, c_in, c_out, side_rows):
    zx = tile_x(pos[0])
    for f in range(F):
        for group in range(3):
            for r in range(2):
                row = ((f * 3 + group) * 2 + r) * 4
                for c, beyond in ((c_in, 6 * zx), (c_out, 6 * (1 - zx))):
                    for k, y in ((0, -2), (2, Y)):
                        to = (f * WIDE + DEEP + y) * HALF + group * 8 + r + beyond
                        side_rows[pl.ds(to, 2, HALF), :] = c[row + k : row + k + 2, :]


def advance(number, source, initial, target, main_ys, side_ys, made=None):
    weight = (0.0, 0.75, 1.0 / 3.0)[number]

    def step(group, _):
        height = lax.broadcasted_iota(jnp.int32, (8, L), 1) % 16
        sub = lax.broadcasted_iota(jnp.int32, (8, L), 0)
        floor, roof = height == 0, height == 15
        left, right = sub == 0, sub == 7
        cells, fluxes = {}, {}

        def cell(part, y):
            if (part, y) not in cells:
                cons = [source(part, y)[wide_at(f, y, group), :] for f in range(F)]
                cells[part, y] = cons, terms(cons)
            return cells[part, y]

        def flux_y(part, y):
            if (part, y) not in fluxes:
                fluxes[part, y] = double_flux(side(*cell(part, y), 1), side(*cell(part, y + 1), 1), 1)
            return fluxes[part, y]

        for y in sorted({*main_ys, *side_ys}):
            own = [side(*cell(part, y), 0) for part in range(2)]
            turned = [[pltpu.roll(q, 7, 0) for q in o] for o in own]
            flux = []
            for part in range(2):
                ahead = [jnp.where(right, q, p) for p, q in zip(turned[part], turned[1 - part])]
                flux.append(double_flux(own[part], ahead, 0))
            turned = [[pltpu.roll(q, 1, 0) for q in o] for o in flux]
            for part, ys in enumerate((main_ys, side_ys)):
                if y not in ys:
                    continue
                cons, t = cell(part, y)
                change = [
                    v - jnp.where(left, q, p) for v, p, q in zip(flux[part], turned[part], turned[1 - part])
                ]
                change = [c + (b - a) for c, a, b in zip(change, flux_y(part, y - 1), flux_y(part, y))]
                low = side(cons, t, 2)
                up = [rolled(q, -1) for q in cons]
                flux_z = double_flux(low, side(up, terms(up), 2), 2)
                for f in range(F):
                    upper = jnp.where(roof, 2.0 * t[1] if f == 3 else 0.0, flux_z[f])
                    lower = rolled(upper, 1)
                    if f == 3:
                        lower = jnp.where(floor, 2.0 * t[1], lower)
                    change[f] = change[f] + (upper - lower)
                out = [c - (0.5 * STEP) * d for c, d in zip(cons, change)]
                if number:
                    out = [
                        weight * initial(part, y)[wide_at(f, y, group), :] + (1.0 - weight) * o
                        for f, o in enumerate(out)
                    ]
                if number == 2:
                    out = primitive(out)
                for f in range(F):
                    target(part, y)[wide_at(f, y, group), :] = out[f]
        if number == 2:
            for f in range(F):
                vectors = [target(0, y)[wide_at(f, y, group), :] for y in range(Y)]
                for i, v in enumerate(transposed(vectors)):
                    made[group * 8 + i, f] = v
        return 0

    lax.fori_loop(0, 3, step, 0)


EARLY_MAIN = range(0, Y)
EARLY_SIDE = range(1, Y - 1)


def begin(pos, cur, x_in, x_out, y_in, y_out, main, side_rows, first_main, first_side):
    widen(pos, cur, x_in, x_out, y_in, y_out, main, side_rows)
    initial, first = (main, side_rows), (first_main, first_side)
    advance(0, lambda part, y: initial[part], None, lambda part, y: first[part], EARLY_MAIN, EARLY_SIDE)


def finish(pos, main, side_rows, early_main, early_side, c_in, c_out, made, corner_rows, *held):
    late, second = held[0:2], held[2:4]
    add_corners(pos, c_in, c_out, corner_rows)

    def initial(part, y):
        return (side_rows if 0 <= y < Y else corner_rows) if part else main

    def first(part, y):
        if part:
            return early_side if y in EARLY_SIDE else late[1]
        return early_main if y in EARLY_MAIN else late[0]

    advance(0, initial, None, first, (-2, -1, Y, Y + 1), (-1, 0, Y - 1, Y))
    advance(1, first, initial, lambda part, y: second[part], range(-1, Y + 1), range(0, Y))
    advance(2, lambda part, y: second[part], initial, lambda part, y: late[part], range(0, Y), (), made)


def pack_out(pos, final, mine, other, *outs):
    z, core = pos[0], pos[1]
    for k in range(4):
        d = (z ^ k) * 2 + core
        for s in range(OUT):
            j = final[d * 8 + s]
            row = jnp.maximum(j, 0) >> 1
            kind = jnp.full((X, L), jnp.where(j < 0, 2, (j & 1) ^ core), jnp.int32)
            for f in range(F):
                outs[k][s, f] = jnp.where(kind == 0, mine[row, f], jnp.where(kind == 1, other[row, f], 0.0))


def body(block_cells, slot_blocks):
    row, col = lax.axis_index("row"), lax.axis_index("col")
    pos = jnp.stack([row // 2, row % 2, col]).astype(jnp.int32)

    def to(array, route):
        pairs = []
        for r in range(N_ROW):
            for c in range(N_COL):
                z, core, c2 = route(r // 2, r % 2, c)
                pairs.append((r * N_COL + c, (z * 2 + core) * N_COL + c2 % N_COL))
        return lax.ppermute(array, ("row", "col"), pairs)

    def over_z(array, k):
        return array if k == 0 else to(array, lambda z, core, c: (z ^ k, core, c))

    def over_core(array):
        return to(array, lambda z, core, c: (z, 1 - core, c))

    tiles = [shape(CAP, F, X, L)] * 4
    parts = pl.pallas_call(
        pack_in,
        out_shape=tiles,
        in_specs=[SMEM, VMEM],
        out_specs=[VMEM] * 4,
        compiler_params=PARAMS,
        name="pack_in",
    )(pos, block_cells)
    final, rows, own = pl.pallas_call(
        table,
        out_shape=[
            jax.ShapeDtypeStruct((N_ROW * 8,), jnp.int32),
            jax.ShapeDtypeStruct((N_ROW * CAP,), jnp.int32),
            tiles[0],
        ],
        in_specs=[SMEM, SMEM, ANY],
        out_specs=[SMEM, SMEM, ANY],
        input_output_aliases={2: 2},
        scratch_shapes=[pltpu.SMEM((N_ROW * 16,), jnp.int32), pltpu.SMEM((N_ROW,), jnp.int32)],
        compiler_params=PARAMS,
        cost_estimate=pl.CostEstimate(flops=0, bytes_accessed=20_000_000, transcendentals=0),
        name="table",
    )(pos, slot_blocks, parts[0])
    gathered = []
    for k in range(4):
        here = over_z(parts[k], k) if k else own
        gathered += [here, over_core(here)]

    whole = shape(F * Y * HALF, L)
    layer = shape(F * DEEP * HALF, L)
    initial, x_in, x_out, y_in, y_out = pl.pallas_call(
        reorder,
        out_shape=[whole] + [layer] * 4,
        in_specs=[SMEM, SMEM] + [VMEM] * 8,
        out_specs=[VMEM] * 5,
        scratch_shapes=[pltpu.VMEM((HALF + 1, F, X, L), jnp.float32)],
        compiler_params=PARAMS,
        name="reorder",
    )(pos, rows, *gathered)

    def x_partner(z):
        return z ^ 1

    def y_partner(z):
        return z ^ 3

    def over_x(inner, outer):
        return (
            to(inner, lambda z, core, c: (x_partner(z), core, c)),
            to(outer, lambda z, core, c: (x_partner(z), core, c + 2 * tile_x(z) - 1)),
        )

    def over_y(inner, outer):
        return (
            to(inner, lambda z, core, c: (y_partner(z), core, c)),
            to(outer, lambda z, core, c: (y_partner(z), 1 - core, c + 2 * tile_y(z) - 1)),
        )

    y_layers = over_y(y_in, y_out)
    x_layers = over_x(x_in, x_out)
    corner_cells = pl.pallas_call(
        corners,
        out_shape=[shape(F * 3 * 8, L)] * 2,
        in_specs=[SMEM, VMEM, VMEM],
        out_specs=[VMEM] * 2,
        compiler_params=PARAMS,
        name="corners",
    )(pos, *y_layers)
    corner_cells = over_x(*corner_cells)
    wide = [F * WIDE * HALF, L]
    early = pl.pallas_call(
        begin,
        out_shape=[shape(*wide)] * 4,
        in_specs=[SMEM] + [VMEM] * 5,
        out_specs=[VMEM] * 4,
        compiler_params=PARAMS,
        cost_estimate=pl.CostEstimate(flops=0, bytes_accessed=10_000_000, transcendentals=0),
        name="begin",
    )(pos, initial, *x_layers, *y_layers)
    current = pl.pallas_call(
        finish,
        out_shape=shape(HALF, F, X, L),
        in_specs=[SMEM] + [VMEM] * 6,
        out_specs=VMEM,
        scratch_shapes=[pltpu.VMEM(wide, jnp.float32)] * 5,
        compiler_params=PARAMS,
        name="finish",
    )(pos, *early, *corner_cells)

    leaving = pl.pallas_call(
        pack_out,
        out_shape=[shape(OUT, F, X, L)] * 4,
        in_specs=[SMEM, SMEM, VMEM, VMEM],
        out_specs=[VMEM] * 4,
        compiler_params=PARAMS,
        name="pack_out",
    )(pos, final, current, over_core(current))
    arrived = [over_z(leaving[k], k) for k in range(4)]
    result = []
    for which in ((0, 1, 3), (2,)):
        n = len(which)
        result = [
            pl.pallas_call(
                lambda *refs, which=which: unpack_out(which, *refs),
                out_shape=shape(OUT, F, 2 * X, 2 * L),
                in_specs=[SMEM] + [ANY] * (n + len(result)),
                out_specs=ANY,
                input_output_aliases={n + 1: 0} if result else {},
                scratch_shapes=[pltpu.SemaphoreType.DMA((n,))],
                compiler_params=PARAMS,
                name="unpack_out",
            )(pos, *[arrived[k] for k in which], *result)
        ]
    return result[0]


def solution(mesh):
    in_specs = (P(("row", "col"), None, None, None), P())
    out_specs = P(("row", "col"), None, None, None)
    return jax.shard_map(body, mesh=mesh, in_specs=in_specs, out_specs=out_specs, check_vma=False)
```

```python
import math

import jax
import jax.numpy as jnp
from jax import lax
from jax.experimental import pallas as pl
from jax.experimental.pallas import tpu as pltpu
from jax.sharding import PartitionSpec as P

CAP = 11
OUT = 7
NBY = 48
N_ROW = 8
N_COL = 16
HALF = NBY // 2
F = 5
X = Y = 8
L = 128
DEEP = 3
WIDE = Y + 2 * DEEP

GAMMA = 1.4
STEP = 0.12
LOG2_E = 1.0 / math.log(2.0)

VMEM = pl.BlockSpec(memory_space=pltpu.VMEM)
SMEM = pl.BlockSpec(memory_space=pltpu.SMEM)
ANY = pl.BlockSpec(memory_space=pl.ANY)
PARAMS = pltpu.CompilerParams(vmem_limit_bytes=48 * 1024 * 1024)


def shape(*dims):
    return jax.ShapeDtypeStruct(dims, jnp.float32)


def tile_x(z):
    return ((z + 1) // 2) % 2


def tile_y(z):
    return z // 2


def pack_in(pos, cells, *outs):
    z = pos[0]
    for k in range(4):
        x = pl.ds(pl.multiple_of(tile_x(z ^ k) * X, X), X)
        y = pl.ds(pl.multiple_of(tile_y(z ^ k) * L, L), L)
        for s in range(CAP):
            for f in range(F):
                outs[k][s, f] = cells[s, f, x, y]


def unpack_out(which, pos, *refs):
    out, sems = refs[-2:]
    z = pos[0]
    copies = []
    for i, k in enumerate(which):
        x = pl.ds(pl.multiple_of(tile_x(z ^ k) * X, X), X)
        y = pl.ds(pl.multiple_of(tile_y(z ^ k) * L, L), L)
        copies.append(pltpu.make_async_copy(refs[i], out.at[:, :, x, y], sems.at[i]))
    for c in copies:
        c.start()
    for c in copies:
        c.wait()


def table(pos, slots, _tile, final, rows, _same, held, count):
    z, core, g = pos[0], pos[1], pos[2]
    for d in range(N_ROW):
        n = jnp.int32(0)
        place = ((z ^ d // 2) * 2 + (core ^ d % 2)) * CAP
        for s in range(CAP):
            b = slots[d * N_COL + g, s]
            j = b - g * NBY
            held[d * 16 + s] = j
            here = jnp.logical_and(b >= 0, (j & 1) == core)
            rows[place + s] = jnp.where(here, j >> 1, HALF)
            n = n + jnp.where(b >= 0, 1, 0)
        count[d] = n
    for bit in range(3):
        for low in range(N_ROW):
            if low >> bit & 1:
                continue
            high = low | 1 << bit
            a, b = count[low], count[high]
            up = a > b
            src = jnp.where(up, low, high)
            dst = jnp.where(up, high, low)
            n_src = jnp.maximum(a, b)
            n_dst = jnp.minimum(a, b)
            moved = (n_src - n_dst) // 2

            def move(i, _, src=src, dst=dst, n_src=n_src, n_dst=n_dst, moved=moved):
                held[dst * 16 + n_dst + i] = held[src * 16 + n_src - moved + i]
                return 0

            lax.fori_loop(0, moved, move, 0)
            count[src] = n_src - moved
            count[dst] = n_dst + moved
    for d in range(N_ROW):
        n = count[d]
        for s in range(8):
            final[d * 8 + s] = jnp.where(s < n, held[d * 16 + s], -1)


def rolled(v, shift):
    shift %= L
    return v if shift == 0 else pltpu.roll(v, shift, 1)


def inverse(rho):
    guess = pl.reciprocal(rho, approx=True)
    return guess * (2.0 - rho * guess)


def terms(cons):
    rho, mx, my, mz, energy = cons
    inv = inverse(rho)
    u, v, w = mx * inv, my * inv, mz * inv
    p = (GAMMA - 1.0) * energy - (0.5 * (GAMMA - 1.0)) * (mx * u + my * v + mz * w)
    theta = p * inv
    power = jnp.log(theta)
    sound = jnp.exp2(power * (0.5 * LOG2_E) + 0.5 * math.log2(GAMMA))
    kappa = jnp.exp2(power * (0.7 * LOG2_E) + math.log2(0.2))
    return (u, v, w), p, theta, sound, kappa


def side(cons, t, n):
    vel, p, theta, sound, kappa = t
    flux = [cons[f] * vel[n] for f in (1, 2, 3)]
    flux[n] = flux[n] + p
    return (*cons, *flux, (cons[4] + p) * vel[n], theta, kappa, jnp.abs(vel[n]) + sound)


def double_flux(low, high, n):
    speed = jnp.maximum(low[11], high[11])
    out = []
    for f in range(F):
        k = F + f - 1 if f else n + 1
        out.append((low[k] + high[k]) - speed * (high[f] - low[f]))
    out[4] = out[4] - (low[10] + high[10]) * (high[9] - low[9])
    return out


def primitive(cons):
    rho, mx, my, mz, energy = cons
    inv = inverse(rho)
    u, v, w = mx * inv, my * inv, mz * inv
    return [rho, u, v, w, (GAMMA - 1.0) * (energy - 0.5 * rho * (u * u + v * v + w * w))]


def conserved(prim):
    rho, u, v, w, p = prim
    return [rho, rho * u, rho * v, rho * w, p * (1.0 / (GAMMA - 1.0)) + 0.5 * rho * (u * u + v * v + w * w)]


def at(f, y, group):
    return pl.ds(pl.multiple_of((f * Y + y) * HALF + group * 8, 8), 8)


def wide_at(f, y, group):
    return pl.ds(pl.multiple_of((f * WIDE + DEEP + y) * HALF + group * 8, 8), 8)


def strip_at(f, t, group):
    return pl.ds(pl.multiple_of((f * DEEP + t) * HALF + group * 8, 8), 8)


def x_layer_at(f, group, x):
    return pl.ds(f * Y * HALF + group * 8 + x, Y, HALF)


def transposed(vectors):
    place = lax.broadcasted_iota(jnp.int32, (8, L), 1) // 16
    vectors = list(vectors)
    for bit in (1, 2, 4):
        clear = (place & bit) == 0
        for i in range(8):
            if i & bit:
                continue
            a, b = vectors[i], vectors[i | bit]
            vectors[i] = jnp.where(clear, a, rolled(b, 16 * bit))
            vectors[i | bit] = jnp.where(clear, rolled(a, -16 * bit), b)
    return vectors


def faces(pos, cur, x_in, x_out, y_in, y_out):
    zx, zy, core = tile_x(pos[0]), tile_y(pos[0]), pos[1]
    place = lax.broadcasted_iota(jnp.int32, (8, L), 1) // 16
    first = jnp.full((8, L), zy, jnp.int32) == 0
    turn = jnp.full((8, L), jnp.where(core == zy, 1, 0), jnp.int32) == 1
    far = Y - DEEP
    for f in range(F):
        for t in range(DEEP):
            ahead, back = [], []
            for group in range(3):
                to = pl.ds(((f * 3 + group) * DEEP + t) * 8, 8)
                x_in[to, :] = cur[x_layer_at(f, group, far * (1 - zx) + t), :]
                x_out[to, :] = cur[x_layer_at(f, group, far * zx + t), :]
                y_in[strip_at(f, t, group), :] = cur[at(f, far * (1 - zy) + t, group), :]
                v = cur[at(f, far * zy + t, group), :]
                ahead.append(rolled(v, 16))
                back.append(rolled(v, -16))
            for group in range(3):
                high = jnp.where(place == 0, ahead[group - 1], ahead[group])
                low = jnp.where(place == 7, back[(group + 1) % 3], back[group])
                v = cur[at(f, far * zy + t, group), :]
                y_out[strip_at(f, t, group), :] = jnp.where(turn, jnp.where(first, low, high), v)


def corners(pos, y_out, y_in, to_in, to_out):
    zx, zy = tile_x(pos[0]), tile_y(pos[0])

    def copy(low, high):
        for f in range(F):
            for group in range(3):
                for r in range(2):
                    for out, x in ((to_in, 6 * (1 - zx) + r), (to_out, 6 * zx + r)):
                        row = ((f * 3 + group) * 2 + r) * 4
                        base = f * DEEP * HALF + group * 8 + x
                        out[row : row + 2, :] = low[pl.ds(base + HALF, 2, HALF), :]
                        out[row + 2 : row + 4, :] = high[pl.ds(base, 2, HALF), :]

    @pl.when(zy == 0)
    def _():
        copy(y_out, y_in)

    @pl.when(zy == 1)
    def _():
        copy(y_in, y_out)


def reorder(pos, rows, *refs):
    parts = refs[:8]
    cur, x_in, x_out, y_in, y_out = refs[8:13]
    held = refs[13]
    for i in range(8):
        for s in range(CAP):
            held[rows[i * CAP + s]] = parts[i][s]

    def convert(group, _):
        for f in range(F):
            vectors = [held[group * 8 + i, f] for i in range(8)]
            for y, v in enumerate(transposed(vectors)):
                cur[at(f, y, group), :] = v
        for y in range(Y):
            prim = [cur[at(f, y, group), :] for f in range(F)]
            for f, v in enumerate(conserved(prim)):
                if f:
                    cur[at(f, y, group), :] = v
        return 0

    lax.fori_loop(0, 3, convert, 0)
    faces(pos, cur, x_in, x_out, y_in, y_out)


def widen(pos, cur, x_in, x_out, y_in, y_out, main, side_rows):
    zx, zy = tile_x(pos[0]), tile_y(pos[0])
    for f in range(F):
        for group in range(3):
            for y in range(Y):
                main[wide_at(f, y, group), :] = cur[at(f, y, group), :]
            for t in range(DEEP):
                main[wide_at(f, Y * (1 - zy) - DEEP * zy + t, group), :] = y_in[strip_at(f, t, group), :]
                main[wide_at(f, Y * zy - DEEP * (1 - zy) + t, group), :] = y_out[strip_at(f, t, group), :]
                at_t = pl.ds(((f * 3 + group) * DEEP + t) * 8, 8)
                base = (f * WIDE + DEEP) * HALF + group * 8 + t
                side_rows[pl.ds(base + 5 * zx, 8, HALF), :] = x_in[at_t, :]
                side_rows[pl.ds(base + 5 * (1 - zx), 8, HALF), :] = x_out[at_t, :]


def add_corners(pos, c_in, c_out, side_rows):
    zx = tile_x(pos[0])
    for f in range(F):
        for group in range(3):
            for r in range(2):
                row = ((f * 3 + group) * 2 + r) * 4
                for c, beyond in ((c_in, 6 * zx), (c_out, 6 * (1 - zx))):
                    for k, y in ((0, -2), (2, Y)):
                        to = (f * WIDE + DEEP + y) * HALF + group * 8 + r + beyond
                        side_rows[pl.ds(to, 2, HALF), :] = c[row + k : row + k + 2, :]


def advance(number, source, initial, target, main_ys, side_ys, made=None):
    weight = (0.0, 0.75, 1.0 / 3.0)[number]

    def step(group, _):
        height = lax.broadcasted_iota(jnp.int32, (8, L), 1) % 16
        sub = lax.broadcasted_iota(jnp.int32, (8, L), 0)
        floor, roof = height == 0, height == 15
        left, right = sub == 0, sub == 7
        cells, fluxes = {}, {}

        def cell(part, y):
            if (part, y) not in cells:
                cons = [source(part, y)[wide_at(f, y, group), :] for f in range(F)]
                cells[part, y] = cons, terms(cons)
            return cells[part, y]

        def flux_y(part, y):
            if (part, y) not in fluxes:
                fluxes[part, y] = double_flux(side(*cell(part, y), 1), side(*cell(part, y + 1), 1), 1)
            return fluxes[part, y]

        for y in sorted({*main_ys, *side_ys}):
            own = [side(*cell(part, y), 0) for part in range(2)]
            turned = [[pltpu.roll(q, 7, 0) for q in o] for o in own]
            flux = []
            for part in range(2):
                ahead = [jnp.where(right, q, p) for p, q in zip(turned[part], turned[1 - part])]
                flux.append(double_flux(own[part], ahead, 0))
            turned = [[pltpu.roll(q, 1, 0) for q in o] for o in flux]
            for part, ys in enumerate((main_ys, side_ys)):
                if y not in ys:
                    continue
                cons, t = cell(part, y)
                change = [
                    v - jnp.where(left, q, p) for v, p, q in zip(flux[part], turned[part], turned[1 - part])
                ]
                change = [c + (b - a) for c, a, b in zip(change, flux_y(part, y - 1), flux_y(part, y))]
                low = side(cons, t, 2)
                up = [rolled(q, -1) for q in cons]
                flux_z = double_flux(low, side(up, terms(up), 2), 2)
                for f in range(F):
                    upper = jnp.where(roof, 2.0 * t[1] if f == 3 else 0.0, flux_z[f])
                    lower = rolled(upper, 1)
                    if f == 3:
                        lower = jnp.where(floor, 2.0 * t[1], lower)
                    change[f] = change[f] + (upper - lower)
                out = [c - (0.5 * STEP) * d for c, d in zip(cons, change)]
                if number:
                    out = [
                        weight * initial(part, y)[wide_at(f, y, group), :] + (1.0 - weight) * o
                        for f, o in enumerate(out)
                    ]
                if number == 2:
                    out = primitive(out)
                for f in range(F):
                    target(part, y)[wide_at(f, y, group), :] = out[f]
        if number == 2:
            for f in range(F):
                vectors = [target(0, y)[wide_at(f, y, group), :] for y in range(Y)]
                for i, v in enumerate(transposed(vectors)):
                    made[group * 8 + i, f] = v
        return 0

    lax.fori_loop(0, 3, step, 0)


EARLY_MAIN = range(0, Y)
EARLY_SIDE = range(1, Y - 1)


def begin(pos, cur, y_out, y_in, x_out, x_in, main, side_rows, first_main, first_side):
    widen(pos, cur, x_in, x_out, y_in, y_out, main, side_rows)
    initial, first = (main, side_rows), (first_main, first_side)
    advance(0, lambda part, y: initial[part], None, lambda part, y: first[part], EARLY_MAIN, EARLY_SIDE)


def finish(pos, main, side_rows, early_main, early_side, c_out, c_in, made, corner_rows, *held):
    late, second = held[0:2], held[2:4]
    add_corners(pos, c_in, c_out, corner_rows)

    def initial(part, y):
        return (side_rows if 0 <= y < Y else corner_rows) if part else main

    def first(part, y):
        if part:
            return early_side if y in EARLY_SIDE else late[1]
        return early_main if y in EARLY_MAIN else late[0]

    advance(0, initial, None, first, (-2, -1, Y, Y + 1), (-1, 0, Y - 1, Y))
    advance(1, first, initial, lambda part, y: second[part], range(-1, Y + 1), range(0, Y))
    advance(2, lambda part, y: second[part], initial, lambda part, y: late[part], range(0, Y), (), made)


def pack_out(pos, final, mine, other, *outs):
    z, core = pos[0], pos[1]
    for k in range(4):
        d = (z ^ k) * 2 + core
        for s in range(OUT):
            j = final[d * 8 + s]
            row = jnp.maximum(j, 0) >> 1
            kind = jnp.full((X, L), jnp.where(j < 0, 2, (j & 1) ^ core), jnp.int32)
            for f in range(F):
                outs[k][s, f] = jnp.where(kind == 0, mine[row, f], jnp.where(kind == 1, other[row, f], 0.0))


def body(block_cells, slot_blocks):
    row, col = lax.axis_index("row"), lax.axis_index("col")
    pos = jnp.stack([row // 2, row % 2, col]).astype(jnp.int32)

    def to(array, route):
        pairs = []
        for r in range(N_ROW):
            for c in range(N_COL):
                z, core, c2 = route(r // 2, r % 2, c)
                pairs.append((r * N_COL + c, (z * 2 + core) * N_COL + c2 % N_COL))
        return lax.ppermute(array, ("row", "col"), pairs)

    def over_z(array, k):
        return array if k == 0 else to(array, lambda z, core, c: (z ^ k, core, c))

    def over_core(array):
        return to(array, lambda z, core, c: (z, 1 - core, c))

    tiles = [shape(CAP, F, X, L)] * 4
    parts = pl.pallas_call(
        pack_in,
        out_shape=tiles,
        in_specs=[SMEM, VMEM],
        out_specs=[VMEM] * 4,
        compiler_params=PARAMS,
        name="pack_in",
    )(pos, block_cells)
    final, rows, own = pl.pallas_call(
        table,
        out_shape=[
            jax.ShapeDtypeStruct((N_ROW * 8,), jnp.int32),
            jax.ShapeDtypeStruct((N_ROW * CAP,), jnp.int32),
            tiles[0],
        ],
        in_specs=[SMEM, SMEM, ANY],
        out_specs=[SMEM, SMEM, ANY],
        input_output_aliases={2: 2},
        scratch_shapes=[pltpu.SMEM((N_ROW * 16,), jnp.int32), pltpu.SMEM((N_ROW,), jnp.int32)],
        compiler_params=PARAMS,
        cost_estimate=pl.CostEstimate(flops=0, bytes_accessed=20_000_000, transcendentals=0),
        name="table",
    )(pos, slot_blocks, parts[0])
    gathered = []
    for k in range(4):
        here = over_z(parts[k], k) if k else own
        gathered += [here, over_core(here)]

    whole = shape(F * Y * HALF, L)
    layer = shape(F * DEEP * HALF, L)
    initial, x_in, x_out, y_in, y_out = pl.pallas_call(
        reorder,
        out_shape=[whole] + [layer] * 4,
        in_specs=[SMEM, SMEM] + [VMEM] * 8,
        out_specs=[VMEM] * 5,
        scratch_shapes=[pltpu.VMEM((HALF + 1, F, X, L), jnp.float32)],
        compiler_params=PARAMS,
        name="reorder",
    )(pos, rows, *gathered)

    def x_partner(z):
        return z ^ 1

    def y_partner(z):
        return z ^ 3

    def over_x(inner, outer):
        outer = to(outer, lambda z, core, c: (x_partner(z), core, c + 2 * tile_x(z) - 1))
        return to(inner, lambda z, core, c: (x_partner(z), core, c)), outer

    def over_y(inner, outer):
        outer = to(outer, lambda z, core, c: (y_partner(z), 1 - core, c + 2 * tile_y(z) - 1))
        return to(inner, lambda z, core, c: (y_partner(z), core, c)), outer

    y_layers = over_y(y_in, y_out)
    x_layers = over_x(x_in, x_out)
    corner_cells = pl.pallas_call(
        corners,
        out_shape=[shape(F * 3 * 8, L)] * 2,
        in_specs=[SMEM, VMEM, VMEM],
        out_specs=[VMEM] * 2,
        compiler_params=PARAMS,
        name="corners",
    )(pos, *y_layers[::-1])
    corner_cells = over_x(*corner_cells)
    wide = [F * WIDE * HALF, L]
    early = pl.pallas_call(
        begin,
        out_shape=[shape(*wide)] * 4,
        in_specs=[SMEM] + [VMEM] * 5,
        out_specs=[VMEM] * 4,
        compiler_params=PARAMS,
        cost_estimate=pl.CostEstimate(flops=0, bytes_accessed=10_000_000, transcendentals=0),
        name="begin",
    )(pos, initial, *y_layers[::-1], *x_layers[::-1])
    current = pl.pallas_call(
        finish,
        out_shape=shape(HALF, F, X, L),
        in_specs=[SMEM] + [VMEM] * 6,
        out_specs=VMEM,
        scratch_shapes=[pltpu.VMEM(wide, jnp.float32)] * 5,
        compiler_params=PARAMS,
        name="finish",
    )(pos, *early, *corner_cells[::-1])

    leaving = pl.pallas_call(
        pack_out,
        out_shape=[shape(OUT, F, X, L)] * 4,
        in_specs=[SMEM, SMEM, VMEM, VMEM],
        out_specs=[VMEM] * 4,
        compiler_params=PARAMS,
        name="pack_out",
    )(pos, final, current, over_core(current))
    arrived = [over_z(leaving[k], k) for k in range(4)]
    result = []
    for which in ((0, 1, 3), (2,)):
        n = len(which)
        result = [
            pl.pallas_call(
                lambda *refs, which=which: unpack_out(which, *refs),
                out_shape=shape(OUT, F, 2 * X, 2 * L),
                in_specs=[SMEM] + [ANY] * (n + len(result)),
                out_specs=ANY,
                input_output_aliases={n + 1: 0} if result else {},
                scratch_shapes=[pltpu.SemaphoreType.DMA((n,))],
                compiler_params=PARAMS,
                name="unpack_out",
            )(pos, *[arrived[k] for k in which], *result)
        ]
    return result[0]


def solution(mesh):
    in_specs = (P(("row", "col"), None, None, None), P())
    out_specs = P(("row", "col"), None, None, None)
    return jax.shard_map(body, mesh=mesh, in_specs=in_specs, out_specs=out_specs, check_vma=False)
```

```python
import math

import jax
import jax.numpy as jnp
from jax import lax
from jax.experimental import pallas as pl
from jax.experimental.pallas import tpu as pltpu
from jax.sharding import PartitionSpec as P

CAP = 11
OUT = 7
NBY = 48
N_ROW = 8
N_COL = 16
HALF = NBY // 2
F = 5
X = Y = 8
L = 128
DEEP = 3
WIDE = Y + 2 * DEEP

GAMMA = 1.4
STEP = 0.12
LOG2_E = 1.0 / math.log(2.0)

VMEM = pl.BlockSpec(memory_space=pltpu.VMEM)
SMEM = pl.BlockSpec(memory_space=pltpu.SMEM)
ANY = pl.BlockSpec(memory_space=pl.ANY)
PARAMS = pltpu.CompilerParams(vmem_limit_bytes=24 * 1024 * 1024)


def shape(*dims):
    return jax.ShapeDtypeStruct(dims, jnp.float32)


def tile_x(z):
    return ((z + 1) // 2) % 2


def tile_y(z):
    return z // 2


def pack_in(pos, cells, *outs):
    z = pos[0]
    for k in range(4):
        x = pl.ds(pl.multiple_of(tile_x(z ^ k) * X, X), X)
        y = pl.ds(pl.multiple_of(tile_y(z ^ k) * L, L), L)
        for s in range(CAP):
            for f in range(F):
                outs[k][s, f] = cells[s, f, x, y]


def unpack_out(which, pos, *refs):
    out, sems = refs[-2:]
    z = pos[0]
    copies = []
    for i, k in enumerate(which):
        x = pl.ds(pl.multiple_of(tile_x(z ^ k) * X, X), X)
        y = pl.ds(pl.multiple_of(tile_y(z ^ k) * L, L), L)
        copies.append(pltpu.make_async_copy(refs[i], out.at[:, :, x, y], sems.at[i]))
    for c in copies:
        c.start()
    for c in copies:
        c.wait()


def table(pos, slots, _tile, final, rows, _same, held, count):
    z, core, g = pos[0], pos[1], pos[2]
    for d in range(N_ROW):
        n = jnp.int32(0)
        place = ((z ^ d // 2) * 2 + (core ^ d % 2)) * CAP
        for s in range(CAP):
            b = slots[d * N_COL + g, s]
            j = b - g * NBY
            held[d * 16 + s] = j
            here = jnp.logical_and(b >= 0, (j & 1) == core)
            rows[place + s] = jnp.where(here, j >> 1, HALF)
            n = n + jnp.where(b >= 0, 1, 0)
        count[d] = n
    for bit in range(3):
        for low in range(N_ROW):
            if low >> bit & 1:
                continue
            high = low | 1 << bit
            a, b = count[low], count[high]
            up = a > b
            src = jnp.where(up, low, high)
            dst = jnp.where(up, high, low)
            n_src = jnp.maximum(a, b)
            n_dst = jnp.minimum(a, b)
            moved = (n_src - n_dst) // 2

            def move(i, _, src=src, dst=dst, n_src=n_src, n_dst=n_dst, moved=moved):
                held[dst * 16 + n_dst + i] = held[src * 16 + n_src - moved + i]
                return 0

            lax.fori_loop(0, moved, move, 0)
            count[src] = n_src - moved
            count[dst] = n_dst + moved
    for d in range(N_ROW):
        n = count[d]
        for s in range(8):
            final[d * 8 + s] = jnp.where(s < n, held[d * 16 + s], -1)


def rolled(v, shift):
    shift %= L
    return v if shift == 0 else pltpu.roll(v, shift, 1)


def inverse(rho):
    guess = pl.reciprocal(rho, approx=True)
    return guess * (2.0 - rho * guess)


def terms(cons):
    rho, mx, my, mz, energy = cons
    inv = inverse(rho)
    u, v, w = mx * inv, my * inv, mz * inv
    p = (GAMMA - 1.0) * energy - (0.5 * (GAMMA - 1.0)) * (mx * u + my * v + mz * w)
    theta = p * inv
    power = jnp.log(theta)
    sound = jnp.exp2(power * (0.5 * LOG2_E) + 0.5 * math.log2(GAMMA))
    kappa = jnp.exp2(power * (0.7 * LOG2_E) + math.log2(0.2))
    return (u, v, w), p, theta, sound, kappa


def side(cons, t, n):
    vel, p, theta, sound, kappa = t
    flux = [cons[f] * vel[n] for f in (1, 2, 3)]
    flux[n] = flux[n] + p
    return (*cons, *flux, (cons[4] + p) * vel[n], theta, kappa, jnp.abs(vel[n]) + sound)


def double_flux(low, high, n):
    speed = jnp.maximum(low[11], high[11])
    out = []
    for f in range(F):
        k = F + f - 1 if f else n + 1
        out.append((low[k] + high[k]) - speed * (high[f] - low[f]))
    out[4] = out[4] - (low[10] + high[10]) * (high[9] - low[9])
    return out


def primitive(cons):
    rho, mx, my, mz, energy = cons
    inv = inverse(rho)
    u, v, w = mx * inv, my * inv, mz * inv
    return [rho, u, v, w, (GAMMA - 1.0) * (energy - 0.5 * rho * (u * u + v * v + w * w))]


def conserved(prim):
    rho, u, v, w, p = prim
    return [rho, rho * u, rho * v, rho * w, p * (1.0 / (GAMMA - 1.0)) + 0.5 * rho * (u * u + v * v + w * w)]


def at(f, y, group):
    return pl.ds(pl.multiple_of((f * Y + y) * HALF + group * 8, 8), 8)


def wide_at(f, y, group):
    return pl.ds(pl.multiple_of((f * WIDE + DEEP + y) * HALF + group * 8, 8), 8)


def strip_at(f, t, group):
    return pl.ds(pl.multiple_of((f * DEEP + t) * HALF + group * 8, 8), 8)


def x_layer_at(f, group, x):
    return pl.ds(f * Y * HALF + group * 8 + x, Y, HALF)


def transposed(vectors):
    place = lax.broadcasted_iota(jnp.int32, (8, L), 1) // 16
    vectors = list(vectors)
    for bit in (1, 2, 4):
        clear = (place & bit) == 0
        for i in range(8):
            if i & bit:
                continue
            a, b = vectors[i], vectors[i | bit]
            vectors[i] = jnp.where(clear, a, rolled(b, 16 * bit))
            vectors[i | bit] = jnp.where(clear, rolled(a, -16 * bit), b)
    return vectors


def faces(pos, cur, x_in, x_out, y_in, y_out):
    zx, zy, core = tile_x(pos[0]), tile_y(pos[0]), pos[1]
    place = lax.broadcasted_iota(jnp.int32, (8, L), 1) // 16
    first = jnp.full((8, L), zy, jnp.int32) == 0
    turn = jnp.full((8, L), jnp.where(core == zy, 1, 0), jnp.int32) == 1
    far = Y - DEEP
    for f in range(F):
        for t in range(DEEP):
            ahead, back = [], []
            for group in range(3):
                to = pl.ds(((f * 3 + group) * DEEP + t) * 8, 8)
                x_in[to, :] = cur[x_layer_at(f, group, far * (1 - zx) + t), :]
                x_out[to, :] = cur[x_layer_at(f, group, far * zx + t), :]
                y_in[strip_at(f, t, group), :] = cur[at(f, far * (1 - zy) + t, group), :]
                v = cur[at(f, far * zy + t, group), :]
                ahead.append(rolled(v, 16))
                back.append(rolled(v, -16))
            for group in range(3):
                high = jnp.where(place == 0, ahead[group - 1], ahead[group])
                low = jnp.where(place == 7, back[(group + 1) % 3], back[group])
                v = cur[at(f, far * zy + t, group), :]
                y_out[strip_at(f, t, group), :] = jnp.where(turn, jnp.where(first, low, high), v)


def corners(pos, y_in, y_out, to_in, to_out):
    zx, zy = tile_x(pos[0]), tile_y(pos[0])

    def copy(low, high):
        for f in range(F):
            for group in range(3):
                for r in range(2):
                    for out, x in ((to_in, 6 * (1 - zx) + r), (to_out, 6 * zx + r)):
                        row = ((f * 3 + group) * 2 + r) * 4
                        base = f * DEEP * HALF + group * 8 + x
                        out[row : row + 2, :] = low[pl.ds(base + HALF, 2, HALF), :]
                        out[row + 2 : row + 4, :] = high[pl.ds(base, 2, HALF), :]

    @pl.when(zy == 0)
    def _():
        copy(y_out, y_in)

    @pl.when(zy == 1)
    def _():
        copy(y_in, y_out)


def reorder(pos, rows, *refs):
    parts = refs[:8]
    cur, x_in, x_out, y_in, y_out = refs[8:13]
    held = refs[13]
    for i in range(8):
        for s in range(CAP):
            held[rows[i * CAP + s]] = parts[i][s]

    def convert(group, _):
        for f in range(F):
            vectors = [held[group * 8 + i, f] for i in range(8)]
            for y, v in enumerate(transposed(vectors)):
                cur[at(f, y, group), :] = v
        for y in range(Y):
            prim = [cur[at(f, y, group), :] for f in range(F)]
            for f, v in enumerate(conserved(prim)):
                if f:
                    cur[at(f, y, group), :] = v
        return 0

    lax.fori_loop(0, 3, convert, 0)
    faces(pos, cur, x_in, x_out, y_in, y_out)


def widen(pos, cur, x_in, x_out, y_in, y_out, main, side_rows):
    zx, zy = tile_x(pos[0]), tile_y(pos[0])
    for f in range(F):
        for group in range(3):
            for y in range(Y):
                main[wide_at(f, y, group), :] = cur[at(f, y, group), :]
            for t in range(DEEP):
                main[wide_at(f, Y * (1 - zy) - DEEP * zy + t, group), :] = y_in[strip_at(f, t, group), :]
                main[wide_at(f, Y * zy - DEEP * (1 - zy) + t, group), :] = y_out[strip_at(f, t, group), :]
                at_t = pl.ds(((f * 3 + group) * DEEP + t) * 8, 8)
                base = (f * WIDE + DEEP) * HALF + group * 8 + t
                side_rows[pl.ds(base + 5 * zx, 8, HALF), :] = x_in[at_t, :]
                side_rows[pl.ds(base + 5 * (1 - zx), 8, HALF), :] = x_out[at_t, :]


def add_corners(pos, c_in, c_out, side_rows):
    zx = tile_x(pos[0])
    for f in range(F):
        for group in range(3):
            for r in range(2):
                row = ((f * 3 + group) * 2 + r) * 4
                for c, beyond in ((c_in, 6 * zx), (c_out, 6 * (1 - zx))):
                    for k, y in ((0, -2), (2, Y)):
                        to = (f * WIDE + DEEP + y) * HALF + group * 8 + r + beyond
                        side_rows[pl.ds(to, 2, HALF), :] = c[row + k : row + k + 2, :]


def advance(number, source, initial, target, main_ys, side_ys, made=None):
    weight = (0.0, 0.75, 1.0 / 3.0)[number]

    def step(group, _):
        height = lax.broadcasted_iota(jnp.int32, (8, L), 1) % 16
        sub = lax.broadcasted_iota(jnp.int32, (8, L), 0)
        floor, roof = height == 0, height == 15
        left, right = sub == 0, sub == 7
        cells, fluxes = {}, {}

        def cell(part, y):
            if (part, y) not in cells:
                cons = [source(part, y)[wide_at(f, y, group), :] for f in range(F)]
                cells[part, y] = cons, terms(cons)
            return cells[part, y]

        def flux_y(part, y):
            if (part, y) not in fluxes:
                fluxes[part, y] = double_flux(side(*cell(part, y), 1), side(*cell(part, y + 1), 1), 1)
            return fluxes[part, y]

        for y in sorted({*main_ys, *side_ys}):
            own = [side(*cell(part, y), 0) for part in range(2)]
            turned = [[pltpu.roll(q, 7, 0) for q in o] for o in own]
            flux = []
            for part in range(2):
                ahead = [jnp.where(right, q, p) for p, q in zip(turned[part], turned[1 - part])]
                flux.append(double_flux(own[part], ahead, 0))
            turned = [[pltpu.roll(q, 1, 0) for q in o] for o in flux]
            for part, ys in enumerate((main_ys, side_ys)):
                if y not in ys:
                    continue
                cons, t = cell(part, y)
                change = [
                    v - jnp.where(left, q, p) for v, p, q in zip(flux[part], turned[part], turned[1 - part])
                ]
                change = [c + (b - a) for c, a, b in zip(change, flux_y(part, y - 1), flux_y(part, y))]
                low = side(cons, t, 2)
                up = [rolled(q, -1) for q in cons]
                flux_z = double_flux(low, side(up, terms(up), 2), 2)
                for f in range(F):
                    upper = jnp.where(roof, 2.0 * t[1] if f == 3 else 0.0, flux_z[f])
                    lower = rolled(upper, 1)
                    if f == 3:
                        lower = jnp.where(floor, 2.0 * t[1], lower)
                    change[f] = change[f] + (upper - lower)
                out = [c - (0.5 * STEP) * d for c, d in zip(cons, change)]
                if number:
                    out = [
                        weight * initial(part, y)[wide_at(f, y, group), :] + (1.0 - weight) * o
                        for f, o in enumerate(out)
                    ]
                if number == 2:
                    out = primitive(out)
                for f in range(F):
                    target(part, y)[wide_at(f, y, group), :] = out[f]
        if number == 2:
            for f in range(F):
                vectors = [target(0, y)[wide_at(f, y, group), :] for y in range(Y)]
                for i, v in enumerate(transposed(vectors)):
                    made[group * 8 + i, f] = v
        return 0

    lax.fori_loop(0, 3, step, 0)


EARLY = ((range(0, Y), range(1, Y - 1)), (range(1, Y - 1), range(2, Y - 2)))


def begin(pos, cur, x_in, x_out, y_in, y_out, main, side_rows, *made):
    widen(pos, cur, x_in, x_out, y_in, y_out, main, side_rows)
    initial = (main, side_rows)
    advance(0, lambda part, y: initial[part], None, lambda part, y: made[part], *EARLY[0])
    advance(1, lambda part, y: made[part], lambda part, y: initial[part], lambda part, y: made[2 + part], *EARLY[1])


def finish(pos, main, side_rows, *refs):
    early, (c_in, c_out, made, corner_rows), late = refs[:4], refs[4:8], refs[8:12]
    add_corners(pos, c_in, c_out, corner_rows)

    def initial(part, y):
        return (side_rows if 0 <= y < Y else corner_rows) if part else main

    def first(part, y):
        return (early if y in EARLY[0][part] else late)[part]

    def second(part, y):
        return (early if y in EARLY[1][part] else late)[2 + part]

    advance(0, initial, None, first, (-2, -1, Y, Y + 1), (-1, 0, Y - 1, Y))
    advance(1, first, initial, second, (-1, 0, Y - 1, Y), (0, 1, Y - 2, Y - 1))
    advance(2, second, initial, lambda part, y: late[part], range(0, Y), (), made)


def pack_out(pos, final, mine, other, *outs):
    z, core = pos[0], pos[1]
    for k in range(4):
        d = (z ^ k) * 2 + core
        for s in range(OUT):
            j = final[d * 8 + s]
            row = jnp.maximum(j, 0) >> 1
            kind = jnp.full((X, L), jnp.where(j < 0, 2, (j & 1) ^ core), jnp.int32)
            for f in range(F):
                outs[k][s, f] = jnp.where(kind == 0, mine[row, f], jnp.where(kind == 1, other[row, f], 0.0))


def body(block_cells, slot_blocks):
    row, col = lax.axis_index("row"), lax.axis_index("col")
    pos = jnp.stack([row // 2, row % 2, col]).astype(jnp.int32)

    def to(array, route):
        pairs = []
        for r in range(N_ROW):
            for c in range(N_COL):
                z, core, c2 = route(r // 2, r % 2, c)
                pairs.append((r * N_COL + c, (z * 2 + core) * N_COL + c2 % N_COL))
        return lax.ppermute(array, ("row", "col"), pairs)

    def over_z(array, k):
        return array if k == 0 else to(array, lambda z, core, c: (z ^ k, core, c))

    def over_core(array):
        return to(array, lambda z, core, c: (z, 1 - core, c))

    tiles = [shape(CAP, F, X, L)] * 4
    parts = pl.pallas_call(
        pack_in,
        out_shape=tiles,
        in_specs=[SMEM, VMEM],
        out_specs=[VMEM] * 4,
        compiler_params=PARAMS,
        name="pack_in",
    )(pos, block_cells)
    final, rows, own = pl.pallas_call(
        table,
        out_shape=[
            jax.ShapeDtypeStruct((N_ROW * 8,), jnp.int32),
            jax.ShapeDtypeStruct((N_ROW * CAP,), jnp.int32),
            tiles[0],
        ],
        in_specs=[SMEM, SMEM, ANY],
        out_specs=[SMEM, SMEM, ANY],
        input_output_aliases={2: 2},
        scratch_shapes=[pltpu.SMEM((N_ROW * 16,), jnp.int32), pltpu.SMEM((N_ROW,), jnp.int32)],
        compiler_params=PARAMS,
        cost_estimate=pl.CostEstimate(flops=0, bytes_accessed=20_000_000, transcendentals=0),
        name="table",
    )(pos, slot_blocks, parts[0])
    gathered = []
    for k in range(4):
        here = over_z(parts[k], k) if k else own
        gathered += [here, over_core(here)]

    whole = shape(F * Y * HALF, L)
    layer = shape(F * DEEP * HALF, L)
    initial, x_in, x_out, y_in, y_out = pl.pallas_call(
        reorder,
        out_shape=[whole] + [layer] * 4,
        in_specs=[SMEM, SMEM] + [VMEM] * 8,
        out_specs=[VMEM] * 5,
        scratch_shapes=[pltpu.VMEM((HALF + 1, F, X, L), jnp.float32)],
        compiler_params=PARAMS,
        name="reorder",
    )(pos, rows, *gathered)

    def x_partner(z):
        return z ^ 1

    def y_partner(z):
        return z ^ 3

    def over_x(inner, outer):
        return (
            to(inner, lambda z, core, c: (x_partner(z), core, c)),
            to(outer, lambda z, core, c: (x_partner(z), core, c + 2 * tile_x(z) - 1)),
        )

    def over_y(inner, outer):
        return (
            to(inner, lambda z, core, c: (y_partner(z), core, c)),
            to(outer, lambda z, core, c: (y_partner(z), 1 - core, c + 2 * tile_y(z) - 1)),
        )

    y_layers = over_y(y_in, y_out)
    x_layers = over_x(x_in, x_out)
    corner_cells = pl.pallas_call(
        corners,
        out_shape=[shape(F * 3 * 8, L)] * 2,
        in_specs=[SMEM, VMEM, VMEM],
        out_specs=[VMEM] * 2,
        compiler_params=PARAMS,
        name="corners",
    )(pos, *y_layers)
    corner_cells = over_x(*corner_cells)
    wide = [F * WIDE * HALF, L]
    early = pl.pallas_call(
        begin,
        out_shape=[shape(*wide)] * 6,
        in_specs=[SMEM] + [VMEM] * 5,
        out_specs=[VMEM] * 6,
        compiler_params=PARAMS,
        cost_estimate=pl.CostEstimate(flops=0, bytes_accessed=10_000_000, transcendentals=0),
        name="begin",
    )(pos, initial, *x_layers, *y_layers)
    current = pl.pallas_call(
        finish,
        out_shape=shape(HALF, F, X, L),
        in_specs=[SMEM] + [VMEM] * 8,
        out_specs=VMEM,
        scratch_shapes=[pltpu.VMEM(wide, jnp.float32)] * 5,
        compiler_params=PARAMS,
        name="finish",
    )(pos, *early, *corner_cells)

    leaving = pl.pallas_call(
        pack_out,
        out_shape=[shape(OUT, F, X, L)] * 4,
        in_specs=[SMEM, SMEM, VMEM, VMEM],
        out_specs=[VMEM] * 4,
        compiler_params=PARAMS,
        name="pack_out",
    )(pos, final, current, over_core(current))
    arrived = [over_z(leaving[k], k) for k in range(4)]
    result = []
    for which in ((0, 1, 3), (2,)):
        n = len(which)
        result = [
            pl.pallas_call(
                lambda *refs, which=which: unpack_out(which, *refs),
                out_shape=shape(OUT, F, 2 * X, 2 * L),
                in_specs=[SMEM] + [ANY] * (n + len(result)),
                out_specs=ANY,
                input_output_aliases={n + 1: 0} if result else {},
                scratch_shapes=[pltpu.SemaphoreType.DMA((n,))],
                compiler_params=PARAMS,
                name="unpack_out",
            )(pos, *[arrived[k] for k in which], *result)
        ]
    return result[0]


def solution(mesh):
    in_specs = (P(("row", "col"), None, None, None), P())
    out_specs = P(("row", "col"), None, None, None)
    return jax.shard_map(body, mesh=mesh, in_specs=in_specs, out_specs=out_specs, check_vma=False)
```

```python
import math

import jax
import jax.numpy as jnp
from jax import lax
from jax.experimental import pallas as pl
from jax.experimental.pallas import tpu as pltpu
from jax.sharding import PartitionSpec as P

CAP = 11
OUT = 7
NBY = 48
N_ROW = 8
N_COL = 16
HALF = NBY // 2
F = 5
X = Y = 8
L = 128
DEEP = 3
WIDE = Y + 2 * DEEP

GAMMA = 1.4
STEP = 0.12
LOG2_E = 1.0 / math.log(2.0)

VMEM = pl.BlockSpec(memory_space=pltpu.VMEM)
SMEM = pl.BlockSpec(memory_space=pltpu.SMEM)
ANY = pl.BlockSpec(memory_space=pl.ANY)
PARAMS = pltpu.CompilerParams(vmem_limit_bytes=24 * 1024 * 1024)


def shape(*dims):
    return jax.ShapeDtypeStruct(dims, jnp.float32)


def tile_x(z):
    return ((z + 1) // 2) % 2


def tile_y(z):
    return z // 2


def pack_in(pos, cells, *outs):
    z = pos[0]
    for k in range(4):
        x = pl.ds(pl.multiple_of(tile_x(z ^ k) * X, X), X)
        y = pl.ds(pl.multiple_of(tile_y(z ^ k) * L, L), L)
        for s in range(CAP):
            for f in range(F):
                outs[k][s, f] = cells[s, f, x, y]


def unpack_out(which, pos, *refs):
    out, sems = refs[-2:]
    z = pos[0]
    copies = []
    for i, k in enumerate(which):
        x = pl.ds(pl.multiple_of(tile_x(z ^ k) * X, X), X)
        y = pl.ds(pl.multiple_of(tile_y(z ^ k) * L, L), L)
        copies.append(pltpu.make_async_copy(refs[i], out.at[:, :, x, y], sems.at[i]))
    for c in copies:
        c.start()
    for c in copies:
        c.wait()


def table(pos, slots, _tile, final, rows, _same, held, count):
    z, core, g = pos[0], pos[1], pos[2]
    for d in range(N_ROW):
        n = jnp.int32(0)
        place = ((z ^ d // 2) * 2 + (core ^ d % 2)) * CAP
        for s in range(CAP):
            b = slots[d * N_COL + g, s]
            j = b - g * NBY
            held[d * 16 + s] = j
            here = jnp.logical_and(b >= 0, (j & 1) == core)
            rows[place + s] = jnp.where(here, j >> 1, HALF)
            n = n + jnp.where(b >= 0, 1, 0)
        count[d] = n
    for bit in range(3):
        for low in range(N_ROW):
            if low >> bit & 1:
                continue
            high = low | 1 << bit
            a, b = count[low], count[high]
            up = a > b
            src = jnp.where(up, low, high)
            dst = jnp.where(up, high, low)
            n_src = jnp.maximum(a, b)
            n_dst = jnp.minimum(a, b)
            moved = (n_src - n_dst) // 2

            def move(i, _, src=src, dst=dst, n_src=n_src, n_dst=n_dst, moved=moved):
                held[dst * 16 + n_dst + i] = held[src * 16 + n_src - moved + i]
                return 0

            lax.fori_loop(0, moved, move, 0)
            count[src] = n_src - moved
            count[dst] = n_dst + moved
    for d in range(N_ROW):
        n = count[d]
        for s in range(8):
            final[d * 8 + s] = jnp.where(s < n, held[d * 16 + s], -1)


def rolled(v, shift):
    shift %= L
    return v if shift == 0 else pltpu.roll(v, shift, 1)


def inverse(rho):
    guess = pl.reciprocal(rho, approx=True)
    return guess * (2.0 - rho * guess)


def terms(cons):
    rho, mx, my, mz, energy = cons
    inv = inverse(rho)
    u, v, w = mx * inv, my * inv, mz * inv
    p = (GAMMA - 1.0) * energy - (0.5 * (GAMMA - 1.0)) * (mx * u + my * v + mz * w)
    theta = p * inv
    power = jnp.log(theta)
    sound = jnp.exp2(power * (0.5 * LOG2_E) + 0.5 * math.log2(GAMMA))
    kappa = jnp.exp2(power * (0.7 * LOG2_E) + math.log2(0.2))
    return (u, v, w), p, theta, sound, kappa


def side(cons, t, n):
    vel, p, theta, sound, kappa = t
    flux = [cons[f] * vel[n] for f in (1, 2, 3)]
    flux[n] = flux[n] + p
    return (*cons, *flux, (cons[4] + p) * vel[n], theta, kappa, jnp.abs(vel[n]) + sound)


def double_flux(low, high, n):
    speed = jnp.maximum(low[11], high[11])
    out = []
    for f in range(F):
        k = F + f - 1 if f else n + 1
        out.append((low[k] + high[k]) - speed * (high[f] - low[f]))
    out[4] = out[4] - (low[10] + high[10]) * (high[9] - low[9])
    return out


def primitive(cons):
    rho, mx, my, mz, energy = cons
    inv = inverse(rho)
    u, v, w = mx * inv, my * inv, mz * inv
    return [rho, u, v, w, (GAMMA - 1.0) * (energy - 0.5 * rho * (u * u + v * v + w * w))]


def conserved(prim):
    rho, u, v, w, p = prim
    return [rho, rho * u, rho * v, rho * w, p * (1.0 / (GAMMA - 1.0)) + 0.5 * rho * (u * u + v * v + w * w)]


def at(f, y, group):
    return pl.ds(pl.multiple_of((f * Y + y) * HALF + group * 8, 8), 8)


def wide_at(f, y, group):
    return pl.ds(pl.multiple_of((f * WIDE + DEEP + y) * HALF + group * 8, 8), 8)


def strip_at(f, t, group):
    return pl.ds(pl.multiple_of((f * DEEP + t) * HALF + group * 8, 8), 8)


def x_layer_at(f, group, x):
    return pl.ds(f * Y * HALF + group * 8 + x, Y, HALF)


def transposed(vectors):
    place = lax.broadcasted_iota(jnp.int32, (8, L), 1) // 16
    vectors = list(vectors)
    for bit in (1, 2, 4):
        clear = (place & bit) == 0
        for i in range(8):
            if i & bit:
                continue
            a, b = vectors[i], vectors[i | bit]
            vectors[i] = jnp.where(clear, a, rolled(b, 16 * bit))
            vectors[i | bit] = jnp.where(clear, rolled(a, -16 * bit), b)
    return vectors


def faces(pos, cur, x_in, x_out, y_in, y_out):
    zx, zy, core = tile_x(pos[0]), tile_y(pos[0]), pos[1]
    place = lax.broadcasted_iota(jnp.int32, (8, L), 1) // 16
    first = jnp.full((8, L), zy, jnp.int32) == 0
    turn = jnp.full((8, L), jnp.where(core == zy, 1, 0), jnp.int32) == 1
    far = Y - DEEP
    for f in range(F):
        for t in range(DEEP):
            ahead, back = [], []
            for group in range(3):
                to = pl.ds(((f * 3 + group) * DEEP + t) * 8, 8)
                x_in[to, :] = cur[x_layer_at(f, group, far * (1 - zx) + t), :]
                x_out[to, :] = cur[x_layer_at(f, group, far * zx + t), :]
                y_in[strip_at(f, t, group), :] = cur[at(f, far * (1 - zy) + t, group), :]
                v = cur[at(f, far * zy + t, group), :]
                ahead.append(rolled(v, 16))
                back.append(rolled(v, -16))
            for group in range(3):
                high = jnp.where(place == 0, ahead[group - 1], ahead[group])
                low = jnp.where(place == 7, back[(group + 1) % 3], back[group])
                v = cur[at(f, far * zy + t, group), :]
                y_out[strip_at(f, t, group), :] = jnp.where(turn, jnp.where(first, low, high), v)


def corners(pos, y_in, y_out, to_in, to_out):
    zx, zy = tile_x(pos[0]), tile_y(pos[0])

    def copy(low, high):
        for f in range(F):
            for group in range(3):
                for r in range(2):
                    for out, x in ((to_in, 6 * (1 - zx) + r), (to_out, 6 * zx + r)):
                        row = ((f * 3 + group) * 2 + r) * 4
                        base = f * DEEP * HALF + group * 8 + x
                        out[row : row + 2, :] = low[pl.ds(base + HALF, 2, HALF), :]
                        out[row + 2 : row + 4, :] = high[pl.ds(base, 2, HALF), :]

    @pl.when(zy == 0)
    def _():
        copy(y_out, y_in)

    @pl.when(zy == 1)
    def _():
        copy(y_in, y_out)


def reorder(pos, rows, *refs):
    parts = refs[:8]
    cur, x_in, x_out, y_in, y_out = refs[8:13]
    held = refs[13]
    for i in range(8):
        for s in range(CAP):
            held[rows[i * CAP + s]] = parts[i][s]

    def convert(group, _):
        for f in range(F):
            vectors = [held[group * 8 + i, f] for i in range(8)]
            for y, v in enumerate(transposed(vectors)):
                cur[at(f, y, group), :] = v
        for y in range(Y):
            prim = [cur[at(f, y, group), :] for f in range(F)]
            for f, v in enumerate(conserved(prim)):
                if f:
                    cur[at(f, y, group), :] = v
        return 0

    lax.fori_loop(0, 3, convert, 0)
    faces(pos, cur, x_in, x_out, y_in, y_out)


def widen(pos, cur, x_in, x_out, y_in, y_out, main, side_rows):
    zx, zy = tile_x(pos[0]), tile_y(pos[0])
    for f in range(F):
        for group in range(3):
            for y in range(Y):
                main[wide_at(f, y, group), :] = cur[at(f, y, group), :]
            for t in range(DEEP):
                main[wide_at(f, Y * (1 - zy) - DEEP * zy + t, group), :] = y_in[strip_at(f, t, group), :]
                main[wide_at(f, Y * zy - DEEP * (1 - zy) + t, group), :] = y_out[strip_at(f, t, group), :]
                at_t = pl.ds(((f * 3 + group) * DEEP + t) * 8, 8)
                base = (f * WIDE + DEEP) * HALF + group * 8 + t
                side_rows[pl.ds(base + 5 * zx, 8, HALF), :] = x_in[at_t, :]
                side_rows[pl.ds(base + 5 * (1 - zx), 8, HALF), :] = x_out[at_t, :]


def add_corners(pos, c_in, c_out, side_rows):
    zx = tile_x(pos[0])
    for f in range(F):
        for group in range(3):
            for r in range(2):
                row = ((f * 3 + group) * 2 + r) * 4
                for c, beyond in ((c_in, 6 * zx), (c_out, 6 * (1 - zx))):
                    for k, y in ((0, -2), (2, Y)):
                        to = (f * WIDE + DEEP + y) * HALF + group * 8 + r + beyond
                        side_rows[pl.ds(to, 2, HALF), :] = c[row + k : row + k + 2, :]


def advance(number, source, initial, target, main_ys, side_ys, made=None):
    weight = (0.0, 0.75, 1.0 / 3.0)[number]

    def step(group, _):
        height = lax.broadcasted_iota(jnp.int32, (8, L), 1) % 16
        sub = lax.broadcasted_iota(jnp.int32, (8, L), 0)
        floor, roof = height == 0, height == 15
        left, right = sub == 0, sub == 7
        cells, fluxes = {}, {}

        def cell(part, y):
            if (part, y) not in cells:
                cons = [source(part, y)[wide_at(f, y, group), :] for f in range(F)]
                cells[part, y] = cons, terms(cons)
            return cells[part, y]

        def flux_y(part, y):
            if (part, y) not in fluxes:
                fluxes[part, y] = double_flux(side(*cell(part, y), 1), side(*cell(part, y + 1), 1), 1)
            return fluxes[part, y]

        for y in sorted({*main_ys, *side_ys}):
            own = [side(*cell(part, y), 0) for part in range(2)]
            turned = [[pltpu.roll(q, 7, 0) for q in o] for o in own]
            flux = []
            for part in range(2):
                ahead = [jnp.where(right, q, p) for p, q in zip(turned[part], turned[1 - part])]
                flux.append(double_flux(own[part], ahead, 0))
            turned = [[pltpu.roll(q, 1, 0) for q in o] for o in flux]
            for part, ys in enumerate((main_ys, side_ys)):
                if y not in ys:
                    continue
                cons, t = cell(part, y)
                change = [
                    v - jnp.where(left, q, p) for v, p, q in zip(flux[part], turned[part], turned[1 - part])
                ]
                change = [c + (b - a) for c, a, b in zip(change, flux_y(part, y - 1), flux_y(part, y))]
                low = side(cons, t, 2)
                up = [rolled(q, -1) for q in cons]
                flux_z = double_flux(low, side(up, terms(up), 2), 2)
                for f in range(F):
                    upper = jnp.where(roof, 2.0 * t[1] if f == 3 else 0.0, flux_z[f])
                    lower = rolled(upper, 1)
                    if f == 3:
                        lower = jnp.where(floor, 2.0 * t[1], lower)
                    change[f] = change[f] + (upper - lower)
                out = [c - (0.5 * STEP) * d for c, d in zip(cons, change)]
                if number:
                    out = [
                        weight * initial(part, y)[wide_at(f, y, group), :] + (1.0 - weight) * o
                        for f, o in enumerate(out)
                    ]
                if number == 2:
                    out = primitive(out)
                for f in range(F):
                    target(part, y)[wide_at(f, y, group), :] = out[f]
        if number == 2:
            for f in range(F):
                vectors = [target(0, y)[wide_at(f, y, group), :] for y in range(Y)]
                for i, v in enumerate(transposed(vectors)):
                    made[group * 8 + i, f] = v
        return 0

    lax.fori_loop(0, 3, step, 0)


EARLY = ((range(0, Y), range(1, Y - 1)), (range(1, Y - 1), range(2, Y - 2)))


def begin(pos, cur, x_in, x_out, y_in, y_out, main, side_rows, *made):
    widen(pos, cur, x_in, x_out, y_in, y_out, main, side_rows)
    initial = (main, side_rows)
    advance(0, lambda part, y: initial[part], None, lambda part, y: made[part], *EARLY[0])
    advance(1, lambda part, y: made[part], lambda part, y: initial[part], lambda part, y: made[2 + part], *EARLY[1])


def finish(pos, main, side_rows, *refs):
    early, (c_in, c_out, made, corner_rows), late = refs[:4], refs[4:8], refs[8:12]
    add_corners(pos, c_in, c_out, corner_rows)

    def initial(part, y):
        return (side_rows if 0 <= y < Y else corner_rows) if part else main

    def first(part, y):
        return (early if y in EARLY[0][part] else late)[part]

    def second(part, y):
        return (early if y in EARLY[1][part] else late)[2 + part]

    advance(0, initial, None, first, (-2, -1, Y, Y + 1), (-1, 0, Y - 1, Y))
    advance(1, first, initial, second, (-1, 0, Y - 1, Y), (0, 1, Y - 2, Y - 1))
    advance(2, second, initial, lambda part, y: late[part], range(0, Y), (), made)


def pack_out(pos, final, mine, other, *outs):
    z, core = pos[0], pos[1]
    for k in range(4):
        d = (z ^ k) * 2 + core
        for s in range(OUT):
            j = final[d * 8 + s]
            row = jnp.maximum(j, 0) >> 1
            kind = jnp.full((X, L), jnp.where(j < 0, 2, (j & 1) ^ core), jnp.int32)
            for f in range(F):
                outs[k][s, f] = jnp.where(kind == 0, mine[row, f], jnp.where(kind == 1, other[row, f], 0.0))


def body(block_cells, slot_blocks):
    row, col = lax.axis_index("row"), lax.axis_index("col")
    pos = jnp.stack([row // 2, row % 2, col]).astype(jnp.int32)

    def to(array, route):
        pairs = []
        for r in range(N_ROW):
            for c in range(N_COL):
                z, core, c2 = route(r // 2, r % 2, c)
                pairs.append((r * N_COL + c, (z * 2 + core) * N_COL + c2 % N_COL))
        return lax.ppermute(array, ("row", "col"), pairs)

    def over_z(array, k):
        return array if k == 0 else to(array, lambda z, core, c: (z ^ k, core, c))

    def over_core(array):
        return to(array, lambda z, core, c: (z, 1 - core, c))

    tiles = [shape(CAP, F, X, L)] * 4
    parts = pl.pallas_call(
        pack_in,
        out_shape=tiles,
        in_specs=[SMEM, VMEM],
        out_specs=[VMEM] * 4,
        compiler_params=PARAMS,
        name="pack_in",
    )(pos, block_cells)
    final, rows, own = pl.pallas_call(
        table,
        out_shape=[
            jax.ShapeDtypeStruct((N_ROW * 8,), jnp.int32),
            jax.ShapeDtypeStruct((N_ROW * CAP,), jnp.int32),
            tiles[0],
        ],
        in_specs=[SMEM, SMEM, ANY],
        out_specs=[SMEM, SMEM, ANY],
        input_output_aliases={2: 2},
        scratch_shapes=[pltpu.SMEM((N_ROW * 16,), jnp.int32), pltpu.SMEM((N_ROW,), jnp.int32)],
        compiler_params=PARAMS,
        cost_estimate=pl.CostEstimate(flops=0, bytes_accessed=20_000_000, transcendentals=0),
        name="table",
    )(pos, slot_blocks, parts[0])
    gathered = []
    for k in range(4):
        here = over_z(parts[k], k) if k else own
        gathered += [here, over_core(here)]

    whole = shape(F * Y * HALF, L)
    layer = shape(F * DEEP * HALF, L)
    initial, x_in, x_out, y_in, y_out = pl.pallas_call(
        reorder,
        out_shape=[whole] + [layer] * 4,
        in_specs=[SMEM, SMEM] + [VMEM] * 8,
        out_specs=[VMEM] * 5,
        scratch_shapes=[pltpu.VMEM((HALF + 1, F, X, L), jnp.float32)],
        compiler_params=PARAMS,
        name="reorder",
    )(pos, rows, *gathered)

    def x_partner(z):
        return z ^ 1

    def y_partner(z):
        return z ^ 3

    def over_x(inner, outer):
        return (
            to(inner, lambda z, core, c: (x_partner(z), core, c)),
            to(outer, lambda z, core, c: (x_partner(z), core, c + 2 * tile_x(z) - 1)),
        )

    def over_y(inner, outer):
        return (
            to(inner, lambda z, core, c: (y_partner(z), core, c)),
            to(outer, lambda z, core, c: (y_partner(z), 1 - core, c + 2 * tile_y(z) - 1)),
        )

    y_layers = over_y(y_in, y_out)
    x_layers = over_x(x_in, x_out)
    corner_cells = pl.pallas_call(
        corners,
        out_shape=[shape(F * 3 * 8, L)] * 2,
        in_specs=[SMEM, VMEM, VMEM],
        out_specs=[VMEM] * 2,
        compiler_params=PARAMS,
        name="corners",
    )(pos, *y_layers)
    corner_cells = over_x(*corner_cells)
    wide = [F * WIDE * HALF, L]
    early = pl.pallas_call(
        begin,
        out_shape=[shape(*wide)] * 6,
        in_specs=[SMEM] + [VMEM] * 5,
        out_specs=[VMEM] * 6,
        compiler_params=PARAMS,
        cost_estimate=pl.CostEstimate(flops=0, bytes_accessed=10_000_000, transcendentals=0),
        name="begin",
    )(pos, initial, *x_layers, *y_layers)
    current = pl.pallas_call(
        finish,
        out_shape=shape(HALF, F, X, L),
        in_specs=[SMEM] + [VMEM] * 8,
        out_specs=VMEM,
        scratch_shapes=[pltpu.VMEM(wide, jnp.float32)] * 5,
        compiler_params=PARAMS,
        name="finish",
    )(pos, *early, *corner_cells)

    leaving = pl.pallas_call(
        pack_out,
        out_shape=[shape(OUT, F, X, L)] * 4,
        in_specs=[SMEM, SMEM, VMEM, VMEM],
        out_specs=[VMEM] * 4,
        compiler_params=PARAMS,
        name="pack_out",
    )(pos, final, current, over_core(current))
    arrived = [over_z(leaving[k], k) for k in range(4)]
    result = []
    for which in ((0,), (2, 1, 3)):
        n = len(which)
        result = [
            pl.pallas_call(
                lambda *refs, which=which: unpack_out(which, *refs),
                out_shape=shape(OUT, F, 2 * X, 2 * L),
                in_specs=[SMEM] + [ANY] * (n + len(result)),
                out_specs=ANY,
                input_output_aliases={n + 1: 0} if result else {},
                scratch_shapes=[pltpu.SemaphoreType.DMA((n,))],
                compiler_params=PARAMS,
                name="unpack_out",
            )(pos, *[arrived[k] for k in which], *result)
        ]
    return result[0]


def solution(mesh):
    in_specs = (P(("row", "col"), None, None, None), P())
    out_specs = P(("row", "col"), None, None, None)
    return jax.shard_map(body, mesh=mesh, in_specs=in_specs, out_specs=out_specs, check_vma=False)
```

```python
import math

import jax
import jax.numpy as jnp
from jax import lax
from jax.experimental import pallas as pl
from jax.experimental.pallas import tpu as pltpu
from jax.sharding import PartitionSpec as P

CAP = 11
OUT = 7
NBY = 48
N_ROW = 8
N_COL = 16
HALF = NBY // 2
F = 5
X = Y = 8
L = 128
DEEP = 3
WIDE = Y + 2 * DEEP
ORDER = (0, 2, 1, 3)

GAMMA = 1.4
STEP = 0.12
LOG2_E = 1.0 / math.log(2.0)

VMEM = pl.BlockSpec(memory_space=pltpu.VMEM)
SMEM = pl.BlockSpec(memory_space=pltpu.SMEM)
ANY = pl.BlockSpec(memory_space=pl.ANY)
PARAMS = pltpu.CompilerParams(vmem_limit_bytes=24 * 1024 * 1024)


def shape(*dims):
    return jax.ShapeDtypeStruct(dims, jnp.float32)


def tile_x(z):
    return ((z + 1) // 2) % 2


def tile_y(z):
    return z // 2


def pack_in(pos, cells, *outs):
    z = pos[0]
    for k in range(4):
        x = pl.ds(pl.multiple_of(tile_x(z ^ k) * X, X), X)
        y = pl.ds(pl.multiple_of(tile_y(z ^ k) * L, L), L)
        for s in range(CAP):
            for f in range(F):
                outs[k][s, f] = cells[s, f, x, y]


def unpack_out(which, pos, *refs):
    out, sems = refs[-2:]
    z = pos[0]
    copies = []
    for i, k in enumerate(which):
        x = pl.ds(pl.multiple_of(tile_x(z ^ k) * X, X), X)
        y = pl.ds(pl.multiple_of(tile_y(z ^ k) * L, L), L)
        copies.append(pltpu.make_async_copy(refs[i], out.at[:, :, x, y], sems.at[i]))
    for c in copies:
        c.start()
    for c in copies:
        c.wait()


def table(pos, slots, _tile, final, rows, _same, held, count):
    z, core, g = pos[0], pos[1], pos[2]
    for d in range(N_ROW):
        n = jnp.int32(0)
        place = ((z ^ d // 2) * 2 + (core ^ d % 2)) * CAP
        for s in range(CAP):
            b = slots[d * N_COL + g, s]
            j = b - g * NBY
            held[d * 16 + s] = j
            here = jnp.logical_and(b >= 0, (j & 1) == core)
            rows[place + s] = jnp.where(here, j >> 1, HALF)
            n = n + jnp.where(b >= 0, 1, 0)
        count[d] = n
    for bit in range(3):
        for low in range(N_ROW):
            if low >> bit & 1:
                continue
            high = low | 1 << bit
            a, b = count[low], count[high]
            up = a > b
            src = jnp.where(up, low, high)
            dst = jnp.where(up, high, low)
            n_src = jnp.maximum(a, b)
            n_dst = jnp.minimum(a, b)
            moved = (n_src - n_dst) // 2

            def move(i, _, src=src, dst=dst, n_src=n_src, n_dst=n_dst, moved=moved):
                held[dst * 16 + n_dst + i] = held[src * 16 + n_src - moved + i]
                return 0

            lax.fori_loop(0, moved, move, 0)
            count[src] = n_src - moved
            count[dst] = n_dst + moved
    for d in range(N_ROW):
        n = count[d]
        for s in range(8):
            final[d * 8 + s] = jnp.where(s < n, held[d * 16 + s], -1)


def rolled(v, shift):
    shift %= L
    return v if shift == 0 else pltpu.roll(v, shift, 1)


def inverse(rho):
    guess = pl.reciprocal(rho, approx=True)
    return guess * (2.0 - rho * guess)


def terms(cons):
    rho, mx, my, mz, energy = cons
    inv = inverse(rho)
    u, v, w = mx * inv, my * inv, mz * inv
    p = (GAMMA - 1.0) * energy - (0.5 * (GAMMA - 1.0)) * (mx * u + my * v + mz * w)
    theta = p * inv
    power = jnp.log(theta)
    sound = jnp.exp2(power * (0.5 * LOG2_E) + 0.5 * math.log2(GAMMA))
    kappa = jnp.exp2(power * (0.7 * LOG2_E) + math.log2(0.2))
    return (u, v, w), p, theta, sound, kappa


def side(cons, t, n):
    vel, p, theta, sound, kappa = t
    flux = [cons[f] * vel[n] for f in (1, 2, 3)]
    flux[n] = flux[n] + p
    return (*cons, *flux, (cons[4] + p) * vel[n], theta, kappa, jnp.abs(vel[n]) + sound)


def double_flux(low, high, n):
    speed = jnp.maximum(low[11], high[11])
    out = []
    for f in range(F):
        k = F + f - 1 if f else n + 1
        out.append((low[k] + high[k]) - speed * (high[f] - low[f]))
    out[4] = out[4] - (low[10] + high[10]) * (high[9] - low[9])
    return out


def primitive(cons):
    rho, mx, my, mz, energy = cons
    inv = inverse(rho)
    u, v, w = mx * inv, my * inv, mz * inv
    return [rho, u, v, w, (GAMMA - 1.0) * (energy - 0.5 * rho * (u * u + v * v + w * w))]


def conserved(prim):
    rho, u, v, w, p = prim
    return [rho, rho * u, rho * v, rho * w, p * (1.0 / (GAMMA - 1.0)) + 0.5 * rho * (u * u + v * v + w * w)]


def at(f, y, group):
    return pl.ds(pl.multiple_of((f * Y + y) * HALF + group * 8, 8), 8)


def wide_at(f, y, group):
    return pl.ds(pl.multiple_of((f * WIDE + DEEP + y) * HALF + group * 8, 8), 8)


def strip_at(f, t, group):
    return pl.ds(pl.multiple_of((f * DEEP + t) * HALF + group * 8, 8), 8)


def x_layer_at(f, group, x):
    return pl.ds(f * Y * HALF + group * 8 + x, Y, HALF)


def transposed(vectors):
    place = lax.broadcasted_iota(jnp.int32, (8, L), 1) // 16
    vectors = list(vectors)
    for bit in (1, 2, 4):
        clear = (place & bit) == 0
        for i in range(8):
            if i & bit:
                continue
            a, b = vectors[i], vectors[i | bit]
            vectors[i] = jnp.where(clear, a, rolled(b, 16 * bit))
            vectors[i | bit] = jnp.where(clear, rolled(a, -16 * bit), b)
    return vectors


def faces(pos, cur, x_in, x_out, y_in, y_out):
    zx, zy, core = tile_x(pos[0]), tile_y(pos[0]), pos[1]
    place = lax.broadcasted_iota(jnp.int32, (8, L), 1) // 16
    first = jnp.full((8, L), zy, jnp.int32) == 0
    turn = jnp.full((8, L), jnp.where(core == zy, 1, 0), jnp.int32) == 1
    far = Y - DEEP
    for f in range(F):
        for t in range(DEEP):
            ahead, back = [], []
            for group in range(3):
                to = pl.ds(((f * 3 + group) * DEEP + t) * 8, 8)
                x_in[to, :] = cur[x_layer_at(f, group, far * (1 - zx) + t), :]
                x_out[to, :] = cur[x_layer_at(f, group, far * zx + t), :]
                y_in[strip_at(f, t, group), :] = cur[at(f, far * (1 - zy) + t, group), :]
                v = cur[at(f, far * zy + t, group), :]
                ahead.append(rolled(v, 16))
                back.append(rolled(v, -16))
            for group in range(3):
                high = jnp.where(place == 0, ahead[group - 1], ahead[group])
                low = jnp.where(place == 7, back[(group + 1) % 3], back[group])
                v = cur[at(f, far * zy + t, group), :]
                y_out[strip_at(f, t, group), :] = jnp.where(turn, jnp.where(first, low, high), v)


def corners(pos, y_in, y_out, to_in, to_out):
    zx, zy = tile_x(pos[0]), tile_y(pos[0])

    def copy(low, high):
        for f in range(F):
            for group in range(3):
                for r in range(2):
                    for out, x in ((to_in, 6 * (1 - zx) + r), (to_out, 6 * zx + r)):
                        row = ((f * 3 + group) * 2 + r) * 4
                        base = f * DEEP * HALF + group * 8 + x
                        out[row : row + 2, :] = low[pl.ds(base + HALF, 2, HALF), :]
                        out[row + 2 : row + 4, :] = high[pl.ds(base, 2, HALF), :]

    @pl.when(zy == 0)
    def _():
        copy(y_out, y_in)

    @pl.when(zy == 1)
    def _():
        copy(y_in, y_out)


def reorder(pos, rows, *refs):
    parts = refs[:8]
    cur, x_in, x_out, y_in, y_out = refs[8:13]
    held = refs[13]
    for i in range(8):
        for s in range(CAP):
            held[rows[(ORDER[i // 2] * 2 + i % 2) * CAP + s]] = parts[i][s]

    def convert(group, _):
        for f in range(F):
            vectors = [held[group * 8 + i, f] for i in range(8)]
            for y, v in enumerate(transposed(vectors)):
                cur[at(f, y, group), :] = v
        for y in range(Y):
            prim = [cur[at(f, y, group), :] for f in range(F)]
            for f, v in enumerate(conserved(prim)):
                if f:
                    cur[at(f, y, group), :] = v
        return 0

    lax.fori_loop(0, 3, convert, 0)
    faces(pos, cur, x_in, x_out, y_in, y_out)


def widen(pos, cur, x_in, x_out, y_in, y_out, main, side_rows):
    zx, zy = tile_x(pos[0]), tile_y(pos[0])
    for f in range(F):
        for group in range(3):
            for y in range(Y):
                main[wide_at(f, y, group), :] = cur[at(f, y, group), :]
            for t in range(DEEP):
                main[wide_at(f, Y * (1 - zy) - DEEP * zy + t, group), :] = y_in[strip_at(f, t, group), :]
                main[wide_at(f, Y * zy - DEEP * (1 - zy) + t, group), :] = y_out[strip_at(f, t, group), :]
                at_t = pl.ds(((f * 3 + group) * DEEP + t) * 8, 8)
                base = (f * WIDE + DEEP) * HALF + group * 8 + t
                side_rows[pl.ds(base + 5 * zx, 8, HALF), :] = x_in[at_t, :]
                side_rows[pl.ds(base + 5 * (1 - zx), 8, HALF), :] = x_out[at_t, :]


def add_corners(pos, c_in, c_out, side_rows):
    zx = tile_x(pos[0])
    for f in range(F):
        for group in range(3):
            for r in range(2):
                row = ((f * 3 + group) * 2 + r) * 4
                for c, beyond in ((c_in, 6 * zx), (c_out, 6 * (1 - zx))):
                    for k, y in ((0, -2), (2, Y)):
                        to = (f * WIDE + DEEP + y) * HALF + group * 8 + r + beyond
                        side_rows[pl.ds(to, 2, HALF), :] = c[row + k : row + k + 2, :]


def advance(number, source, initial, target, main_ys, side_ys, made=None):
    weight = (0.0, 0.75, 1.0 / 3.0)[number]

    def step(group, _):
        height = lax.broadcasted_iota(jnp.int32, (8, L), 1) % 16
        sub = lax.broadcasted_iota(jnp.int32, (8, L), 0)
        floor, roof = height == 0, height == 15
        left, right = sub == 0, sub == 7
        cells, fluxes = {}, {}

        def cell(part, y):
            if (part, y) not in cells:
                cons = [source(part, y)[wide_at(f, y, group), :] for f in range(F)]
                cells[part, y] = cons, terms(cons)
            return cells[part, y]

        def flux_y(part, y):
            if (part, y) not in fluxes:
                fluxes[part, y] = double_flux(side(*cell(part, y), 1), side(*cell(part, y + 1), 1), 1)
            return fluxes[part, y]

        for y in sorted({*main_ys, *side_ys}):
            own = [side(*cell(part, y), 0) for part in range(2)]
            turned = [[pltpu.roll(q, 7, 0) for q in o] for o in own]
            flux = []
            for part in range(2):
                ahead = [jnp.where(right, q, p) for p, q in zip(turned[part], turned[1 - part])]
                flux.append(double_flux(own[part], ahead, 0))
            turned = [[pltpu.roll(q, 1, 0) for q in o] for o in flux]
            for part, ys in enumerate((main_ys, side_ys)):
                if y not in ys:
                    continue
                cons, t = cell(part, y)
                change = [
                    v - jnp.where(left, q, p) for v, p, q in zip(flux[part], turned[part], turned[1 - part])
                ]
                change = [c + (b - a) for c, a, b in zip(change, flux_y(part, y - 1), flux_y(part, y))]
                low = side(cons, t, 2)
                up = [rolled(q, -1) for q in cons]
                flux_z = double_flux(low, side(up, terms(up), 2), 2)
                for f in range(F):
                    upper = jnp.where(roof, 2.0 * t[1] if f == 3 else 0.0, flux_z[f])
                    lower = rolled(upper, 1)
                    if f == 3:
                        lower = jnp.where(floor, 2.0 * t[1], lower)
                    change[f] = change[f] + (upper - lower)
                out = [c - (0.5 * STEP) * d for c, d in zip(cons, change)]
                if number:
                    out = [
                        weight * initial(part, y)[wide_at(f, y, group), :] + (1.0 - weight) * o
                        for f, o in enumerate(out)
                    ]
                if number == 2:
                    out = primitive(out)
                for f in range(F):
                    target(part, y)[wide_at(f, y, group), :] = out[f]
        if number == 2:
            for f in range(F):
                vectors = [target(0, y)[wide_at(f, y, group), :] for y in range(Y)]
                for i, v in enumerate(transposed(vectors)):
                    made[group * 8 + i, f] = v
        return 0

    lax.fori_loop(0, 3, step, 0)


EARLY = ((range(0, Y), range(1, Y - 1)), (range(1, Y - 1), range(2, Y - 2)))


def begin(pos, cur, x_in, x_out, y_in, y_out, main, side_rows, *made):
    widen(pos, cur, x_in, x_out, y_in, y_out, main, side_rows)
    initial = (main, side_rows)
    advance(0, lambda part, y: initial[part], None, lambda part, y: made[part], *EARLY[0])
    advance(1, lambda part, y: made[part], lambda part, y: initial[part], lambda part, y: made[2 + part], *EARLY[1])


def finish(pos, main, side_rows, *refs):
    early, (c_in, c_out, made, corner_rows), late = refs[:4], refs[4:8], refs[8:12]
    add_corners(pos, c_in, c_out, corner_rows)

    def initial(part, y):
        return (side_rows if 0 <= y < Y else corner_rows) if part else main

    def first(part, y):
        return (early if y in EARLY[0][part] else late)[part]

    def second(part, y):
        return (early if y in EARLY[1][part] else late)[2 + part]

    advance(0, initial, None, first, (-2, -1, Y, Y + 1), (-1, 0, Y - 1, Y))
    advance(1, first, initial, second, (-1, 0, Y - 1, Y), (0, 1, Y - 2, Y - 1))
    advance(2, second, initial, lambda part, y: late[part], range(0, Y), (), made)


def pack_out(pos, final, mine, other, *outs):
    z, core = pos[0], pos[1]
    for k in range(4):
        d = (z ^ k) * 2 + core
        for s in range(OUT):
            j = final[d * 8 + s]
            row = jnp.maximum(j, 0) >> 1
            kind = jnp.full((X, L), jnp.where(j < 0, 2, (j & 1) ^ core), jnp.int32)
            for f in range(F):
                outs[k][s, f] = jnp.where(kind == 0, mine[row, f], jnp.where(kind == 1, other[row, f], 0.0))


def body(block_cells, slot_blocks):
    row, col = lax.axis_index("row"), lax.axis_index("col")
    pos = jnp.stack([row // 2, row % 2, col]).astype(jnp.int32)

    def to(array, route):
        pairs = []
        for r in range(N_ROW):
            for c in range(N_COL):
                z, core, c2 = route(r // 2, r % 2, c)
                pairs.append((r * N_COL + c, (z * 2 + core) * N_COL + c2 % N_COL))
        return lax.ppermute(array, ("row", "col"), pairs)

    def over_z(array, k):
        return array if k == 0 else to(array, lambda z, core, c: (z ^ k, core, c))

    def over_core(array):
        return to(array, lambda z, core, c: (z, 1 - core, c))

    tiles = [shape(CAP, F, X, L)] * 4
    parts = pl.pallas_call(
        pack_in,
        out_shape=tiles,
        in_specs=[SMEM, VMEM],
        out_specs=[VMEM] * 4,
        compiler_params=PARAMS,
        name="pack_in",
    )(pos, block_cells)
    final, rows, own = pl.pallas_call(
        table,
        out_shape=[
            jax.ShapeDtypeStruct((N_ROW * 8,), jnp.int32),
            jax.ShapeDtypeStruct((N_ROW * CAP,), jnp.int32),
            tiles[0],
        ],
        in_specs=[SMEM, SMEM, ANY],
        out_specs=[SMEM, SMEM, ANY],
        input_output_aliases={2: 2},
        scratch_shapes=[pltpu.SMEM((N_ROW * 16,), jnp.int32), pltpu.SMEM((N_ROW,), jnp.int32)],
        compiler_params=PARAMS,
        cost_estimate=pl.CostEstimate(flops=0, bytes_accessed=20_000_000, transcendentals=0),
        name="table",
    )(pos, slot_blocks, parts[0])
    gathered = []
    for k in ORDER:
        here = over_z(parts[k], k) if k else own
        gathered += [here, over_core(here)]

    whole = shape(F * Y * HALF, L)
    layer = shape(F * DEEP * HALF, L)
    initial, x_in, x_out, y_in, y_out = pl.pallas_call(
        reorder,
        out_shape=[whole] + [layer] * 4,
        in_specs=[SMEM, SMEM] + [VMEM] * 8,
        out_specs=[VMEM] * 5,
        scratch_shapes=[pltpu.VMEM((HALF + 1, F, X, L), jnp.float32)],
        compiler_params=PARAMS,
        name="reorder",
    )(pos, rows, *gathered)

    def x_partner(z):
        return z ^ 1

    def y_partner(z):
        return z ^ 3

    def over_x(inner, outer):
        return (
            to(inner, lambda z, core, c: (x_partner(z), core, c)),
            to(outer, lambda z, core, c: (x_partner(z), core, c + 2 * tile_x(z) - 1)),
        )

    def over_y(inner, outer):
        return (
            to(inner, lambda z, core, c: (y_partner(z), core, c)),
            to(outer, lambda z, core, c: (y_partner(z), 1 - core, c + 2 * tile_y(z) - 1)),
        )

    y_layers = over_y(y_in, y_out)
    x_layers = over_x(x_in, x_out)
    corner_cells = pl.pallas_call(
        corners,
        out_shape=[shape(F * 3 * 8, L)] * 2,
        in_specs=[SMEM, VMEM, VMEM],
        out_specs=[VMEM] * 2,
        compiler_params=PARAMS,
        name="corners",
    )(pos, *y_layers)
    corner_cells = over_x(*corner_cells)
    wide = [F * WIDE * HALF, L]
    early = pl.pallas_call(
        begin,
        out_shape=[shape(*wide)] * 6,
        in_specs=[SMEM] + [VMEM] * 5,
        out_specs=[VMEM] * 6,
        compiler_params=PARAMS,
        cost_estimate=pl.CostEstimate(flops=0, bytes_accessed=10_000_000, transcendentals=0),
        name="begin",
    )(pos, initial, *x_layers, *y_layers)
    current = pl.pallas_call(
        finish,
        out_shape=shape(HALF, F, X, L),
        in_specs=[SMEM] + [VMEM] * 8,
        out_specs=VMEM,
        scratch_shapes=[pltpu.VMEM(wide, jnp.float32)] * 5,
        compiler_params=PARAMS,
        name="finish",
    )(pos, *early, *corner_cells)

    leaving = pl.pallas_call(
        pack_out,
        out_shape=[shape(OUT, F, X, L)] * 4,
        in_specs=[SMEM, SMEM, VMEM, VMEM],
        out_specs=[VMEM] * 4,
        compiler_params=PARAMS,
        name="pack_out",
    )(pos, final, current, over_core(current))
    arrived = [over_z(leaving[k], k) for k in range(4)]
    result = []
    for which in ((0,), (2, 1, 3)):
        n = len(which)
        result = [
            pl.pallas_call(
                lambda *refs, which=which: unpack_out(which, *refs),
                out_shape=shape(OUT, F, 2 * X, 2 * L),
                in_specs=[SMEM] + [ANY] * (n + len(result)),
                out_specs=ANY,
                input_output_aliases={n + 1: 0} if result else {},
                scratch_shapes=[pltpu.SemaphoreType.DMA((n,))],
                compiler_params=PARAMS,
                name="unpack_out",
            )(pos, *[arrived[k] for k in which], *result)
        ]
    return result[0]


def solution(mesh):
    in_specs = (P(("row", "col"), None, None, None), P())
    out_specs = P(("row", "col"), None, None, None)
    return jax.shard_map(body, mesh=mesh, in_specs=in_specs, out_specs=out_specs, check_vma=False)
```

```python
import math

import jax
import jax.numpy as jnp
from jax import lax
from jax.experimental import pallas as pl
from jax.experimental.pallas import tpu as pltpu
from jax.sharding import PartitionSpec as P

CAP = 11
OUT = 7
NBY = 48
N_ROW = 8
N_COL = 16
HALF = NBY // 2
F = 5
X = Y = 8
L = 128
DEEP = 3
WIDE = Y + 2 * DEEP
ORDER = (0, 2, 1, 3)

GAMMA = 1.4
STEP = 0.12
LOG2_E = 1.0 / math.log(2.0)

VMEM = pl.BlockSpec(memory_space=pltpu.VMEM)
SMEM = pl.BlockSpec(memory_space=pltpu.SMEM)
ANY = pl.BlockSpec(memory_space=pl.ANY)
PARAMS = pltpu.CompilerParams(vmem_limit_bytes=24 * 1024 * 1024)


def shape(*dims):
    return jax.ShapeDtypeStruct(dims, jnp.float32)


def tile_x(z):
    return ((z + 1) // 2) % 2


def tile_y(z):
    return z // 2


def pack_in(pos, cells, *outs):
    z = pos[0]
    for k in range(4):
        x = pl.ds(pl.multiple_of(tile_x(z ^ k) * X, X), X)
        y = pl.ds(pl.multiple_of(tile_y(z ^ k) * L, L), L)
        for s in range(CAP):
            for f in range(F):
                outs[k][s, f] = cells[s, f, x, y]


def unpack_out(which, pos, *refs):
    out, sems = refs[-2:]
    z = pos[0]
    copies = []
    for i, k in enumerate(which):
        x = pl.ds(pl.multiple_of(tile_x(z ^ k) * X, X), X)
        y = pl.ds(pl.multiple_of(tile_y(z ^ k) * L, L), L)
        copies.append(pltpu.make_async_copy(refs[i], out.at[:, :, x, y], sems.at[i]))
    for c in copies:
        c.start()
    for c in copies:
        c.wait()


def table(pos, slots, _tile, final, rows, _same, held, count):
    z, core, g = pos[0], pos[1], pos[2]
    for d in range(N_ROW):
        n = jnp.int32(0)
        place = ((z ^ d // 2) * 2 + (core ^ d % 2)) * CAP
        for s in range(CAP):
            b = slots[d * N_COL + g, s]
            j = b - g * NBY
            held[d * 16 + s] = j
            here = jnp.logical_and(b >= 0, (j & 1) == core)
            rows[place + s] = jnp.where(here, j >> 1, HALF)
            n = n + jnp.where(b >= 0, 1, 0)
        count[d] = n
    for bit in range(3):
        for low in range(N_ROW):
            if low >> bit & 1:
                continue
            high = low | 1 << bit
            a, b = count[low], count[high]
            up = a > b
            src = jnp.where(up, low, high)
            dst = jnp.where(up, high, low)
            n_src = jnp.maximum(a, b)
            n_dst = jnp.minimum(a, b)
            moved = (n_src - n_dst) // 2

            def move(i, _, src=src, dst=dst, n_src=n_src, n_dst=n_dst, moved=moved):
                held[dst * 16 + n_dst + i] = held[src * 16 + n_src - moved + i]
                return 0

            lax.fori_loop(0, moved, move, 0)
            count[src] = n_src - moved
            count[dst] = n_dst + moved
    for d in range(N_ROW):
        n = count[d]
        for s in range(8):
            final[d * 8 + s] = jnp.where(s < n, held[d * 16 + s], -1)


def rolled(v, shift):
    shift %= L
    return v if shift == 0 else pltpu.roll(v, shift, 1)


def inverse(rho):
    guess = pl.reciprocal(rho, approx=True)
    return guess * (2.0 - rho * guess)


def terms(cons):
    rho, mx, my, mz, energy = cons
    inv = inverse(rho)
    u, v, w = mx * inv, my * inv, mz * inv
    p = (GAMMA - 1.0) * energy - (0.5 * (GAMMA - 1.0)) * (mx * u + my * v + mz * w)
    theta = p * inv
    power = jnp.log(theta)
    sound = jnp.exp2(power * (0.5 * LOG2_E) + 0.5 * math.log2(GAMMA))
    kappa = jnp.exp2(power * (0.7 * LOG2_E) + math.log2(0.2))
    return (u, v, w), p, theta, sound, kappa


def side(cons, t, n):
    vel, p, theta, sound, kappa = t
    flux = [cons[f] * vel[n] for f in (1, 2, 3)]
    flux[n] = flux[n] + p
    return (*cons, *flux, (cons[4] + p) * vel[n], theta, kappa, jnp.abs(vel[n]) + sound)


def double_flux(low, high, n):
    speed = jnp.maximum(low[11], high[11])
    out = []
    for f in range(F):
        k = F + f - 1 if f else n + 1
        out.append((low[k] + high[k]) - speed * (high[f] - low[f]))
    out[4] = out[4] - (low[10] + high[10]) * (high[9] - low[9])
    return out


def primitive(cons):
    rho, mx, my, mz, energy = cons
    inv = inverse(rho)
    u, v, w = mx * inv, my * inv, mz * inv
    return [rho, u, v, w, (GAMMA - 1.0) * (energy - 0.5 * rho * (u * u + v * v + w * w))]


def conserved(prim):
    rho, u, v, w, p = prim
    return [rho, rho * u, rho * v, rho * w, p * (1.0 / (GAMMA - 1.0)) + 0.5 * rho * (u * u + v * v + w * w)]


def at(f, y, group):
    return pl.ds(pl.multiple_of((f * Y + y) * HALF + group * 8, 8), 8)


def wide_at(f, y, group):
    return pl.ds(pl.multiple_of((f * WIDE + DEEP + y) * HALF + group * 8, 8), 8)


def strip_at(f, t, group):
    return pl.ds(pl.multiple_of((f * DEEP + t) * HALF + group * 8, 8), 8)


def x_layer_at(f, group, x):
    return pl.ds(f * Y * HALF + group * 8 + x, Y, HALF)


def transposed(vectors):
    place = lax.broadcasted_iota(jnp.int32, (8, L), 1) // 16
    vectors = list(vectors)
    for bit in (1, 2, 4):
        clear = (place & bit) == 0
        for i in range(8):
            if i & bit:
                continue
            a, b = vectors[i], vectors[i | bit]
            vectors[i] = jnp.where(clear, a, rolled(b, 16 * bit))
            vectors[i | bit] = jnp.where(clear, rolled(a, -16 * bit), b)
    return vectors


def faces(pos, cur, x_in, x_out, y_in, y_out):
    zx, zy, core = tile_x(pos[0]), tile_y(pos[0]), pos[1]
    place = lax.broadcasted_iota(jnp.int32, (8, L), 1) // 16
    first = jnp.full((8, L), zy, jnp.int32) == 0
    turn = jnp.full((8, L), jnp.where(core == zy, 1, 0), jnp.int32) == 1
    far = Y - DEEP
    for f in range(F):
        for t in range(DEEP):
            ahead, back = [], []
            for group in range(3):
                to = pl.ds(((f * 3 + group) * DEEP + t) * 8, 8)
                x_in[to, :] = cur[x_layer_at(f, group, far * (1 - zx) + t), :]
                x_out[to, :] = cur[x_layer_at(f, group, far * zx + t), :]
                y_in[strip_at(f, t, group), :] = cur[at(f, far * (1 - zy) + t, group), :]
                v = cur[at(f, far * zy + t, group), :]
                ahead.append(rolled(v, 16))
                back.append(rolled(v, -16))
            for group in range(3):
                high = jnp.where(place == 0, ahead[group - 1], ahead[group])
                low = jnp.where(place == 7, back[(group + 1) % 3], back[group])
                v = cur[at(f, far * zy + t, group), :]
                y_out[strip_at(f, t, group), :] = jnp.where(turn, jnp.where(first, low, high), v)


def corners(pos, y_in, y_out, to_in, to_out):
    zx, zy = tile_x(pos[0]), tile_y(pos[0])

    def copy(low, high):
        for f in range(F):
            for group in range(3):
                for r in range(2):
                    for out, x in ((to_in, 6 * (1 - zx) + r), (to_out, 6 * zx + r)):
                        row = ((f * 3 + group) * 2 + r) * 4
                        base = f * DEEP * HALF + group * 8 + x
                        out[row : row + 2, :] = low[pl.ds(base + HALF, 2, HALF), :]
                        out[row + 2 : row + 4, :] = high[pl.ds(base, 2, HALF), :]

    @pl.when(zy == 0)
    def _():
        copy(y_out, y_in)

    @pl.when(zy == 1)
    def _():
        copy(y_in, y_out)


def reorder(pos, rows, *refs):
    parts = refs[:8]
    cur, x_in, x_out, y_in, y_out = refs[8:13]
    held = refs[13]
    for i in range(8):
        for s in range(CAP):
            held[rows[(ORDER[i // 2] * 2 + i % 2) * CAP + s]] = parts[i][s]

    def convert(group, _):
        for f in range(F):
            vectors = [held[group * 8 + i, f] for i in range(8)]
            for y, v in enumerate(transposed(vectors)):
                cur[at(f, y, group), :] = v
        for y in range(Y):
            prim = [cur[at(f, y, group), :] for f in range(F)]
            for f, v in enumerate(conserved(prim)):
                if f:
                    cur[at(f, y, group), :] = v
        return 0

    lax.fori_loop(0, 3, convert, 0)
    faces(pos, cur, x_in, x_out, y_in, y_out)


def widen(pos, cur, x_in, x_out, y_in, y_out, main, side_rows):
    zx, zy = tile_x(pos[0]), tile_y(pos[0])
    for f in range(F):
        for group in range(3):
            for y in range(Y):
                main[wide_at(f, y, group), :] = cur[at(f, y, group), :]
            for t in range(DEEP):
                main[wide_at(f, Y * (1 - zy) - DEEP * zy + t, group), :] = y_in[strip_at(f, t, group), :]
                main[wide_at(f, Y * zy - DEEP * (1 - zy) + t, group), :] = y_out[strip_at(f, t, group), :]
                at_t = pl.ds(((f * 3 + group) * DEEP + t) * 8, 8)
                base = (f * WIDE + DEEP) * HALF + group * 8 + t
                side_rows[pl.ds(base + 5 * zx, 8, HALF), :] = x_in[at_t, :]
                side_rows[pl.ds(base + 5 * (1 - zx), 8, HALF), :] = x_out[at_t, :]


def add_corners(pos, c_in, c_out, side_rows):
    zx = tile_x(pos[0])
    for f in range(F):
        for group in range(3):
            for r in range(2):
                row = ((f * 3 + group) * 2 + r) * 4
                for c, beyond in ((c_in, 6 * zx), (c_out, 6 * (1 - zx))):
                    for k, y in ((0, -2), (2, Y)):
                        to = (f * WIDE + DEEP + y) * HALF + group * 8 + r + beyond
                        side_rows[pl.ds(to, 2, HALF), :] = c[row + k : row + k + 2, :]


def advance(number, source, initial, target, main_ys, side_ys, made=None):
    weight = (0.0, 0.75, 1.0 / 3.0)[number]

    def step(group, _):
        height = lax.broadcasted_iota(jnp.int32, (8, L), 1) % 16
        sub = lax.broadcasted_iota(jnp.int32, (8, L), 0)
        floor, roof = height == 0, height == 15
        left, right = sub == 0, sub == 7
        cells, fluxes = {}, {}

        def cell(part, y):
            if (part, y) not in cells:
                cons = [source(part, y)[wide_at(f, y, group), :] for f in range(F)]
                cells[part, y] = cons, terms(cons)
            return cells[part, y]

        def flux_y(part, y):
            if (part, y) not in fluxes:
                fluxes[part, y] = double_flux(side(*cell(part, y), 1), side(*cell(part, y + 1), 1), 1)
            return fluxes[part, y]

        for y in sorted({*main_ys, *side_ys}):
            own = [side(*cell(part, y), 0) for part in range(2)]
            turned = [[pltpu.roll(q, 7, 0) for q in o] for o in own]
            flux = []
            for part in range(2):
                ahead = [jnp.where(right, q, p) for p, q in zip(turned[part], turned[1 - part])]
                flux.append(double_flux(own[part], ahead, 0))
            turned = [[pltpu.roll(q, 1, 0) for q in o] for o in flux]
            for part, ys in enumerate((main_ys, side_ys)):
                if y not in ys:
                    continue
                cons, t = cell(part, y)
                change = [
                    v - jnp.where(left, q, p) for v, p, q in zip(flux[part], turned[part], turned[1 - part])
                ]
                change = [c + (b - a) for c, a, b in zip(change, flux_y(part, y - 1), flux_y(part, y))]
                low = side(cons, t, 2)
                up = [rolled(q, -1) for q in cons]
                flux_z = double_flux(low, side(up, terms(up), 2), 2)
                for f in range(F):
                    upper = jnp.where(roof, 2.0 * t[1] if f == 3 else 0.0, flux_z[f])
                    lower = rolled(upper, 1)
                    if f == 3:
                        lower = jnp.where(floor, 2.0 * t[1], lower)
                    change[f] = change[f] + (upper - lower)
                out = [c - (0.5 * STEP) * d for c, d in zip(cons, change)]
                if number:
                    out = [
                        weight * initial(part, y)[wide_at(f, y, group), :] + (1.0 - weight) * o
                        for f, o in enumerate(out)
                    ]
                if number == 2:
                    out = primitive(out)
                for f in range(F):
                    target(part, y)[wide_at(f, y, group), :] = out[f]
        if number == 2:
            for f in range(F):
                vectors = [target(0, y)[wide_at(f, y, group), :] for y in range(Y)]
                for i, v in enumerate(transposed(vectors)):
                    made[group * 8 + i, f] = v
        return 0

    lax.fori_loop(0, 3, step, 0)


EARLY = ((range(0, Y), range(1, Y - 1)), (range(1, Y - 1), range(2, Y - 2)))


def begin(pos, cur, x_in, x_out, y_in, y_out, main, side_rows, *made):
    widen(pos, cur, x_in, x_out, y_in, y_out, main, side_rows)
    initial = (main, side_rows)
    advance(0, lambda part, y: initial[part], None, lambda part, y: made[part], *EARLY[0])
    advance(1, lambda part, y: made[part], lambda part, y: initial[part], lambda part, y: made[2 + part], *EARLY[1])


def finish(pos, main, side_rows, *refs):
    early, (c_out, c_in, made, corner_rows), late = refs[:4], refs[4:8], refs[8:12]
    add_corners(pos, c_in, c_out, corner_rows)

    def initial(part, y):
        return (side_rows if 0 <= y < Y else corner_rows) if part else main

    def first(part, y):
        return (early if y in EARLY[0][part] else late)[part]

    def second(part, y):
        return (early if y in EARLY[1][part] else late)[2 + part]

    advance(0, initial, None, first, (-2, -1, Y, Y + 1), (-1, 0, Y - 1, Y))
    advance(1, first, initial, second, (-1, 0, Y - 1, Y), (0, 1, Y - 2, Y - 1))
    advance(2, second, initial, lambda part, y: late[part], range(0, Y), (), made)


def pack_out(pos, final, mine, other, *outs):
    z, core = pos[0], pos[1]
    for k in range(4):
        d = (z ^ k) * 2 + core
        for s in range(OUT):
            j = final[d * 8 + s]
            row = jnp.maximum(j, 0) >> 1
            kind = jnp.full((X, L), jnp.where(j < 0, 2, (j & 1) ^ core), jnp.int32)
            for f in range(F):
                outs[k][s, f] = jnp.where(kind == 0, mine[row, f], jnp.where(kind == 1, other[row, f], 0.0))


def body(block_cells, slot_blocks):
    row, col = lax.axis_index("row"), lax.axis_index("col")
    pos = jnp.stack([row // 2, row % 2, col]).astype(jnp.int32)

    def to(array, route):
        pairs = []
        for r in range(N_ROW):
            for c in range(N_COL):
                z, core, c2 = route(r // 2, r % 2, c)
                pairs.append((r * N_COL + c, (z * 2 + core) * N_COL + c2 % N_COL))
        return lax.ppermute(array, ("row", "col"), pairs)

    def over_z(array, k):
        return array if k == 0 else to(array, lambda z, core, c: (z ^ k, core, c))

    def over_core(array):
        return to(array, lambda z, core, c: (z, 1 - core, c))

    tiles = [shape(CAP, F, X, L)] * 4
    parts = pl.pallas_call(
        pack_in,
        out_shape=tiles,
        in_specs=[SMEM, VMEM],
        out_specs=[VMEM] * 4,
        compiler_params=PARAMS,
        name="pack_in",
    )(pos, block_cells)
    final, rows, own = pl.pallas_call(
        table,
        out_shape=[
            jax.ShapeDtypeStruct((N_ROW * 8,), jnp.int32),
            jax.ShapeDtypeStruct((N_ROW * CAP,), jnp.int32),
            tiles[0],
        ],
        in_specs=[SMEM, SMEM, ANY],
        out_specs=[SMEM, SMEM, ANY],
        input_output_aliases={2: 2},
        scratch_shapes=[pltpu.SMEM((N_ROW * 16,), jnp.int32), pltpu.SMEM((N_ROW,), jnp.int32)],
        compiler_params=PARAMS,
        cost_estimate=pl.CostEstimate(flops=0, bytes_accessed=20_000_000, transcendentals=0),
        name="table",
    )(pos, slot_blocks, parts[0])
    gathered = []
    for k in ORDER:
        here = over_z(parts[k], k) if k else own
        gathered += [here, over_core(here)]

    whole = shape(F * Y * HALF, L)
    layer = shape(F * DEEP * HALF, L)
    initial, x_in, x_out, y_in, y_out = pl.pallas_call(
        reorder,
        out_shape=[whole] + [layer] * 4,
        in_specs=[SMEM, SMEM] + [VMEM] * 8,
        out_specs=[VMEM] * 5,
        scratch_shapes=[pltpu.VMEM((HALF + 1, F, X, L), jnp.float32)],
        compiler_params=PARAMS,
        name="reorder",
    )(pos, rows, *gathered)

    def x_partner(z):
        return z ^ 1

    def y_partner(z):
        return z ^ 3

    def over_x(inner, outer):
        return (
            to(inner, lambda z, core, c: (x_partner(z), core, c)),
            to(outer, lambda z, core, c: (x_partner(z), core, c + 2 * tile_x(z) - 1)),
        )

    def over_y(inner, outer):
        return (
            to(inner, lambda z, core, c: (y_partner(z), core, c)),
            to(outer, lambda z, core, c: (y_partner(z), 1 - core, c + 2 * tile_y(z) - 1)),
        )

    y_layers = over_y(y_in, y_out)
    x_layers = over_x(x_in, x_out)
    corner_cells = pl.pallas_call(
        corners,
        out_shape=[shape(F * 3 * 8, L)] * 2,
        in_specs=[SMEM, VMEM, VMEM],
        out_specs=[VMEM] * 2,
        compiler_params=PARAMS,
        name="corners",
    )(pos, *y_layers)
    corner_cells = over_x(*corner_cells)
    wide = [F * WIDE * HALF, L]
    early = pl.pallas_call(
        begin,
        out_shape=[shape(*wide)] * 6,
        in_specs=[SMEM] + [VMEM] * 5,
        out_specs=[VMEM] * 6,
        compiler_params=PARAMS,
        cost_estimate=pl.CostEstimate(flops=0, bytes_accessed=10_000_000, transcendentals=0),
        name="begin",
    )(pos, initial, *x_layers, *y_layers)
    current = pl.pallas_call(
        finish,
        out_shape=shape(HALF, F, X, L),
        in_specs=[SMEM] + [VMEM] * 8,
        out_specs=VMEM,
        scratch_shapes=[pltpu.VMEM(wide, jnp.float32)] * 5,
        compiler_params=PARAMS,
        name="finish",
    )(pos, *early, *corner_cells[::-1])

    leaving = pl.pallas_call(
        pack_out,
        out_shape=[shape(OUT, F, X, L)] * 4,
        in_specs=[SMEM, SMEM, VMEM, VMEM],
        out_specs=[VMEM] * 4,
        compiler_params=PARAMS,
        name="pack_out",
    )(pos, final, current, over_core(current))
    arrived = [over_z(leaving[k], k) for k in range(4)]
    result = []
    for which in ((0,), (2, 1, 3)):
        n = len(which)
        result = [
            pl.pallas_call(
                lambda *refs, which=which: unpack_out(which, *refs),
                out_shape=shape(OUT, F, 2 * X, 2 * L),
                in_specs=[SMEM] + [ANY] * (n + len(result)),
                out_specs=ANY,
                input_output_aliases={n + 1: 0} if result else {},
                scratch_shapes=[pltpu.SemaphoreType.DMA((n,))],
                compiler_params=PARAMS,
                name="unpack_out",
            )(pos, *[arrived[k] for k in which], *result)
        ]
    return result[0]


def solution(mesh):
    in_specs = (P(("row", "col"), None, None, None), P())
    out_specs = P(("row", "col"), None, None, None)
    return jax.shard_map(body, mesh=mesh, in_specs=in_specs, out_specs=out_specs, check_vma=False)
```
